32 devices in a mesh: section: 2 (over x), dp: 16 (over z, y, core).
Axes of the slice: x: 2, y: 2, z: 4, core: 2. Of those that a mesh axis runs over, the one named last changes fastest.
Arguments:
- tokens: bfloat16 [2, 3584, 768], P(None, 'dp'), may hold values from -6 to 6
- cotangent: bfloat16 [2, 3584, 768], P(None, 'dp'), may hold values from -6 to 6
- crop_ids: int32 [2, 3584], P(None, 'dp'), may hold values from 0 to 6, as said below
- attn_weights: float32 [2, 768, 3072], P('section', 'dp')
- up_weights: float32 [2, 768, 3072], P('section', 'dp'), may hold values from -0.21875 to 0.21875
- down_weights: float32 [2, 3072, 768], P('section', 'dp'), may hold values from -0.109375 to 0.109375
- vectors: float32 [2, 12, 768], P('section', None, 'dp')
- first_attn: float32 [2, 768, 3072], P('section', 'dp'), may hold values from -0.0004272461 to 0.0004272461
- first_up: float32 [2, 768, 3072], P('section', 'dp'), may hold values from -0.0004272461 to 0.0004272461
- first_down: float32 [2, 3072, 768], P('section', 'dp'), may hold values from -0.0004272461 to 0.0004272461
- first_vectors: float32 [2, 12, 768], P('section', None, 'dp'), may hold values from -0.0012207031 to 0.0012207031
- second_attn: float32 [2, 768, 3072], P('section', 'dp'), may hold values from 7.064254e-11 to 2.8257016e-10
- second_up: float32 [2, 768, 3072], P('section', 'dp'), may hold values from 7.064254e-11 to 2.8257016e-10
- second_down: float32 [2, 3072, 768], P('section', 'dp'), may hold values from 7.064254e-11 to 2.8257016e-10
- second_vectors: float32 [2, 12, 768], P('section', None, 'dp'), may hold values from 6.3578287e-10 to 2.5431315e-09
Outputs:
- boundary: bfloat16 [2, 2, 3584, 768], P('section', None, 'dp')
- input_grads: bfloat16 [2, 2, 3584, 768], P('section', None, 'dp')
- grad_norm: float32 [], replicated
- new_attn: float32 [2, 768, 3072], P('section', 'dp')
- new_up: float32 [2, 768, 3072], P('section', 'dp')
- new_down: float32 [2, 3072, 768], P('section', 'dp')
- new_vectors: float32 [2, 12, 768], P('section', None, 'dp')
- new_first_attn: float32 [2, 768, 3072], P('section', 'dp')
- new_first_up: float32 [2, 768, 3072], P('section', 'dp')
- new_first_down: float32 [2, 3072, 768], P('section', 'dp')
- new_first_vectors: float32 [2, 12, 768], P('section', None, 'dp')
- new_second_attn: float32 [2, 768, 3072], P('section', 'dp')
- new_second_up: float32 [2, 768, 3072], P('section', 'dp')
- new_second_down: float32 [2, 3072, 768], P('section', 'dp')
- new_second_vectors: float32 [2, 12, 768], P('section', None, 'dp')
The draws below stay inside these ranges and needn't reach their ends.
Inputs may be any that keep to these rules, and one draw needn't show every extreme that they name: `crop_ids`: within each aligned block of 224 tokens of one micro-batch, ids start at 0 and never fall; a crop is a run of equal ids, of 197 or 37 tokens, except that the last run of a block may be shorter; equal ids in different blocks are different crops.
All inputs are finite; a program needn't handle non-finite values.
Results may differ from the reference program's by a relative error of at most 0.024.
The reference program's roundings to bfloat16 on the way count: a program that leaves them out, or rounds other values in their place, can miss the bound.
Values may be sent and summed in bfloat16 or wider, within the bound.
A program may use at most 384 MiB of HBM per device.

```python
import math
import jax
import jax.numpy as jnp
from jax import lax

D = 768
FF = 3072
HEADS = 12
HDIM = 64
PACK = 224
BIG_CROP = 197
SMALL_CROP = 37
MICRO = 2
STEP = 10
VROWS = 12
TOKENS = 3584


def draw_crop_ids(key, part):
    key = jax.random.fold_in(key, 11)
    pack_count = TOKENS // PACK
    key_large, key_zero = jax.random.split(key)
    large_count = jax.random.randint(key_large, (MICRO, pack_count, 1), 0, PACK // BIG_CROP + 1)
    chosen = jax.random.randint(key_zero, (1, 1, 1), 0, MICRO * pack_count)
    flat_index = jnp.arange(MICRO)[:, None, None] * pack_count + jnp.arange(pack_count)[None, :, None]
    large_count = jnp.where(flat_index == chosen, 0, large_count)
    position = jnp.arange(PACK)[None, None, :]
    large_end = large_count * BIG_CROP
    small_count = (PACK - large_end) // SMALL_CROP
    small_end = large_end + small_count * SMALL_CROP
    crop = jnp.where(position < large_end, position // BIG_CROP, jnp.where(position < small_end, large_count + (position - large_end) // SMALL_CROP, large_count + small_count))
    return crop.reshape(MICRO, TOKENS).astype(jnp.int32)


def draw_attn_weights(key, part):
    key = jax.random.fold_in(key, 23)
    base = jax.random.normal(key, (2, D, 4 * D), jnp.float32)
    column = jnp.arange(4 * D)[None, None, :]
    return base * jnp.where(column < 3 * D, D ** (-0.5), 4.0 * D ** (-0.5))


def draw_vectors(key, part):
    key = jax.random.fold_in(key, 37)
    key_gain, key_bias = jax.random.split(key)
    ramp = jnp.arange(D).astype(jnp.float32) / (D - 1)
    rising = 0.6 * jnp.exp(ramp * math.log(3.0))
    jitter = jnp.exp(jax.random.uniform(key_gain, (2, 2, D), jnp.float32, -0.35, 0.35))
    biases = 0.2 * jax.random.normal(key_bias, (2, VROWS, D), jnp.float32)
    gains = rising[None, None, :] * jitter
    row_index = jnp.arange(VROWS)[None, :, None]
    gain_rows = jnp.where(row_index == 0, gains[:, 0:1], gains[:, 1:2])
    return jnp.where((row_index == 0) | (row_index == 5), gain_rows, biases)


def block_levels(rng, dims, cuts, smallest, largest):
    gain = 1.0
    for dim, blocks in cuts:
        heights = jax.random.uniform(jax.random.fold_in(jax.random.fold_in(rng, 6), dim), (blocks,), jnp.float32, smallest / len(cuts), largest / len(cuts))
        gain = gain * jnp.repeat(jnp.exp(heights), dims[dim] // blocks).reshape((-1,) + (1,) * (len(dims) - 1 - dim))
    return gain


def noise(rng, shape, scale, limit, cuts=(), kind=jnp.bfloat16):
    factor_of = block_levels(rng, shape, cuts, -0.22, 0.18) if cuts else 1.0
    array = jax.random.normal(rng, shape, jnp.float32) * scale * factor_of
    return jnp.minimum(jnp.maximum(array, -limit), limit).astype(kind)


def setup_inputs(seed: int = 0) -> dict:
    splits = jax.random.split(jax.random.key(seed), 16)
    tokens = noise(splits[0], (MICRO, TOKENS, D), 1.0, 6.0, ((1, 16),))
    cotangent = noise(splits[1], (MICRO, TOKENS, D), 1.0, 6.0, ((1, 16),))
    crop_ids = draw_crop_ids(jax.random.fold_in(splits[15], 71), 0)
    attn_weights = draw_attn_weights(jax.random.fold_in(splits[15], 71), 0)
    up_weights = noise(splits[4], (2, D, FF), D ** -0.5, 0.21875, ((0, 2), (1, 16)), jnp.float32)
    down_weights = noise(splits[5], (2, FF, D), FF ** -0.5, 0.109375, ((0, 2), (1, 16)), jnp.float32)
    vectors = draw_vectors(jax.random.fold_in(splits[15], 71), 0)
    first_attn = noise(splits[7], (2, D, 4 * D), (0.111 * (8 * D * D + 4 * D * FF) ** -0.5), 0.0004272461, ((0, 2), (1, 16)), jnp.float32)
    first_up = noise(splits[8], (2, D, FF), (0.111 * (8 * D * D + 4 * D * FF) ** -0.5), 0.0004272461, ((0, 2), (1, 16)), jnp.float32)
    first_down = noise(splits[9], (2, FF, D), (0.111 * (8 * D * D + 4 * D * FF) ** -0.5), 0.0004272461, ((0, 2), (1, 16)), jnp.float32)
    first_vectors = noise(splits[10], (2, VROWS, D), (0.333 * (8 * D * D + 4 * D * FF) ** -0.5), 0.0012207031, ((0, 2), (2, 16)), jnp.float32)
    second_attn = jnp.clip(jnp.exp(math.log(2.825701617137355e-10) - 1.3862944 * jax.random.uniform(splits[11], (2, D, 4 * D), jnp.float32) ** block_levels(splits[11], (2, D, 4 * D), ((0, 2), (1, 16)), -0.2, 0.2)), 7.064254042843388e-11, 2.825701617137355e-10)
    second_up = jnp.clip(jnp.exp(math.log(2.825701617137355e-10) - 1.3862944 * jax.random.uniform(splits[12], (2, D, FF), jnp.float32) ** block_levels(splits[12], (2, D, FF), ((0, 2), (1, 16)), -0.2, 0.2)), 7.064254042843388e-11, 2.825701617137355e-10)
    second_down = jnp.clip(jnp.exp(math.log(2.825701617137355e-10) - 1.3862944 * jax.random.uniform(splits[13], (2, FF, D), jnp.float32) ** block_levels(splits[13], (2, FF, D), ((0, 2), (1, 16)), -0.2, 0.2)), 7.064254042843388e-11, 2.825701617137355e-10)
    second_vectors = jnp.clip(jnp.exp(math.log(2.543131483179195e-09) - 1.3862944 * jax.random.uniform(splits[14], (2, VROWS, D), jnp.float32) ** block_levels(splits[14], (2, VROWS, D), ((0, 2), (2, 16)), -0.2, 0.2)), 6.357828707947988e-10, 2.543131483179195e-09)
    return dict(tokens=tokens, cotangent=cotangent, crop_ids=crop_ids, attn_weights=attn_weights, up_weights=up_weights, down_weights=down_weights, vectors=vectors, first_attn=first_attn, first_up=first_up, first_down=first_down, first_vectors=first_vectors, second_attn=second_attn, second_up=second_up, second_down=second_down, second_vectors=second_vectors)


@jax.custom_vjp
def low(v):
    return lax.optimization_barrier(v.astype(jnp.bfloat16)).astype(jnp.float32)

@jax.custom_vjp
def low_back(v):
    return v

def low_keep(v):
    return (low(v), None)

def low_pass(kept, grad):
    return (grad,)

def back_keep(v):
    return (v, None)

def back_low(kept, grad):
    return (low(grad),)
low.defvjp(low_keep, low_pass)
low_back.defvjp(back_keep, back_low)
HIGHEST = lax.Precision.HIGHEST
LN_EPS = 1e-06
NEG_BIG = -1e+30
BETA_ONE = 0.9
BETA_TWO = 0.999
RATE = 0.1
VECTOR_RATE = 0.5
DECAY_RATE = 0.01
ADAM_EPS = 1e-08
MAX_NORM = 1.0

def layer_norm(features, gain_row, shift_row):
    center = lax.optimization_barrier(jnp.mean(features, axis=-1, keepdims=True))
    centered = features - center
    spread = lax.optimization_barrier(jnp.mean(centered * centered, axis=-1, keepdims=True))
    return centered * lax.rsqrt(spread + LN_EPS) * gain_row + shift_row

def one_layer(inputs, crop_group, attn, upward_w, downward_w, params):
    pack_count, pack_rows, model_width = inputs.shape
    flat_rows = pack_count * pack_rows
    flat = inputs.reshape(flat_rows, model_width)
    hidden = low(layer_norm(flat, params[0], params[1]))
    qkv_bias = jnp.concatenate([params[2], jnp.zeros_like(params[2]), params[3]])
    packed = low_back(low(jnp.dot(hidden, attn[:, :3 * model_width], precision=HIGHEST) + qkv_bias))
    shaped = packed.reshape(pack_count, pack_rows, 3, HEADS, HDIM)
    queries = shaped[:, :, 0]
    keys_all = shaped[:, :, 1]
    values_all = shaped[:, :, 2]
    scores = low_back(jnp.einsum('gqhd,gkhd->ghqk', queries, keys_all, precision=HIGHEST) * HDIM ** (-0.5))
    same_crop = crop_group[:, None, :, None] == crop_group[:, None, None, :]
    probs = jax.nn.softmax(jnp.where(same_crop, scores, NEG_BIG), axis=-1)
    mixed = jnp.einsum('ghqk,gkhd->gqhd', low(probs), values_all, precision=HIGHEST)
    mixed = low(low_back(mixed.reshape(flat_rows, model_width)))
    branch = low_back(jnp.dot(mixed, attn[:, 3 * model_width:], precision=HIGHEST) + params[4])
    middle = flat + branch
    hidden_two = low(layer_norm(middle, params[5], params[6]))
    upward = low_back(jnp.dot(hidden_two, upward_w, precision=HIGHEST) + params[8:].reshape(-1))
    active = low(jax.nn.gelu(upward, approximate=False))
    downward = low_back(jnp.dot(active, downward_w, precision=HIGHEST) + params[7])
    return (middle + downward).reshape(inputs.shape)

def adam_update(master, gradient, moment_one, moment_two, decay_rate, step_rate):
    new_one = BETA_ONE * moment_one + (1.0 - BETA_ONE) * gradient
    new_two = BETA_TWO * moment_two + (1.0 - BETA_TWO) * gradient * gradient
    ratio = new_one / (1.0 - BETA_ONE ** STEP) / (jnp.sqrt(new_two / (1.0 - BETA_TWO ** STEP)) + ADAM_EPS)
    return (master - step_rate * (ratio + decay_rate * master), new_one, new_two)

def reference(tokens, cotangent, crop_ids, attn_weights, up_weights, down_weights, vectors, first_attn, first_up, first_down, first_vectors, second_attn, second_up, second_down, second_vectors):
    pack_total = MICRO * TOKENS // PACK
    group_size = math.gcd(pack_total, 8)
    group_count = pack_total // group_size
    inputs_all = tokens.astype(jnp.float32).reshape(group_count, group_size, PACK, D)
    crops_all = crop_ids.reshape(group_count, group_size, PACK).astype(jnp.int32)
    probes_all = jnp.zeros_like(inputs_all)

    def stacked(attn_m, up_m, down_m, vec_m, inputs_in, probes_in):
        attn_b = low(attn_m)
        up_b = low(up_m)
        down_b = low(down_m)
        vec_b = low(vec_m)

        def group_step(carried):
            inputs_g, probe_g, crop_g = carried
            first_out = one_layer(inputs_g, crop_g, attn_b[0], up_b[0], down_b[0], vec_b[0])
            sent = low(first_out)
            second_in = low_back(sent) + probe_g
            second_out = one_layer(second_in, crop_g, attn_b[1], up_b[1], down_b[1], vec_b[1])
            return (second_out, sent)
        return lax.map(jax.checkpoint(group_step), (inputs_in, probes_in, crops_all))
    second_out, vjp_fn, first_out = jax.vjp(stacked, attn_weights, up_weights, down_weights, vectors, inputs_all, probes_all, has_aux=True)
    grads = vjp_fn(cotangent.astype(jnp.float32).reshape(inputs_all.shape))
    grad_attn, grad_up, grad_down, grad_vec, grad_first, grad_second = grads
    boundary = jnp.stack([first_out.reshape(MICRO, TOKENS, D), second_out.reshape(MICRO, TOKENS, D)]).astype(jnp.bfloat16)
    input_grads = jnp.stack([grad_first.reshape(MICRO, TOKENS, D), grad_second.reshape(MICRO, TOKENS, D)]).astype(jnp.bfloat16)
    squares = jnp.sum(grad_attn * grad_attn) + jnp.sum(grad_up * grad_up) + jnp.sum(grad_down * grad_down) + jnp.sum(grad_vec * grad_vec)
    grad_norm = jnp.sqrt(squares)
    clip_factor = jnp.minimum(1.0, MAX_NORM / (grad_norm + 1e-06))
    new_attn, one_attn, two_attn = adam_update(attn_weights, grad_attn * clip_factor, first_attn, second_attn, DECAY_RATE, RATE)
    new_up, one_up, two_up = adam_update(up_weights, grad_up * clip_factor, first_up, second_up, DECAY_RATE, RATE)
    new_down, one_down, two_down = adam_update(down_weights, grad_down * clip_factor, first_down, second_down, DECAY_RATE, RATE)
    new_vec, one_vec, two_vec = adam_update(vectors, grad_vec * clip_factor, first_vectors, second_vectors, 0.0, VECTOR_RATE)
    return (boundary, input_grads, grad_norm, new_attn, new_up, new_down, new_vec, one_attn, one_up, one_down, one_vec, two_attn, two_up, two_down, two_vec)
```

```python
from functools import partial

import jax
import jax.numpy as jnp
from jax import lax
from jax.experimental import pallas as pl
from jax.experimental.pallas import tpu as pltpu
from jax.sharding import PartitionSpec as P

HEADS = 12
STEP = 10
LN_EPS = 1e-06
NEG_BIG = -1e30
BETA_ONE = 0.9
BETA_TWO = 0.999
RATE = 0.1
VECTOR_RATE = 0.5
DECAY_RATE = 0.01
ADAM_EPS = 1e-08
MAX_NORM = 1.0
MESH = pl.DeviceIdType.MESH
VMEM_LIMIT = 60 * 2**20
F32 = jnp.float32
BF16 = jnp.bfloat16


class Ring:
    def __init__(self, devices):
        self.devices = devices
        self.chips = devices // 2
        self.reach = self.chips // 2
        self.me = lax.axis_index("dp")
        self.core = self.me % 2
        chip = self.me // 2
        row, column = chip // 2, chip % 2
        self.place = row * (1 - column) + (self.chips - 1 - row) * column

    def device(self, place, core):
        place = (place + 2 * self.chips) % self.chips
        column = place // self.reach
        row = place * (1 - column) + (self.chips - 1 - place) * column
        return (row * 2 + column) * 2 + core

    def target(self, device):
        return (lax.axis_index("section"), device)

    def right(self):
        return self.target(self.device(self.place + 1, self.core))

    def left(self):
        return self.target(self.device(self.place - 1, self.core))

    def sibling(self):
        return self.target(self.device(self.place, 1 - self.core))

    def greet(self):
        barrier = pltpu.get_barrier_semaphore()
        for device in (self.right(), self.left(), self.sibling()):
            pl.semaphore_signal(barrier, inc=1, device_id=device, device_id_type=MESH)
        pl.semaphore_wait(barrier, 3)


def shard_view(ref, device, rows, part=None):
    start = pl.multiple_of(device * rows, rows)
    if part is None:
        return ref.at[pl.ds(start, rows), :]
    columns = ref.shape[1] // 2
    return ref.at[pl.ds(start, rows), pl.ds(part * columns, columns)]


def remote(source, target, send, receive, device):
    return pltpu.make_async_remote_copy(
        src_ref=source,
        dst_ref=target,
        send_sem=send,
        recv_sem=receive,
        device_id=device,
        device_id_type=MESH,
    )


class Gather:
    def __init__(self, ring, whole, rows, halves, send, receive):
        self.ring, self.whole, self.rows, self.halves = ring, whole, rows, halves
        self.send, self.receive = send, receive
        self.sent = []

    def view(self, distance, core, part=None):
        device = self.ring.device(self.ring.place + distance, core)
        return shard_view(self.whole, device, self.rows, part)

    def push(self, way, step):
        ring = self.ring
        direction = 1 if way == 0 else -1
        part = None
        if step == ring.reach:
            if self.halves:
                part = way
            elif way == 1:
                return
        view = self.view(-direction * (step - 1), ring.core, part)
        device = ring.right() if way == 0 else ring.left()
        copy = remote(view, view, self.send.at[way, step], self.receive.at[way, step], device)
        copy.start()
        self.sent.append(copy)

    def arrive(self, way, step):
        ring = self.ring
        direction = 1 if way == 0 else -1
        part = None
        if step == ring.reach:
            if self.halves:
                part = way
            elif way == 1:
                return
        view = self.view(-direction * step, ring.core, part)
        device = ring.right() if way == 0 else ring.left()
        remote(view, view, self.send.at[way, step], self.receive.at[way, step], device).wait_recv()

    def share(self, distance, key):
        ring = self.ring
        view = self.view(distance, ring.core)
        copy = remote(view, view, self.send.at[2, key], self.receive.at[2, key], ring.sibling())
        copy.start()
        self.sent.append(copy)

    def shared(self, distance, key):
        ring = self.ring
        view = self.view(distance, 1 - ring.core)
        remote(view, view, self.send.at[2, key], self.receive.at[2, key], ring.sibling()).wait_recv()

    def begin(self):
        self.push(0, 1)
        self.push(1, 1)
        self.share(0, 0)

    def step(self, step):
        reach = self.ring.reach
        self.arrive(0, step)
        if step < reach:
            self.push(0, step + 1)
        self.arrive(1, step)
        if step < reach:
            self.push(1, step + 1)
            self.share(-step, step)
            self.share(step, reach + step)
        else:
            self.share(reach, reach)

    def finish_shares(self):
        reach = self.ring.reach
        self.shared(0, 0)
        for step in range(1, reach):
            self.shared(-step, step)
            self.shared(step, reach + step)
        self.shared(reach, reach)

    def drain(self):
        for copy in self.sent:
            copy.wait_send()


class Reduce:
    def __init__(self, ring, whole, out, other, slots, rows, halves, block, send, receive):
        self.ring, self.whole, self.out, self.other, self.slots = ring, whole, out, other, slots
        self.rows, self.halves, self.block = rows, halves, block
        self.send, self.receive = send, receive
        self.sent = []

    def view(self, distance, core, part=None):
        device = self.ring.device(self.ring.place + distance, core)
        return shard_view(self.whole, device, self.rows, part)

    def keys(self):
        reach = self.ring.reach
        order = [(reach, reach)]
        for distance in range(reach - 1, 0, -1):
            order += [(distance, reach + distance), (-distance, distance)]
        return order + [(0, 0)]

    def exchange(self):
        ring = self.ring
        for distance, key in self.keys():
            copy = remote(
                self.view(distance, 1 - ring.core),
                self.other.at[key],
                self.send.at[2, key],
                self.receive.at[2, key],
                ring.sibling(),
            )
            copy.start()
            self.sent.append(copy)

    def exchanged(self, key):
        ring = self.ring
        slot = self.other.at[key]
        remote(slot, slot, self.send.at[2, key], self.receive.at[2, key], ring.sibling()).wait_recv()

    def slot(self, way, step, part=None):
        ref = self.slots.at[way, step]
        if part is None:
            return ref
        columns = ref.shape[1] // 2
        return ref.at[:, pl.ds(part * columns, columns)]

    def part_of(self, way, distance):
        if distance == self.ring.reach and self.halves:
            return way
        return None

    def push(self, way, distance):
        ring = self.ring
        if distance == ring.reach and not self.halves and way == 1:
            return
        part = self.part_of(way, distance)
        device = ring.right() if way == 0 else ring.left()
        copy = remote(
            self.view(distance if way == 0 else -distance, ring.core, part),
            self.slot(way, distance, part),
            self.send.at[way, distance],
            self.receive.at[way, distance],
            device,
        )
        copy.start()
        self.sent.append(copy)

    def arrive(self, way, distance):
        ring = self.ring
        if distance == ring.reach and not self.halves and way == 1:
            return
        slot = self.slot(way, distance, self.part_of(way, distance))
        device = ring.right() if way == 0 else ring.left()
        remote(slot, slot, self.send.at[way, distance], self.receive.at[way, distance], device).wait_recv()

    def add(self, distance, key, arrivals, target=None):
        ring = self.ring
        base = ring.device(ring.place + distance, ring.core) * self.rows
        block = self.block
        columns = self.whole.shape[1]
        half = columns // 2

        def body(index, _):
            start = pl.multiple_of(index * block, block)
            here = pl.ds(pl.multiple_of(base + index * block, block), block)
            rows = pl.ds(start, block)
            total = self.whole[here, :].astype(F32) + self.other[key, rows, :].astype(F32)
            whole_total = total
            for way, step in arrivals:
                if step == ring.reach:
                    if not self.halves:
                        if way == 0:
                            whole_total = whole_total + self.slots[way, step, rows, :].astype(F32)
                        continue
                    low = whole_total[:, :half]
                    high = whole_total[:, half:]
                    if way == 0:
                        low = low + self.slots[way, step, rows, :half].astype(F32)
                    else:
                        high = high + self.slots[way, step, rows, half:].astype(F32)
                    whole_total = jnp.concatenate([low, high], axis=1)
                else:
                    whole_total = whole_total + self.slots[way, step, rows, :].astype(F32)
            if target is None:
                self.whole[here, :] = whole_total.astype(self.whole.dtype)
            else:
                target[rows, :] = whole_total.astype(target.dtype)
            return 0

        lax.fori_loop(0, self.rows // block, body, 0)

    def first(self):
        reach = self.ring.reach
        self.exchanged(reach)
        self.add(reach, reach, [])
        self.push(0, reach)
        self.push(1, reach)

    def step(self, distance):
        reach = self.ring.reach
        self.exchanged(reach + distance)
        self.arrive(0, distance + 1)
        self.add(distance, reach + distance, [(0, distance + 1)])
        self.push(0, distance)
        self.exchanged(distance)
        self.arrive(1, distance + 1)
        self.add(-distance, distance, [(1, distance + 1)])
        self.push(1, distance)

    def last(self):
        self.exchanged(0)
        self.arrive(0, 1)
        self.arrive(1, 1)
        self.add(0, 0, [(0, 1), (1, 1)], self.out)

    def drain(self):
        for copy in self.sent:
            copy.wait_send()


def ring_semaphores(count, reach):
    shape = (count, 3, 2 * reach)
    return [pltpu.SemaphoreType.DMA(shape), pltpu.SemaphoreType.DMA(shape)]


def gather_kernel(devices, own_qkv, own_out, own_up, own_down, own_vec, qkv, out, up, down, vec, local, send, receive):
    ring = Ring(devices)
    owned = (own_vec, own_qkv, own_out, own_up, own_down)
    wholes = (vec, qkv, out, up, down)
    gathers = []
    copies = []
    for index, (own, whole) in enumerate(zip(owned, wholes)):
        gathers.append(
            Gather(ring, whole, own.shape[0], index > 0, send.at[index], receive.at[index])
        )
        copies.append(
            pltpu.make_async_copy(own, shard_view(whole, ring.me, own.shape[0]), local.at[index])
        )
    for copy in copies:
        copy.start()
    for copy in copies:
        copy.wait()
    ring.greet()
    for gather in gathers:
        gather.begin()
    for step in range(1, ring.reach + 1):
        for gather in gathers:
            gather.step(step)
    for gather in gathers:
        gather.finish_shares()
        gather.drain()


def ring_gather(devices, owned):
    reach = devices // 4
    return pl.pallas_call(
        partial(gather_kernel, devices),
        out_shape=[
            jax.ShapeDtypeStruct((devices * own.shape[0], own.shape[1]), own.dtype) for own in owned
        ],
        in_specs=[pl.BlockSpec(memory_space=pltpu.VMEM)] * 5,
        out_specs=[pl.BlockSpec(memory_space=pltpu.VMEM)] * 5,
        scratch_shapes=[pltpu.SemaphoreType.DMA((5,))] + ring_semaphores(5, reach),
        compiler_params=pltpu.CompilerParams(
            collective_id=0, has_side_effects=True, vmem_limit_bytes=VMEM_LIMIT
        ),
        name="ring_gather",
    )(*owned)


def reduce_kernel(devices, *refs):
    sums, outs, others, slots = refs[:5], refs[5:10], refs[10:15], refs[15:20]
    send, receive = refs[20:]
    ring = Ring(devices)
    reduces = [
        Reduce(
            ring,
            sums[i],
            outs[i],
            others[i],
            slots[i],
            outs[i].shape[0],
            i < 4,
            16,
            send.at[i],
            receive.at[i],
        )
        for i in range(5)
    ]
    ring.greet()
    for reduce in reduces:
        reduce.exchange()
    for reduce in reduces:
        reduce.first()
    for distance in range(ring.reach - 1, 0, -1):
        for reduce in reduces:
            reduce.step(distance)
    for reduce in reduces:
        reduce.last()
    for reduce in reduces:
        reduce.drain()


def ring_reduce(devices, sums):
    reach = devices // 4
    chips = devices // 2
    out_shapes, others, slots = [], [], []
    for member in sums:
        rows, columns = member.shape[0] // devices, member.shape[1]
        out_shapes.append(jax.ShapeDtypeStruct((rows, columns), F32))
        others.append(pltpu.VMEM((chips, rows, columns), member.dtype))
        slots.append(pltpu.VMEM((2, reach + 1, rows, columns), member.dtype))
    return pl.pallas_call(
        partial(reduce_kernel, devices),
        out_shape=out_shapes,
        in_specs=[pl.BlockSpec(memory_space=pltpu.VMEM)] * 5,
        out_specs=[pl.BlockSpec(memory_space=pltpu.VMEM)] * 5,
        scratch_shapes=others + slots + ring_semaphores(5, reach),
        compiler_params=pltpu.CompilerParams(
            collective_id=1, has_side_effects=True, vmem_limit_bytes=VMEM_LIMIT
        ),
        name="ring_reduce",
    )(*sums)


def pad_tile(block):
    return jnp.pad(block, ((0, 16 - block.shape[0]), (0, 128 - block.shape[1])))


def gather_weights(fast, devices, attn, upward_w, downward_w, vectors):
    shards = (attn.astype(BF16), upward_w.astype(BF16), downward_w.astype(BF16))
    if not fast:
        return tuple(lax.all_gather(s, "dp", axis=0, tiled=True) for s in shards) + (
            lax.all_gather(vectors.astype(BF16), "dp", axis=1, tiled=True),
        )
    width = downward_w.shape[1]
    tile = pad_tile(vectors.astype(BF16))
    qkv, out, up, down, tiles = ring_gather(
        devices, (shards[0][:, : 3 * width], shards[0][:, 3 * width :], shards[1], shards[2], tile)
    )
    rows, columns = vectors.shape
    spread = tiles.reshape(devices, 16, 128)[:, :rows, :columns]
    return (jnp.concatenate([qkv, out], axis=1), up, down, spread.transpose(1, 0, 2).reshape(rows, -1))


def reduce_gradients(fast, devices, gradients):
    attn, upward_w, downward_w, vectors = gradients
    if not fast:
        return tuple(
            lax.psum_scatter(g, "dp", scatter_dimension=0, tiled=True)
            for g in (attn, upward_w, downward_w)
        ) + (lax.psum_scatter(vectors, "dp", scatter_dimension=1, tiled=True),)
    width = downward_w.shape[1]
    rows, columns = vectors.shape[0], vectors.shape[1] // devices
    spread = vectors.reshape(rows, devices, columns).transpose(1, 0, 2)
    tiles = jnp.pad(spread, ((0, 0), (0, 16 - rows), (0, 128 - columns))).reshape(-1, 128)
    qkv, out, up, down, tile = ring_reduce(
        devices,
        (
            attn[:, : 3 * width].astype(BF16),
            attn[:, 3 * width :].astype(BF16),
            upward_w.astype(BF16),
            downward_w.astype(BF16),
            tiles,
        ),
    )
    return (jnp.concatenate([qkv, out], axis=1), up, down, tile[:rows, :columns])


def layer_norm(features, gain_row, shift_row):
    center = jnp.mean(features, axis=-1, keepdims=True)
    centered = features - center
    spread = jnp.mean(centered * centered, axis=-1, keepdims=True)
    return centered * lax.rsqrt(spread + LN_EPS) * gain_row + shift_row


def split_heads(packed, micro_count, model_width):
    shaped = packed.reshape(micro_count, -1, 3, HEADS, model_width // HEADS)
    return (shaped[:, :, 0], shaped[:, :, 1], shaped[:, :, 2])


def attention_scores(queries, keys_block, crop_rows):
    head_scale = queries.shape[-1] ** (-0.5)
    scores = (
        jnp.einsum("mqhd,mkhd->mhqk", queries, keys_block, preferred_element_type=F32) * head_scale
    )
    same_crop = crop_rows[:, :, None] == crop_rows[:, None, :]
    return jnp.where(same_crop[:, None], scores, NEG_BIG)


def forward_layer(inputs, crop_rows, weights):
    attn, upward_w, downward_w, vectors_b = weights
    model_width = attn.shape[0]
    rows = inputs.shape[0]
    params = vectors_b.astype(F32)
    hidden = layer_norm(inputs, params[0], params[1]).astype(BF16)
    qkv_bias = jnp.concatenate([params[2], jnp.zeros_like(params[2]), params[3]])
    packed = (
        jnp.dot(hidden, attn[:, : 3 * model_width], preferred_element_type=F32) + qkv_bias
    ).astype(BF16)
    queries, keys_block, values_block = split_heads(packed, crop_rows.shape[0], model_width)
    scores = attention_scores(queries, keys_block, crop_rows)
    row_peak = jnp.max(scores, axis=-1, keepdims=True)
    exponent = jnp.exp(scores - row_peak)
    totals = jnp.sum(exponent, axis=-1, keepdims=True)
    soft_weights = (exponent / totals).astype(BF16)
    log_total = row_peak + jnp.log(totals)
    mixed = jnp.einsum("mhqk,mkhd->mqhd", soft_weights, values_block, preferred_element_type=F32)
    mixed = mixed.reshape(rows, model_width).astype(BF16)
    middle = inputs + (
        jnp.dot(mixed, attn[:, 3 * model_width :], preferred_element_type=F32) + params[4]
    )
    hidden_two = layer_norm(middle, params[5], params[6]).astype(BF16)
    upward = jnp.dot(hidden_two, upward_w, preferred_element_type=F32) + params[8:].reshape(-1)
    active = jax.nn.gelu(upward, approximate=False).astype(BF16)
    output = middle + (jnp.dot(active, downward_w, preferred_element_type=F32) + params[7])
    return (output, (inputs, hidden, packed, log_total, mixed, middle, hidden_two, upward, active))


def backward_layer(kept, crop_rows, grad_out, weights, with_grads):
    attn, upward_w, downward_w, vectors_b = weights
    inputs, hidden, packed, log_total, mixed, middle, hidden_two, upward, active = kept
    model_width = attn.shape[0]
    rows = inputs.shape[0]
    params = vectors_b.astype(F32)
    grad_down = grad_out.astype(BF16)
    grad_active = jnp.einsum("pj,ij->pi", grad_down, downward_w, preferred_element_type=F32)
    gelu_back = jax.vjp(partial(jax.nn.gelu, approximate=False), upward)[1]
    grad_up = gelu_back(grad_active)[0].astype(BF16)
    grad_hidden_two = jnp.einsum("pj,ij->pi", grad_up, upward_w, preferred_element_type=F32)
    norm_back_two = jax.vjp(layer_norm, middle, params[5], params[6])[1]
    grad_middle_part, grad_gain_two, grad_shift_two = norm_back_two(grad_hidden_two)
    grad_middle = grad_out + grad_middle_part
    grad_branch = grad_middle.astype(BF16)
    grad_mixed = jnp.einsum(
        "pj,ij->pi", grad_branch, attn[:, 3 * model_width :], preferred_element_type=F32
    ).astype(BF16)
    micro_count = crop_rows.shape[0]
    queries, keys_block, values_block = split_heads(packed, micro_count, model_width)
    scores = attention_scores(queries, keys_block, crop_rows)
    probs = jnp.exp(scores - log_total)
    grad_heads = grad_mixed.reshape(micro_count, -1, HEADS, model_width // HEADS)
    grad_probs = jnp.einsum("mqhd,mkhd->mhqk", grad_heads, values_block, preferred_element_type=F32)
    grad_values = jnp.einsum(
        "mhqk,mqhd->mkhd", probs.astype(BF16), grad_heads, preferred_element_type=F32
    )
    grad_scores = (
        probs * (grad_probs - jnp.sum(grad_probs * probs, axis=-1, keepdims=True))
    ).astype(BF16)
    head_scale = queries.shape[-1] ** (-0.5)
    grad_queries = (
        jnp.einsum("mhqk,mkhd->mqhd", grad_scores, keys_block, preferred_element_type=F32)
        * head_scale
    )
    grad_keys = (
        jnp.einsum("mhqk,mqhd->mkhd", grad_scores, queries, preferred_element_type=F32) * head_scale
    )
    grad_packed = jnp.concatenate(
        [
            grad_queries.reshape(rows, model_width),
            grad_keys.reshape(rows, model_width),
            grad_values.reshape(rows, model_width),
        ],
        axis=1,
    ).astype(BF16)
    grad_hidden = jnp.einsum(
        "pj,ij->pi", grad_packed, attn[:, : 3 * model_width], preferred_element_type=F32
    )
    norm_back_one = jax.vjp(layer_norm, inputs, params[0], params[1])[1]
    grad_in_part, grad_gain_one, grad_shift_one = norm_back_one(grad_hidden)
    grad_inputs = grad_middle + grad_in_part
    if not with_grads:
        return (grad_inputs, None)
    grad_w_down = jnp.einsum("pi,pj->ij", active, grad_down, preferred_element_type=F32)
    grad_w_up = jnp.einsum("pi,pj->ij", hidden_two, grad_up, preferred_element_type=F32)
    grad_w_out = jnp.einsum("pi,pj->ij", mixed, grad_branch, preferred_element_type=F32)
    grad_w_qkv = jnp.einsum("pi,pj->ij", hidden, grad_packed, preferred_element_type=F32)
    packed_sums = jnp.sum(grad_packed, axis=0, dtype=F32)
    vector_rows = jnp.stack(
        [
            grad_gain_one,
            grad_shift_one,
            packed_sums[:model_width],
            packed_sums[2 * model_width :],
            jnp.sum(grad_branch, axis=0, dtype=F32),
            grad_gain_two,
            grad_shift_two,
            jnp.sum(grad_down, axis=0, dtype=F32),
        ]
    )
    up_bias_rows = jnp.sum(grad_up, axis=0, dtype=F32).reshape(-1, model_width)
    grad_vectors = jnp.concatenate([vector_rows, up_bias_rows], axis=0)
    grad_attn = jnp.concatenate([grad_w_qkv, grad_w_out], axis=1)
    return (grad_inputs, (grad_attn, grad_w_up, grad_w_down, grad_vectors))


def adam_update(master, gradient, moment_one, moment_two, decay_rate, step_rate):
    new_one = BETA_ONE * moment_one + (1.0 - BETA_ONE) * gradient
    new_two = BETA_TWO * moment_two + (1.0 - BETA_TWO) * gradient * gradient
    ratio = (
        new_one / (1.0 - BETA_ONE**STEP) / (jnp.sqrt(new_two / (1.0 - BETA_TWO**STEP)) + ADAM_EPS)
    )
    return (master - step_rate * (ratio + decay_rate * master), new_one, new_two)


def shards(
    devices,
    tokens,
    cotangent,
    crop_ids,
    attn_weights,
    up_weights,
    down_weights,
    vectors,
    first_attn,
    first_up,
    first_down,
    first_vectors,
    second_attn,
    second_up,
    second_down,
    second_vectors,
):
    section_index = lax.axis_index("section")
    micro_count, pack_rows, model_width = tokens.shape
    flat = (micro_count * pack_rows, model_width)
    fast = (
        devices % 8 == 0
        and all(w.shape[1] % 16 == 0 for w in (attn_weights, up_weights, down_weights))
        and vectors.shape[1] <= 16
        and vectors.shape[2] <= 128
    )
    weights = gather_weights(
        fast, devices, attn_weights[0], up_weights[0], down_weights[0], vectors[0]
    )
    own_tokens = tokens.reshape(flat)
    first_output, _ = forward_layer(own_tokens.astype(F32), crop_ids, weights)
    received = lax.ppermute(first_output.astype(BF16), "section", [(0, 1)])
    layer_input = jnp.where(section_index == 0, own_tokens, received)
    output, kept = forward_layer(layer_input.astype(F32), crop_ids, weights)
    boundary = output.astype(BF16).reshape(tokens.shape)
    own_grad = cotangent.reshape(flat)
    first_back, _ = backward_layer(kept, crop_ids, own_grad.astype(F32), weights, False)
    back_received = lax.ppermute(first_back.astype(BF16), "section", [(1, 0)])
    grad_out = jnp.where(section_index == 1, own_grad, back_received).astype(F32)
    grad_inputs, gradients = backward_layer(kept, crop_ids, grad_out, weights, True)
    input_grads = grad_inputs.astype(BF16).reshape(tokens.shape)
    reduced = reduce_gradients(fast, devices, gradients)
    squares = sum_squares(reduced)
    grad_norm = jnp.sqrt(lax.psum(squares, ("section", "dp")))
    clip_factor = jnp.minimum(1.0, MAX_NORM / (grad_norm + 1e-06))
    masters = (attn_weights, up_weights, down_weights, vectors)
    firsts = (first_attn, first_up, first_down, first_vectors)
    seconds = (second_attn, second_up, second_down, second_vectors)
    decays = (DECAY_RATE, DECAY_RATE, DECAY_RATE, 0.0)
    rates = (RATE, RATE, RATE, VECTOR_RATE)
    updated = [
        adam_update(
            master[0], gradient * clip_factor, moment_one[0], moment_two[0], decay_rate, step_rate
        )
        for master, gradient, moment_one, moment_two, decay_rate, step_rate in zip(
            masters, reduced, firsts, seconds, decays, rates
        )
    ]
    new_masters = tuple((entry[0][None] for entry in updated))
    new_firsts = tuple((entry[1][None] for entry in updated))
    new_seconds = tuple((entry[2][None] for entry in updated))
    return (boundary[None], input_grads[None], grad_norm) + new_masters + new_firsts + new_seconds


def sum_squares(arrays):
    running = jnp.zeros((), F32)
    for member in arrays:
        running = running + jnp.sum(member * member)
    return running


def solution(mesh):
    token_spec = P(None, "dp", None)
    row_spec = P("section", "dp", None)
    column_spec = P("section", None, "dp")
    state = (row_spec, row_spec, row_spec, column_spec)
    micro_spec = P("section", None, "dp", None)
    return jax.shard_map(
        partial(shards, mesh.shape["dp"]),
        mesh=mesh,
        in_specs=(token_spec, token_spec, P(None, "dp")) + 3 * state,
        out_specs=(micro_spec, micro_spec, P()) + 3 * state,
        check_vma=False,
    )
```

```python
from functools import partial

import jax
import jax.numpy as jnp
from jax import lax
from jax.experimental import pallas as pl
from jax.experimental.pallas import tpu as pltpu
from jax.sharding import PartitionSpec as P

HEADS = 12
STEP = 10
LN_EPS = 1e-06
NEG_BIG = -1e30
BETA_ONE = 0.9
BETA_TWO = 0.999
RATE = 0.1
VECTOR_RATE = 0.5
DECAY_RATE = 0.01
ADAM_EPS = 1e-08
MAX_NORM = 1.0
MESH = pl.DeviceIdType.MESH
VMEM_LIMIT = 60 * 2**20
F32 = jnp.float32
BF16 = jnp.bfloat16


class Ring:
    def __init__(self, devices):
        self.devices = devices
        self.chips = devices // 2
        self.reach = self.chips // 2
        self.me = lax.axis_index("dp")
        self.core = self.me % 2
        chip = self.me // 2
        row, column = chip // 2, chip % 2
        self.place = row * (1 - column) + (self.chips - 1 - row) * column

    def device(self, place, core):
        place = (place + 2 * self.chips) % self.chips
        column = place // self.reach
        row = place * (1 - column) + (self.chips - 1 - place) * column
        return (row * 2 + column) * 2 + core

    def target(self, device):
        return (lax.axis_index("section"), device)

    def right(self):
        return self.target(self.device(self.place + 1, self.core))

    def left(self):
        return self.target(self.device(self.place - 1, self.core))

    def sibling(self):
        return self.target(self.device(self.place, 1 - self.core))

    def greet(self):
        barrier = pltpu.get_barrier_semaphore()
        for device in (self.right(), self.left(), self.sibling()):
            pl.semaphore_signal(barrier, inc=1, device_id=device, device_id_type=MESH)
        pl.semaphore_wait(barrier, 3)


def shard_view(ref, device, rows, part=None):
    start = pl.multiple_of(device * rows, rows)
    if part is None:
        return ref.at[pl.ds(start, rows), :]
    columns = ref.shape[1] // 2
    return ref.at[pl.ds(start, rows), pl.ds(part * columns, columns)]


def remote(source, target, send, receive, device):
    return pltpu.make_async_remote_copy(
        src_ref=source,
        dst_ref=target,
        send_sem=send,
        recv_sem=receive,
        device_id=device,
        device_id_type=MESH,
    )


class Gather:
    def __init__(self, ring, whole, rows, halves, send, receive):
        self.ring, self.whole, self.rows, self.halves = ring, whole, rows, halves
        self.send, self.receive = send, receive

    def view(self, distance, core, part=None):
        device = self.ring.device(self.ring.place + distance, core)
        return shard_view(self.whole, device, self.rows, part)

    def hop(self, way, step, came):
        ring = self.ring
        direction = 1 if way == 0 else -1
        part = None
        if step == ring.reach:
            if self.halves:
                part = way
            elif way == 1:
                return None
        view = self.view(-direction * (step if came else step - 1), ring.core, part)
        device = ring.right() if way == 0 else ring.left()
        return remote(view, view, self.send.at[way, step], self.receive.at[way, step], device)

    def push(self, way, step):
        copy = self.hop(way, step, False)
        if copy is not None:
            copy.start()

    def arrive(self, way, step):
        copy = self.hop(way, step, True)
        if copy is not None:
            copy.wait_recv()

    def share(self, distance, key, core):
        view = self.view(distance, core)
        return remote(view, view, self.send.at[2, key], self.receive.at[2, key], self.ring.sibling())

    def shares(self):
        reach = self.ring.reach
        keys = [(0, 0), (reach, reach)]
        for step in range(1, reach):
            keys += [(-step, step), (step, reach + step)]
        return keys

    def begin(self):
        self.push(0, 1)
        self.push(1, 1)
        self.share(0, 0, self.ring.core).start()

    def step(self, step):
        reach, core = self.ring.reach, self.ring.core
        self.arrive(0, step)
        if step < reach:
            self.push(0, step + 1)
        self.arrive(1, step)
        if step < reach:
            self.push(1, step + 1)
            self.share(-step, step, core).start()
            self.share(step, reach + step, core).start()
        else:
            self.share(reach, reach, core).start()

    def finish(self):
        for distance, key in self.shares():
            self.share(distance, key, 1 - self.ring.core).wait_recv()

    def drain(self):
        for distance, key in self.shares():
            self.share(distance, key, self.ring.core).wait_send()
        for step in range(1, self.ring.reach + 1):
            for way in (0, 1):
                copy = self.hop(way, step, False)
                if copy is not None:
                    copy.wait_send()


class Reduce:
    def __init__(self, ring, whole, base, put, other, slots, halves, block, send, receive):
        self.ring, self.whole, self.base, self.put, self.other, self.slots = ring, whole, base, put, other, slots
        self.rows, self.halves, self.block = other.shape[1], halves, block
        self.send, self.receive = send, receive

    def row(self, distance, core):
        device = self.ring.device(self.ring.place + distance, core)
        return pl.multiple_of(self.base + device * self.rows, 16)

    def view(self, distance, core, part=None):
        rows = pl.ds(self.row(distance, core), self.rows)
        if part is None:
            return self.whole.at[rows, :]
        columns = self.whole.shape[1] // 2
        return self.whole.at[rows, pl.ds(part * columns, columns)]

    def keys(self):
        reach = self.ring.reach
        order = [(reach, reach)]
        for distance in range(reach - 1, 0, -1):
            order += [(distance, reach + distance), (-distance, distance)]
        return order + [(0, 0)]

    def swap(self, distance, key):
        return remote(
            self.view(distance, 1 - self.ring.core),
            self.other.at[key],
            self.send.at[2, key],
            self.receive.at[2, key],
            self.ring.sibling(),
        )

    def exchange(self):
        for distance, key in self.keys():
            self.swap(distance, key).start()

    def exchanged(self, key):
        slot = self.other.at[key]
        remote(
            slot, slot, self.send.at[2, key], self.receive.at[2, key], self.ring.sibling()
        ).wait_recv()

    def slot(self, way, distance):
        ref = self.slots.at[way, distance - 1]
        if distance == self.ring.reach and self.halves:
            columns = ref.shape[1] // 2
            return ref.at[:, pl.ds(way * columns, columns)]
        return ref

    def hop(self, way, distance, came):
        ring = self.ring
        if distance == ring.reach and not self.halves and way == 1:
            return None
        slot = self.slot(way, distance)
        source = slot
        if not came:
            part = way if distance == ring.reach and self.halves else None
            source = self.view(distance if way == 0 else -distance, ring.core, part)
        device = ring.right() if way == 0 else ring.left()
        return remote(
            source, slot, self.send.at[way, distance], self.receive.at[way, distance], device
        )

    def push(self, way, distance):
        copy = self.hop(way, distance, False)
        if copy is not None:
            copy.start()

    def arrive(self, way, distance):
        copy = self.hop(way, distance, True)
        if copy is not None:
            copy.wait_recv()

    def add(self, distance, key, arrivals, final=False):
        ring = self.ring
        base = self.row(distance, ring.core)
        block = self.block
        half = self.whole.shape[1] // 2

        def body(index, _):
            here = pl.ds(pl.multiple_of(base + index * block, 16), block)
            rows = pl.ds(pl.multiple_of(index * block, block), block)
            total = self.whole[here, :].astype(F32) + self.other[key, rows, :].astype(F32)
            for way, far in arrivals:
                if far == ring.reach and self.halves:
                    low, high = total[:, :half], total[:, half:]
                    if way == 0:
                        low = low + self.slots[way, far - 1, rows, :half].astype(F32)
                    else:
                        high = high + self.slots[way, far - 1, rows, half:].astype(F32)
                    total = jnp.concatenate([low, high], axis=1)
                elif far < ring.reach or way == 0:
                    total = total + self.slots[way, far - 1, rows, :].astype(F32)
            if final:
                self.put(rows, total)
            else:
                self.whole[here, :] = total.astype(self.whole.dtype)
            return 0

        lax.fori_loop(0, self.rows // block, body, 0)

    def first(self):
        reach = self.ring.reach
        self.exchanged(reach)
        self.add(reach, reach, [])
        self.push(0, reach)
        self.push(1, reach)

    def step(self, distance):
        reach = self.ring.reach
        self.exchanged(reach + distance)
        self.arrive(0, distance + 1)
        self.add(distance, reach + distance, [(0, distance + 1)])
        self.push(0, distance)
        self.exchanged(distance)
        self.arrive(1, distance + 1)
        self.add(-distance, distance, [(1, distance + 1)])
        self.push(1, distance)

    def last(self):
        self.exchanged(0)
        self.arrive(0, 1)
        self.arrive(1, 1)
        self.add(0, 0, [(0, 1), (1, 1)], True)

    def drain(self):
        for distance, key in self.keys():
            self.swap(distance, key).wait_send()
        for distance in range(1, self.ring.reach + 1):
            for way in (0, 1):
                copy = self.hop(way, distance, False)
                if copy is not None:
                    copy.wait_send()


def dot_nn(a, b):
    return lax.dot_general(a, b, (((1,), (0,)), ((), ())), preferred_element_type=F32)


def dot_nt(a, b):
    return lax.dot_general(a, b, (((1,), (1,)), ((), ())), preferred_element_type=F32)


def dot_tn(a, b):
    return lax.dot_general(a, b, (((0,), (0,)), ((), ())), preferred_element_type=F32)


def erf(value):
    bound = 3.832506856900711
    value = jnp.clip(value, -bound, bound)
    square = value * value
    top = 0.00022905065861350646
    for factor in (
        0.0034082910107109506,
        0.050955695062380861,
        0.18520832239976145,
        1.128379143519084,
    ):
        top = top * square + factor
    bottom = -1.1791602954361697e-7
    for factor in (
        0.000023547966471313185,
        0.0010179625278914885,
        0.014070470171167667,
        0.11098505178285362,
        0.49746925110067538,
        1.0,
    ):
        bottom = bottom * square + factor
    return value * top / bottom


def norm_parts(features):
    center = jnp.mean(features, axis=-1, keepdims=True)
    centered = features - center
    spread = jnp.mean(centered * centered, axis=-1, keepdims=True)
    scale = lax.rsqrt(spread + LN_EPS)
    return centered * scale, scale


def norm_back(z, scale, e, gain):
    t = e * gain
    return (
        t - jnp.mean(t, axis=-1, keepdims=True) - z * jnp.mean(t * z, axis=-1, keepdims=True)
    ) * scale


def column_sum(value):
    return jnp.sum(value, axis=0, keepdims=True)


def layer_kernel(
    devices,
    sections,
    tokens,
    cotangent,
    crops,
    own_attn,
    own_up,
    own_down,
    own_vec,
    boundary,
    input_grads,
    sum_attn,
    sum_up,
    sum_down,
    sum_vec,
    norm,
    w_qkv,
    w_out,
    w_up,
    w_down,
    tiles,
    params,
    x_in,
    hidden,
    qkv,
    log_total,
    mixed,
    middle,
    hidden_two,
    slope,
    active,
    mask,
    dy_in,
    grad_up,
    grad_branch,
    grad_heads,
    grad_qkv,
    flow,
    flow_two,
    vec_sums,
    vec_tiles,
    g_down,
    other_down,
    other_up,
    other_attn,
    other_vec,
    slots_down,
    slots_up,
    slots_attn,
    slots_vec,
    norm_slots,
    local,
    send,
    receive,
    across,
    norm_sem,
):
    section = lax.axis_index("section")
    first_section = section == 0
    last_section = section == 1
    ring = Ring(devices)
    me = ring.me
    micro_count, pack = tokens.shape[0], tokens.shape[1]
    width = tokens.shape[2]
    hidden_units = w_up.shape[1]
    tiles_up = hidden_units // width
    head_width = width // HEADS
    pairs = HEADS // 2
    pair_width = 2 * head_width
    head_scale = head_width ** (-0.5)
    vec_rows, vec_columns = own_vec.shape[1], own_vec.shape[2]

    def rows_of(micro):
        return pl.ds(pl.multiple_of(micro * pack, 16), pack)

    def lanes(start, count):
        return pl.ds(pl.multiple_of(start, 128), count)


    stage_attn = slope.at[pl.ds(0, own_attn.shape[1]), :]
    stage_up = slope.at[pl.ds(own_attn.shape[1], own_up.shape[1]), :]
    stage_down = middle.at[pl.ds(0, own_down.shape[1]), :]
    loads = [
        pltpu.make_async_copy(own_attn.at[0], stage_attn, local.at[0]),
        pltpu.make_async_copy(own_up.at[0], stage_up, local.at[1]),
        pltpu.make_async_copy(own_down.at[0], stage_down, local.at[2]),
    ]
    for load in loads:
        load.start()

    def load_tokens(micro):
        return pltpu.make_async_copy(tokens.at[micro], x_in.at[rows_of(micro), :], local.at[3 + micro])

    def load_cotangent(micro):
        return pltpu.make_async_copy(
            cotangent.at[micro], dy_in.at[rows_of(micro), :], local.at[3 + micro]
        )

    @pl.when(first_section)
    def _():
        for micro in range(micro_count):
            load_tokens(micro).start()

    @pl.when(last_section)
    def _():
        for micro in range(micro_count):
            load_cotangent(micro).start()

    total_devices = sections * devices
    flat = section * devices + me

    def other_device(distance):
        other = (flat + distance) % total_devices
        return (other // devices, other % devices)

    barrier = pltpu.get_barrier_semaphore()

    def greet(distance, _):
        pl.semaphore_signal(
            barrier, inc=1, device_id=other_device(distance), device_id_type=MESH
        )
        return 0

    lax.fori_loop(1, total_devices, greet, 0)

    vec_tiles[...] = jnp.zeros_like(vec_tiles)
    vec_tiles[0:vec_rows, 0:vec_columns] = own_vec[0]
    tiles[pl.ds(pl.multiple_of(me * 16, 16), 16), :] = vec_tiles[0:16, :].astype(BF16)
    vec_sums[...] = jnp.zeros_like(vec_sums)
    log_total[...] = jnp.zeros_like(log_total)
    for load in loads:
        load.wait()
    count = own_attn.shape[1]
    here = pl.ds(pl.multiple_of(me * count, 16), count)
    w_qkv[here, :] = stage_attn[:, : 3 * width].astype(BF16)
    w_out[here, :] = stage_attn[:, 3 * width :].astype(BF16)
    count = own_up.shape[1]
    w_up[pl.ds(pl.multiple_of(me * count, 16), count), :] = stage_up[...].astype(BF16)
    count = own_down.shape[1]
    w_down[pl.ds(pl.multiple_of(me * count, 16), count), :] = stage_down[...].astype(BF16)

    pl.semaphore_wait(barrier, total_devices - 1)


    def gather_of(index, whole, rows, halves=True):
        return Gather(ring, whole, rows, halves, send.at[index], receive.at[index])

    get_vec = gather_of(0, tiles, 16, False)
    get_qkv = gather_of(1, w_qkv, own_attn.shape[1])
    get_out = gather_of(2, w_out, own_attn.shape[1])
    get_up = gather_of(3, w_up, own_up.shape[1])
    get_down = gather_of(4, w_down, own_down.shape[1])

    reach = ring.reach
    for gather in (get_vec, get_qkv, get_out):
        gather.begin()
    for step in range(1, reach + 1):
        for gather in (get_vec, get_qkv, get_out):
            gather.step(step)
        if step == reach // 2:
            get_up.begin()
    get_up.step(1)
    get_down.begin()
    for gather in (get_vec, get_qkv, get_out):
        gather.finish()

    late = []
    for step in range(2, reach + 1):
        late.append(partial(get_up.step, step))
        late.append(partial(get_down.step, step - 1))
    late.append(get_up.finish)
    late_down = [partial(get_down.step, reach), get_down.finish]

    @pl.when(last_section)
    def _():
        for call in late + late_down:
            call()

    for device in range(devices):
        params[:, device * vec_columns : (device + 1) * vec_columns] = tiles[
            device * 16 : (device + 1) * 16, 0:vec_columns
        ].astype(F32)


    for micro in range(micro_count):
        row = crops[micro : micro + 1, :].astype(F32)
        square = jnp.broadcast_to(row, (pack, pack))
        mask[micro] = jnp.where(square == square.T, 1.0, 0.0)

    lane = lax.broadcasted_iota(jnp.int32, (1, pair_width), 1)
    in_low = lane < head_width

    def of_head(value, sub):
        return jnp.where(in_low if sub == 0 else ~in_low, value, jnp.zeros_like(value))

    def forward_micro(micro, serve):
        here = rows_of(micro)
        inputs = x_in[here, :].astype(F32)
        z, _ = norm_parts(inputs)
        hidden[here, :] = (z * params[0:1, :] + params[1:2, :]).astype(BF16)
        for part in range(3):
            value = dot_nn(hidden[here, :], w_qkv[:, part * width : (part + 1) * width])
            if part == 0:
                value = value + params[2:3, :]
            if part == 2:
                value = value + params[3:4, :]
            qkv[here, part * width : (part + 1) * width] = value.astype(BF16)
        serve(0)

        def pair(index, _):
            at = index * pair_width
            queries = qkv[here, lanes(at, pair_width)]
            keys = qkv[here, lanes(width + at, pair_width)]
            values = qkv[here, lanes(2 * width + at, pair_width)]
            outs = []
            logs = log_total[here, :]
            head_lane = lax.broadcasted_iota(jnp.int32, (1, 128), 1)
            for sub in range(2):
                scores = dot_nt(of_head(queries, sub), keys) * head_scale
                scores = jnp.where(mask[micro] > 0.5, scores, NEG_BIG)
                peak = jnp.max(scores, axis=-1, keepdims=True)
                exponent = jnp.exp(scores - peak)
                totals = jnp.sum(exponent, axis=-1, keepdims=True)
                probs = (exponent * (1.0 / totals)).astype(BF16)
                logs = jnp.where(head_lane == 2 * index + sub, peak + jnp.log(totals), logs)
                outs.append(dot_nn(probs, values))
            log_total[here, :] = logs
            mixed[here, lanes(at, pair_width)] = jnp.where(in_low, outs[0], outs[1]).astype(BF16)
            return 0

        lax.fori_loop(0, pairs, pair, 0)
        serve(1)
        middle_value = x_in[here, :].astype(F32) + (
            dot_nn(mixed[here, :], w_out[...]) + params[4:5, :]
        )
        middle[here, :] = middle_value
        z, _ = norm_parts(middle_value)
        hidden_two[here, :] = (z * params[5:6, :] + params[6:7, :]).astype(BF16)
        serve(2)
        for part in range(tiles_up):
            columns = slice(part * width, (part + 1) * width)
            upward = dot_nn(hidden_two[here, :], w_up[:, columns]) + params[8 + part : 9 + part, :]
            half = 0.5 + 0.5 * erf(upward * 0.7071067811865476)
            active[here, columns] = (upward * half).astype(BF16)
            slope[here, columns] = half + upward * (
                jnp.exp(-0.5 * upward * upward) * 0.3989422804014327
            )
        serve(3)

    def hand_over(source, target, micro):
        here = rows_of(micro)
        return remote(
            source.at[micro],
            target.at[here, :],
            across.at[0, micro],
            across.at[1, micro],
            (1 - section, me),
        )

    def forward_step(micro, _):
        @pl.when(last_section)
        def _():
            hand_over(boundary, x_in, micro).wait_recv()

        @pl.when(first_section)
        def _():
            load_tokens(micro).wait()

        def serve(point):
            @pl.when(first_section & (micro == 0))
            def _():
                split = [late[0:2], late[2:4], late[4:], []]
                for call in split[point]:
                    call()

        forward_micro(micro, serve)
        return 0

    lax.fori_loop(0, micro_count, forward_step, 0)

    @pl.when(first_section)
    def _():
        for call in late_down:
            call()

    def finish_step(micro, _):
        here = rows_of(micro)
        output = middle[here, :] + (dot_nn(active[here, :], w_down[...]) + params[7:8, :])
        boundary[micro] = output.astype(BF16)

        @pl.when(first_section)
        def _():
            hand_over(boundary, x_in, micro).start()

        return 0

    lax.fori_loop(0, micro_count, finish_step, 0)
    for gather in (get_vec, get_qkv, get_out, get_up, get_down):
        gather.drain()


    def into(ref, first):
        def put(rows, value):
            ref[rows, pl.ds(first, value.shape[1])] = value

        return put

    def reduce_of(index, whole, base, put, other, slots, halves=True, block=16):
        return Reduce(
            ring, whole, base, put, other, slots, halves, block, send.at[index], receive.at[index]
        )

    put_down = reduce_of(5, g_down, 0, into(sum_down, 0), other_down, slots_down, block=64)
    put_up = reduce_of(6, w_up, 0, into(sum_up, 0), other_up, slots_up)
    put_attn = [
        reduce_of(
            7 + part,
            w_down,
            part * width,
            into(sum_attn, part * width),
            other_attn.at[part],
            slots_attn.at[part],
            block=other_attn.shape[2],
        )
        for part in range(4)
    ]
    put_vec = reduce_of(11, vec_tiles, 0, into(sum_vec, 0), other_vec, slots_vec, False)

    def weigh_down():
        chunk = 2 * own_down.shape[1]

        def body(index, _):
            columns = lanes(index * chunk, chunk)
            g_down[pl.ds(pl.multiple_of(index * chunk, 16), chunk), :] = dot_tn(
                active[:, columns], dy_in[...]
            ).astype(BF16)
            return 0

        lax.fori_loop(0, hidden_units // chunk, body, 0)

    def add_vec(row, value):
        vec_sums[row : row + 1, :] += value

    def backward_micro(micro, serve):
        here = rows_of(micro)
        add_vec(7, column_sum(dy_in[here, :].astype(F32)))
        for part in range(tiles_up):
            columns = slice(part * width, (part + 1) * width)
            back = dot_nt(dy_in[here, :], w_down[columns, :]) * slope[here, columns]
            back = back.astype(BF16)
            grad_up[here, columns] = back
            add_vec(8 + part, column_sum(back.astype(F32)))
            more = dot_nt(back, w_up[:, columns])
            if part == 0:
                flow[...] = more
            else:
                flow[...] += more
        serve(0)
        e = flow[...]
        z, scale = norm_parts(middle[here, :])
        add_vec(5, column_sum(e * z))
        add_vec(6, column_sum(e))
        back = dy_in[here, :].astype(F32) + norm_back(z, scale, e, params[5:6, :])
        flow_two[...] = back
        back = back.astype(BF16)
        grad_branch[here, :] = back
        add_vec(4, column_sum(back.astype(F32)))
        grad_heads[...] = dot_nt(back, w_out[...]).astype(BF16)
        serve(1)

        def pair(index, _):
            at = index * pair_width
            queries = qkv[here, lanes(at, pair_width)]
            keys = qkv[here, lanes(width + at, pair_width)]
            values = qkv[here, lanes(2 * width + at, pair_width)]
            back_out = grad_heads[:, lanes(at, pair_width)]
            head_lane = lax.broadcasted_iota(jnp.int32, (1, 128), 1)
            results = []
            for sub in range(2):
                scores = dot_nt(of_head(queries, sub), keys) * head_scale
                scores = jnp.where(mask[micro] > 0.5, scores, NEG_BIG)
                logs = jnp.sum(
                    jnp.where(head_lane == 2 * index + sub, log_total[here, :], 0.0),
                    axis=-1,
                    keepdims=True,
                )
                probs = jnp.exp(scores - logs)
                back_probs = dot_nt(of_head(back_out, sub), values)
                inner = jnp.sum(back_probs * probs, axis=-1, keepdims=True)
                back_scores = (probs * (back_probs - inner)).astype(BF16)
                results.append(
                    (
                        dot_nn(back_scores, keys) * head_scale,
                        dot_tn(back_scores, queries) * head_scale,
                        dot_tn(probs.astype(BF16), back_out),
                    )
                )
            for part in range(3):
                grad_qkv[here, lanes(part * width + at, pair_width)] = jnp.where(
                    in_low, results[0][part], results[1][part]
                ).astype(BF16)
            return 0

        lax.fori_loop(0, pairs, pair, 0)
        serve(2)
        e = dot_nt(grad_qkv[here, :], w_qkv[...])
        z, scale = norm_parts(x_in[here, :].astype(F32))
        add_vec(0, column_sum(e * z))
        add_vec(1, column_sum(e))
        add_vec(2, column_sum(grad_qkv[here, 0:width].astype(F32)))
        add_vec(3, column_sum(grad_qkv[here, 2 * width : 3 * width].astype(F32)))
        back = flow_two[...] + norm_back(z, scale, e, params[0:1, :])
        input_grads[micro] = back.astype(BF16)
        serve(3)

    def backward_step(micro, _):
        @pl.when(first_section)
        def _():
            hand_over(input_grads, dy_in, micro).wait_recv()

        @pl.when(last_section)
        def _():
            load_cotangent(micro).wait()

        is_last = micro == micro_count - 1

        def serve(point):
            @pl.when(first_section & is_last)
            def _():
                if point == 0:
                    put_down.step(reach - 1)
                if point == 2:
                    put_down.step(reach - 2)

        @pl.when(first_section & is_last)
        def _():
            weigh_down()
            put_down.exchange()
            put_down.first()

        backward_micro(micro, serve)

        @pl.when(last_section)
        def _():
            hand_over(input_grads, dy_in, micro).start()

        return 0

    lax.fori_loop(0, micro_count, backward_step, 0)

    @pl.when(last_section)
    def _():
        weigh_down()
        put_down.exchange()
        put_down.first()

    third = width // 3

    def weigh(source, grad, columns, target, base):
        def body(index, _):
            rows = lanes(index * third, third)
            target[pl.ds(pl.multiple_of(base + index * third, 16), third), :] = dot_tn(
                source[:, rows], grad[:, columns]
            ).astype(BF16)
            return 0

        lax.fori_loop(0, 3, body, 0)

    weigh(hidden_two, grad_up, slice(0, hidden_units), w_up, 0)
    put_up.exchange()

    @pl.when(last_section)
    def _():
        put_down.step(reach - 1)

    put_up.first()
    for part in range(3):
        weigh(hidden, grad_qkv, slice(part * width, (part + 1) * width), w_down, part * width)
        put_attn[part].exchange()
    weigh(mixed, grad_branch, slice(0, width), w_down, 3 * width)
    put_attn[3].exchange()

    vec_tiles[...] = jnp.zeros_like(vec_tiles)
    for device in range(devices):
        vec_tiles[device * 16 : (device + 1) * 16, 0:vec_columns] = vec_sums[
            :, device * vec_columns : (device + 1) * vec_columns
        ]
    put_vec.exchange()

    @pl.when(last_section)
    def _():
        put_down.step(reach - 2)

    put_up.step(reach - 1)
    put_vec.first()
    for part in range(4):
        put_attn[part].first()
    for distance in range(reach - 3, 0, -1):
        put_down.step(distance)
    put_up.step(reach - 2)
    for part in range(4):
        put_attn[part].step(reach - 1)
    put_vec.step(reach - 1)
    put_down.last()
    for distance in range(reach - 3, 0, -1):
        put_up.step(distance)
    for distance in range(reach - 2, 0, -1):
        for part in range(4):
            put_attn[part].step(distance)
        put_vec.step(distance)
        if distance == reach - 2:
            put_up.last()
    for part in range(4):
        put_attn[part].last()
    put_vec.last()


    def squares(ref):
        value = ref[...]
        value = value * value
        while value.shape[1] > 128:
            value = sum(
                value[:, start : start + 128] for start in range(0, value.shape[1], 128)
            )
        return sum(value[start : start + 8, :] for start in range(0, value.shape[0], 8))

    norm_slots[0] = squares(sum_attn) + squares(sum_up) + squares(sum_down) + squares(sum_vec)

    def tell(distance, _):
        remote(
            norm_slots.at[0],
            norm_slots.at[distance],
            norm_sem.at[0],
            norm_sem.at[1],
            other_device(distance),
        ).start()
        return 0

    lax.fori_loop(1, total_devices, tell, 0)
    rest = norm_slots.at[pl.ds(1, total_devices - 1)]
    heard = remote(rest, rest, norm_sem.at[0], norm_sem.at[1], other_device(1))
    heard.wait_recv()
    order = jnp.zeros(norm_slots.shape[1:], F32)

    def gather_up(device, order):
        return order + norm_slots[(flat - device + total_devices) % total_devices]

    order = lax.fori_loop(0, total_devices, gather_up, order)
    total = jnp.sum(jnp.sum(order, axis=0, keepdims=True), axis=1, keepdims=True)
    norm[...] = jnp.broadcast_to(jnp.sqrt(total), norm.shape)
    heard.wait_send()


    put_down.drain()
    put_up.drain()
    for part in range(4):
        put_attn[part].drain()
    put_vec.drain()
    for micro in range(micro_count):

        @pl.when(first_section)
        def _():
            hand_over(boundary, x_in, micro).wait_send()

        @pl.when(last_section)
        def _():
            hand_over(input_grads, dy_in, micro).wait_send()


def run_layers(devices, sections, tokens, cotangent, crop_ids, attn, upward_w, downward_w, vectors):
    micro_count, pack, width = tokens.shape
    rows = micro_count * pack
    chips, reach = devices // 2, devices // 4
    hidden_units = upward_w.shape[2]
    attn_rows, up_rows, down_rows = attn.shape[1], upward_w.shape[1], downward_w.shape[1]
    in_hbm = pl.BlockSpec(memory_space=pl.ANY)
    in_vmem = pl.BlockSpec(memory_space=pltpu.VMEM)

    def other(rows_of_shard, columns, kind=BF16):
        return pltpu.VMEM((chips, rows_of_shard, columns), kind)

    def slots(rows_of_shard, columns, kind=BF16):
        return pltpu.VMEM((2, reach, rows_of_shard, columns), kind)

    scratch = [
        pltpu.VMEM((width, 3 * width), BF16),
        pltpu.VMEM((width, width), BF16),
        pltpu.VMEM((width, hidden_units), BF16),
        pltpu.VMEM((hidden_units, width), BF16),
        pltpu.VMEM((devices * 16, 128), BF16),
        pltpu.VMEM((16, width), F32),
        pltpu.VMEM((rows, width), BF16),
        pltpu.VMEM((rows, width), BF16),
        pltpu.VMEM((rows, 3 * width), BF16),
        pltpu.VMEM((rows, 128), F32),
        pltpu.VMEM((rows, width), BF16),
        pltpu.VMEM((rows, width), F32),
        pltpu.VMEM((rows, width), BF16),
        pltpu.VMEM((rows, hidden_units), F32),
        pltpu.VMEM((rows, hidden_units), BF16),
        pltpu.VMEM((micro_count, pack, pack), F32),
        pltpu.VMEM((rows, width), BF16),
        pltpu.VMEM((rows, hidden_units), BF16),
        pltpu.VMEM((rows, width), BF16),
        pltpu.VMEM((pack, width), BF16),
        pltpu.VMEM((rows, 3 * width), BF16),
        pltpu.VMEM((pack, width), F32),
        pltpu.VMEM((pack, width), F32),
        pltpu.VMEM((16, width), F32),
        pltpu.VMEM((devices * 16, 128), F32),
        pltpu.VMEM((hidden_units, width), BF16),
        other(down_rows, width),
        other(up_rows, hidden_units),
        pltpu.VMEM((4, chips, attn_rows, width), BF16),
        other(16, 128, F32),
        slots(down_rows, width),
        slots(up_rows, hidden_units),
        pltpu.VMEM((4, 2, reach, attn_rows, width), BF16),
        slots(16, 128, F32),
        pltpu.VMEM((sections * devices, 8, 128), F32),
        pltpu.SemaphoreType.DMA((3 + micro_count,)),
        pltpu.SemaphoreType.DMA((12, 3, 2 * reach)),
        pltpu.SemaphoreType.DMA((12, 3, 2 * reach)),
        pltpu.SemaphoreType.DMA((2, micro_count)),
        pltpu.SemaphoreType.DMA((2,)),
    ]
    return pl.pallas_call(
        partial(layer_kernel, devices, sections),
        out_shape=[
            jax.ShapeDtypeStruct(tokens.shape, BF16),
            jax.ShapeDtypeStruct(tokens.shape, BF16),
            jax.ShapeDtypeStruct(attn.shape[1:], F32),
            jax.ShapeDtypeStruct(upward_w.shape[1:], F32),
            jax.ShapeDtypeStruct(downward_w.shape[1:], F32),
            jax.ShapeDtypeStruct((16, 128), F32),
            jax.ShapeDtypeStruct((8, 128), F32),
        ],
        in_specs=[in_hbm, in_hbm, in_vmem, in_hbm, in_hbm, in_hbm, in_vmem],
        out_specs=[in_vmem] * 7,
        scratch_shapes=scratch,
        compiler_params=pltpu.CompilerParams(
            collective_id=0, has_side_effects=True, vmem_limit_bytes=VMEM_LIMIT
        ),
        name="two_layers",
    )(tokens, cotangent, crop_ids, attn, upward_w, downward_w, vectors)


def adam_kernel(norm, *refs):
    grads, states, results = refs[:4], refs[4:16], refs[16:28]
    clip_factor = jnp.minimum(1.0, MAX_NORM / (norm[0:1, 0:1] + 1e-06))
    for index in range(4):
        master, moment_one, moment_two = (states[index + 4 * part] for part in range(3))
        shape = master.shape[1:]
        gradient = grads[index][0 : shape[0], 0 : shape[1]] * clip_factor
        decay, rate = (0.0, VECTOR_RATE) if index == 3 else (DECAY_RATE, RATE)
        updated = adam_update(master[0], gradient, moment_one[0], moment_two[0], decay, rate)
        for part in range(3):
            results[index + 4 * part][0] = updated[part]


def run_adam(norm, grads, states):
    steps = 3

    def cut(shape):
        block = shape[:-2] + (shape[-2] // steps, shape[-1])
        lead = (0,) * (len(shape) - 2)
        return pl.BlockSpec(block, lambda i: lead + (i, 0))

    def keep(shape):
        lead = (0,) * len(shape)
        return pl.BlockSpec(shape, lambda i: lead)

    def spec(index, array):
        return keep(array.shape) if index % 4 == 3 else cut(array.shape)

    state_specs = [spec(i, a) for i, a in enumerate(states)]
    return pl.pallas_call(
        adam_kernel,
        grid=(steps,),
        out_shape=[jax.ShapeDtypeStruct(a.shape, F32) for a in states],
        in_specs=[keep(norm.shape)] + [spec(i, a) for i, a in enumerate(grads)] + state_specs,
        out_specs=state_specs,
        compiler_params=pltpu.CompilerParams(vmem_limit_bytes=VMEM_LIMIT),
        name="adam",
    )(norm, *grads, *states)


def layer_norm(features, gain_row, shift_row):
    center = jnp.mean(features, axis=-1, keepdims=True)
    centered = features - center
    spread = jnp.mean(centered * centered, axis=-1, keepdims=True)
    return centered * lax.rsqrt(spread + LN_EPS) * gain_row + shift_row


def split_heads(packed, micro_count, model_width):
    shaped = packed.reshape(micro_count, -1, 3, HEADS, model_width // HEADS)
    return (shaped[:, :, 0], shaped[:, :, 1], shaped[:, :, 2])


def attention_scores(queries, keys_block, crop_rows):
    head_scale = queries.shape[-1] ** (-0.5)
    scores = (
        jnp.einsum("mqhd,mkhd->mhqk", queries, keys_block, preferred_element_type=F32) * head_scale
    )
    same_crop = crop_rows[:, :, None] == crop_rows[:, None, :]
    return jnp.where(same_crop[:, None], scores, NEG_BIG)


def forward_layer(inputs, crop_rows, weights):
    attn, upward_w, downward_w, vectors_b = weights
    model_width = attn.shape[0]
    rows = inputs.shape[0]
    params = vectors_b.astype(F32)
    hidden = layer_norm(inputs, params[0], params[1]).astype(BF16)
    qkv_bias = jnp.concatenate([params[2], jnp.zeros_like(params[2]), params[3]])
    packed = (
        jnp.dot(hidden, attn[:, : 3 * model_width], preferred_element_type=F32) + qkv_bias
    ).astype(BF16)
    queries, keys_block, values_block = split_heads(packed, crop_rows.shape[0], model_width)
    scores = attention_scores(queries, keys_block, crop_rows)
    row_peak = jnp.max(scores, axis=-1, keepdims=True)
    exponent = jnp.exp(scores - row_peak)
    totals = jnp.sum(exponent, axis=-1, keepdims=True)
    soft_weights = (exponent / totals).astype(BF16)
    log_total = row_peak + jnp.log(totals)
    mixed = jnp.einsum("mhqk,mkhd->mqhd", soft_weights, values_block, preferred_element_type=F32)
    mixed = mixed.reshape(rows, model_width).astype(BF16)
    middle = inputs + (
        jnp.dot(mixed, attn[:, 3 * model_width :], preferred_element_type=F32) + params[4]
    )
    hidden_two = layer_norm(middle, params[5], params[6]).astype(BF16)
    upward = jnp.dot(hidden_two, upward_w, preferred_element_type=F32) + params[8:].reshape(-1)
    active = jax.nn.gelu(upward, approximate=False).astype(BF16)
    output = middle + (jnp.dot(active, downward_w, preferred_element_type=F32) + params[7])
    return (output, (inputs, hidden, packed, log_total, mixed, middle, hidden_two, upward, active))


def backward_layer(kept, crop_rows, grad_out, weights, with_grads):
    attn, upward_w, downward_w, vectors_b = weights
    inputs, hidden, packed, log_total, mixed, middle, hidden_two, upward, active = kept
    model_width = attn.shape[0]
    rows = inputs.shape[0]
    params = vectors_b.astype(F32)
    grad_down = grad_out.astype(BF16)
    grad_active = jnp.einsum("pj,ij->pi", grad_down, downward_w, preferred_element_type=F32)
    gelu_back = jax.vjp(partial(jax.nn.gelu, approximate=False), upward)[1]
    grad_up = gelu_back(grad_active)[0].astype(BF16)
    grad_hidden_two = jnp.einsum("pj,ij->pi", grad_up, upward_w, preferred_element_type=F32)
    norm_back_two = jax.vjp(layer_norm, middle, params[5], params[6])[1]
    grad_middle_part, grad_gain_two, grad_shift_two = norm_back_two(grad_hidden_two)
    grad_middle = grad_out + grad_middle_part
    grad_branch = grad_middle.astype(BF16)
    grad_mixed = jnp.einsum(
        "pj,ij->pi", grad_branch, attn[:, 3 * model_width :], preferred_element_type=F32
    ).astype(BF16)
    micro_count = crop_rows.shape[0]
    queries, keys_block, values_block = split_heads(packed, micro_count, model_width)
    scores = attention_scores(queries, keys_block, crop_rows)
    probs = jnp.exp(scores - log_total)
    grad_heads = grad_mixed.reshape(micro_count, -1, HEADS, model_width // HEADS)
    grad_probs = jnp.einsum("mqhd,mkhd->mhqk", grad_heads, values_block, preferred_element_type=F32)
    grad_values = jnp.einsum(
        "mhqk,mqhd->mkhd", probs.astype(BF16), grad_heads, preferred_element_type=F32
    )
    grad_scores = (
        probs * (grad_probs - jnp.sum(grad_probs * probs, axis=-1, keepdims=True))
    ).astype(BF16)
    head_scale = queries.shape[-1] ** (-0.5)
    grad_queries = (
        jnp.einsum("mhqk,mkhd->mqhd", grad_scores, keys_block, preferred_element_type=F32)
        * head_scale
    )
    grad_keys = (
        jnp.einsum("mhqk,mqhd->mkhd", grad_scores, queries, preferred_element_type=F32) * head_scale
    )
    grad_packed = jnp.concatenate(
        [
            grad_queries.reshape(rows, model_width),
            grad_keys.reshape(rows, model_width),
            grad_values.reshape(rows, model_width),
        ],
        axis=1,
    ).astype(BF16)
    grad_hidden = jnp.einsum(
        "pj,ij->pi", grad_packed, attn[:, : 3 * model_width], preferred_element_type=F32
    )
    norm_back_one = jax.vjp(layer_norm, inputs, params[0], params[1])[1]
    grad_in_part, grad_gain_one, grad_shift_one = norm_back_one(grad_hidden)
    grad_inputs = grad_middle + grad_in_part
    if not with_grads:
        return (grad_inputs, None)
    grad_w_down = jnp.einsum("pi,pj->ij", active, grad_down, preferred_element_type=F32)
    grad_w_up = jnp.einsum("pi,pj->ij", hidden_two, grad_up, preferred_element_type=F32)
    grad_w_out = jnp.einsum("pi,pj->ij", mixed, grad_branch, preferred_element_type=F32)
    grad_w_qkv = jnp.einsum("pi,pj->ij", hidden, grad_packed, preferred_element_type=F32)
    packed_sums = jnp.sum(grad_packed, axis=0, dtype=F32)
    vector_rows = jnp.stack(
        [
            grad_gain_one,
            grad_shift_one,
            packed_sums[:model_width],
            packed_sums[2 * model_width :],
            jnp.sum(grad_branch, axis=0, dtype=F32),
            grad_gain_two,
            grad_shift_two,
            jnp.sum(grad_down, axis=0, dtype=F32),
        ]
    )
    up_bias_rows = jnp.sum(grad_up, axis=0, dtype=F32).reshape(-1, model_width)
    grad_vectors = jnp.concatenate([vector_rows, up_bias_rows], axis=0)
    grad_attn = jnp.concatenate([grad_w_qkv, grad_w_out], axis=1)
    return (grad_inputs, (grad_attn, grad_w_up, grad_w_down, grad_vectors))


def adam_update(master, gradient, moment_one, moment_two, decay_rate, step_rate):
    new_one = BETA_ONE * moment_one + (1.0 - BETA_ONE) * gradient
    new_two = BETA_TWO * moment_two + (1.0 - BETA_TWO) * gradient * gradient
    ratio = (
        new_one / (1.0 - BETA_ONE**STEP) / (jnp.sqrt(new_two / (1.0 - BETA_TWO**STEP)) + ADAM_EPS)
    )
    return (master - step_rate * (ratio + decay_rate * master), new_one, new_two)


def shards_by_kernels(devices, sections, tokens, cotangent, crop_ids, *states):
    boundary, input_grads, attn, upward_w, downward_w, vectors, norm = run_layers(
        devices, sections, tokens, cotangent, crop_ids, *states[:4]
    )
    updated = run_adam(norm, (attn, upward_w, downward_w, vectors), states)
    return (boundary[None], input_grads[None], norm[0, 0]) + tuple(updated)


def shards_by_collectives(devices, sections, tokens, cotangent, crop_ids, *states):
    section_index = lax.axis_index("section")
    flat = (-1, tokens.shape[2])
    masters, firsts, seconds = states[:4], states[4:8], states[8:]
    shards = [master[0].astype(BF16) for master in masters]
    weights = tuple(
        lax.all_gather(shard, "dp", axis=axis, tiled=True) for shard, axis in zip(shards, (0, 0, 0, 1))
    )
    own_tokens = tokens.reshape(flat)
    first_output, _ = forward_layer(own_tokens.astype(F32), crop_ids, weights)
    received = lax.ppermute(first_output.astype(BF16), "section", [(0, 1)])
    layer_input = jnp.where(section_index == 0, own_tokens, received)
    output, kept = forward_layer(layer_input.astype(F32), crop_ids, weights)
    boundary = output.astype(BF16).reshape(tokens.shape)
    own_grad = cotangent.reshape(flat)
    first_back, _ = backward_layer(kept, crop_ids, own_grad.astype(F32), weights, False)
    back_received = lax.ppermute(first_back.astype(BF16), "section", [(1, 0)])
    grad_out = jnp.where(section_index == 1, own_grad, back_received).astype(F32)
    grad_inputs, gradients = backward_layer(kept, crop_ids, grad_out, weights, True)
    input_grads = grad_inputs.astype(BF16).reshape(tokens.shape)
    reduced = tuple(
        lax.psum_scatter(gradient, "dp", scatter_dimension=axis, tiled=True)
        for gradient, axis in zip(gradients, (0, 0, 0, 1))
    )
    squares = sum(jnp.sum(member * member) for member in reduced)
    grad_norm = jnp.sqrt(lax.psum(squares, ("section", "dp")))
    clip_factor = jnp.minimum(1.0, MAX_NORM / (grad_norm + 1e-06))
    decays = (DECAY_RATE, DECAY_RATE, DECAY_RATE, 0.0)
    rates = (RATE, RATE, RATE, VECTOR_RATE)
    updated = [
        adam_update(master[0], gradient * clip_factor, one[0], two[0], decay_rate, step_rate)
        for master, gradient, one, two, decay_rate, step_rate in zip(
            masters, reduced, firsts, seconds, decays, rates
        )
    ]
    new_states = tuple(entry[part][None] for part in range(3) for entry in updated)
    return (boundary[None], input_grads[None], grad_norm) + new_states


def shards(devices, sections, tokens, cotangent, crop_ids, *states):
    whole_tiles = (
        devices % 8 == 0
        and all(state.shape[1] % 16 == 0 for state in states[:3])
        and states[2].shape[1] % 64 == 0
        and states[3].shape[1] <= 16
        and states[3].shape[2] <= 128
    )
    run = shards_by_kernels if whole_tiles else shards_by_collectives
    return run(devices, sections, tokens, cotangent, crop_ids, *states)


def solution(mesh):
    token_spec = P(None, "dp", None)
    row_spec = P("section", "dp", None)
    column_spec = P("section", None, "dp")
    state = (row_spec, row_spec, row_spec, column_spec)
    micro_spec = P("section", None, "dp", None)
    return jax.shard_map(
        partial(shards, mesh.shape["dp"], mesh.shape["section"]),
        mesh=mesh,
        in_specs=(token_spec, token_spec, P(None, "dp")) + 3 * state,
        out_specs=(micro_spec, micro_spec, P()) + 3 * state,
        check_vma=False,
    )
```

```python
from functools import partial

import jax
import jax.numpy as jnp
from jax import lax
from jax.experimental import pallas as pl
from jax.experimental.pallas import tpu as pltpu
from jax.sharding import PartitionSpec as P

HEADS = 12
STEP = 10
LN_EPS = 1e-06
NEG_BIG = -1e30
BETA_ONE = 0.9
BETA_TWO = 0.999
RATE = 0.1
VECTOR_RATE = 0.5
DECAY_RATE = 0.01
ADAM_EPS = 1e-08
MAX_NORM = 1.0
MESH = pl.DeviceIdType.MESH
VMEM_LIMIT = 60 * 2**20
F32 = jnp.float32
BF16 = jnp.bfloat16


class Ring:
    def __init__(self, devices):
        self.devices = devices
        self.chips = devices // 2
        self.reach = self.chips // 2
        self.me = lax.axis_index("dp")
        self.core = self.me % 2
        chip = self.me // 2
        row, column = chip // 2, chip % 2
        self.place = row * (1 - column) + (self.chips - 1 - row) * column

    def device(self, place, core):
        place = (place + 2 * self.chips) % self.chips
        column = place // self.reach
        row = place * (1 - column) + (self.chips - 1 - place) * column
        return (row * 2 + column) * 2 + core

    def target(self, device):
        return (lax.axis_index("section"), device)

    def right(self):
        return self.target(self.device(self.place + 1, self.core))

    def left(self):
        return self.target(self.device(self.place - 1, self.core))

    def sibling(self):
        return self.target(self.device(self.place, 1 - self.core))


def remote(source, target, send, receive, device):
    return pltpu.make_async_remote_copy(
        src_ref=source,
        dst_ref=target,
        send_sem=send,
        recv_sem=receive,
        device_id=device,
        device_id_type=MESH,
    )


class Shards:
    def __init__(self, ring, whole, rows, stride=None, base=0, first=0, columns=None):
        self.ring, self.whole, self.rows = ring, whole, rows
        self.stride = rows if stride is None else stride
        self.base, self.first = base, first
        self.columns = whole.shape[1] if columns is None else columns

    def row(self, distance, core):
        device = self.ring.device(self.ring.place + distance, core)
        return pl.multiple_of(device * self.stride + self.base, 16)

    def view(self, distance, core, part=None):
        rows = pl.ds(self.row(distance, core), self.rows)
        if part is None:
            return self.whole.at[rows, pl.ds(self.first, self.columns)]
        columns = self.columns // 2
        return self.whole.at[rows, pl.ds(self.first + part * columns, columns)]

    def of_bytes(self, count):
        return self.whole.at[pl.ds(0, count * self.rows), pl.ds(self.first, self.columns)]


class Gather:
    def __init__(self, shards, halves, sent, shared, arrived):
        self.ring, self.shards, self.halves = shards.ring, shards, halves
        self.sent, self.shared, self.arrived = sent, shared, arrived

    def hop(self, way, step, came):
        ring = self.ring
        direction = 1 if way == 0 else -1
        part = None
        if step == ring.reach:
            if self.halves:
                part = way
            elif way == 1:
                return None
        view = self.shards.view(-direction * (step if came else step - 1), ring.core, part)
        device = ring.right() if way == 0 else ring.left()
        return remote(view, view, self.sent, self.arrived.at[way, step - 1], device)

    def push(self, way, step):
        copy = self.hop(way, step, False)
        if copy is not None:
            copy.start()

    def arrive(self, way, step):
        copy = self.hop(way, step, True)
        if copy is not None:
            copy.wait_recv()

    def share(self, distance):
        view = self.shards.view(distance, self.ring.core)
        remote(view, view, self.sent, self.shared, self.ring.sibling()).start()

    def begin(self):
        self.push(0, 1)
        self.push(1, 1)
        self.share(0)

    def step(self, step):
        reach = self.ring.reach
        self.arrive(0, step)
        if step < reach:
            self.push(0, step + 1)
        self.arrive(1, step)
        if step < reach:
            self.push(1, step + 1)
            self.share(-step)
            self.share(step)
        else:
            self.share(reach)

    def bytes_of(self, count):
        view = self.shards.of_bytes(count)
        return remote(view, view, self.sent, self.shared, self.ring.sibling())

    def finish(self):
        self.bytes_of(self.ring.chips).wait_recv()

    def drain(self):
        self.bytes_of(2 * self.ring.chips - 1).wait_send()


class Reduce:
    def __init__(self, shards, put, other, slots, halves, block, sent, swapped, arrived):
        self.ring, self.shards, self.put = shards.ring, shards, put
        self.other, self.slots, self.halves, self.block = other, slots, halves, block
        self.sent, self.swapped, self.arrived = sent, swapped, arrived

    def keys(self):
        reach = self.ring.reach
        order = [(reach, 0)]
        for distance in range(reach - 1, 0, -1):
            order += [(distance, 2 * (reach - distance) - 1), (-distance, 2 * (reach - distance))]
        return order + [(0, 2 * reach - 1)]

    def key(self, distance):
        return dict(self.keys())[distance]

    def swap(self, distance):
        key = self.key(distance)
        remote(
            self.shards.view(distance, 1 - self.ring.core),
            self.other.at[key],
            self.sent,
            self.swapped.at[min(key, 1)],
            self.ring.sibling(),
        ).start()

    def exchange(self):
        for distance, _ in self.keys():
            self.swap(distance)

    def exchanged(self, first):
        slots = self.other.at[pl.ds(0, 1)] if first else self.other.at[pl.ds(1, self.ring.chips - 1)]
        semaphore = self.swapped.at[0 if first else 1]
        remote(slots, slots, self.sent, semaphore, self.ring.sibling()).wait_recv()

    def slot(self, way, distance):
        ref = self.slots.at[way, distance - 1]
        if distance == self.ring.reach and self.halves:
            columns = ref.shape[1] // 2
            return ref.at[:, pl.ds(way * columns, columns)]
        return ref

    def hop(self, way, distance, came):
        ring = self.ring
        if distance == ring.reach and not self.halves and way == 1:
            return None
        slot = self.slot(way, distance)
        source = slot
        if not came:
            part = way if distance == ring.reach and self.halves else None
            source = self.shards.view(distance if way == 0 else -distance, ring.core, part)
        device = ring.right() if way == 0 else ring.left()
        return remote(source, slot, self.sent, self.arrived.at[way, distance - 1], device)

    def push(self, way, distance):
        copy = self.hop(way, distance, False)
        if copy is not None:
            copy.start()

    def arrive(self, way, distance):
        copy = self.hop(way, distance, True)
        if copy is not None:
            copy.wait_recv()

    def add(self, distance, arrivals, final=False):
        ring, shards = self.ring, self.shards
        key = self.key(distance)
        base = shards.row(distance, ring.core)
        block = self.block
        half = shards.columns // 2
        columns = pl.ds(shards.first, shards.columns)

        def body(index, _):
            here = pl.ds(pl.multiple_of(base + index * block, 16), block)
            rows = pl.ds(pl.multiple_of(index * block, block), block)
            total = shards.whole[here, columns].astype(F32) + self.other[key, rows, :].astype(F32)
            for way, far in arrivals:
                if far == ring.reach and self.halves:
                    low, high = total[:, :half], total[:, half:]
                    if way == 0:
                        low = low + self.slots[way, far - 1, rows, :half].astype(F32)
                    else:
                        high = high + self.slots[way, far - 1, rows, half:].astype(F32)
                    total = jnp.concatenate([low, high], axis=1)
                elif far < ring.reach or way == 0:
                    total = total + self.slots[way, far - 1, rows, :].astype(F32)
            if final:
                self.put(rows, total)
            else:
                shards.whole[here, columns] = total.astype(shards.whole.dtype)
            return 0

        lax.fori_loop(0, shards.rows // block, body, 0)

    def first(self):
        reach = self.ring.reach
        self.exchanged(True)
        self.add(reach, [])
        self.push(0, reach)
        self.push(1, reach)

    def step(self, distance):
        if distance == self.ring.reach - 1:
            self.exchanged(False)
        self.arrive(0, distance + 1)
        self.add(distance, [(0, distance + 1)])
        self.push(0, distance)
        self.arrive(1, distance + 1)
        self.add(-distance, [(1, distance + 1)])
        self.push(1, distance)

    def last(self):
        self.arrive(0, 1)
        self.arrive(1, 1)
        self.add(0, [(0, 1), (1, 1)], True)

    def drain(self):
        view = self.shards.of_bytes(2 * self.ring.chips - 1)
        remote(view, view, self.sent, self.swapped.at[0], self.ring.sibling()).wait_send()


def dot_nn(a, b):
    return lax.dot_general(a, b, (((1,), (0,)), ((), ())), preferred_element_type=F32)


def dot_nt(a, b):
    return lax.dot_general(a, b, (((1,), (1,)), ((), ())), preferred_element_type=F32)


def dot_tn(a, b):
    return lax.dot_general(a, b, (((0,), (0,)), ((), ())), preferred_element_type=F32)


def gelu_parts(value):
    bell = jnp.exp(-0.5 * value * value)
    t = 1.0 / (1.0 + (0.3275911 * 0.7071067811865476) * jnp.abs(value))
    tail = 0.5 * 1.061405429
    for factor in (-1.453152027, 1.421413741, -0.284496736, 0.254829592):
        tail = tail * t + 0.5 * factor
    tail = tail * t * bell
    return jnp.where(value >= 0.0, 1.0 - tail, tail), bell * 0.3989422804014327


def norm_parts(features):
    center = jnp.mean(features, axis=-1, keepdims=True)
    centered = features - center
    spread = jnp.mean(centered * centered, axis=-1, keepdims=True)
    scale = lax.rsqrt(spread + LN_EPS)
    return centered * scale, scale


def norm_back(z, scale, e, gain):
    t = e * gain
    return (
        t - jnp.mean(t, axis=-1, keepdims=True) - z * jnp.mean(t * z, axis=-1, keepdims=True)
    ) * scale


def column_sum(value):
    return jnp.sum(value, axis=0, keepdims=True)


def layer_kernel(
    devices,
    sections,
    tokens,
    cotangent,
    crops_in,
    own_attn,
    own_up,
    own_down,
    own_vec_in,
    boundary_out,
    input_grads_out,
    sum_attn,
    sum_up,
    sum_down,
    sum_vec,
    norm,
    crops,
    own_vec,
    boundary,
    input_grads,
    w_attn,
    w_up,
    w_down,
    tiles,
    params,
    x_in,
    hidden,
    qkv,
    log_total,
    mixed,
    middle,
    hidden_two,
    slope,
    active,
    mask,
    dy_in,
    grad_up,
    grad_branch,
    grad_heads,
    grad_qkv,
    flow,
    flow_two,
    vec_sums,
    vec_tiles,
    g_down,
    other_down,
    other_up,
    other_attn,
    other_vec,
    slots_down,
    slots_up,
    slots_attn,
    slots_vec,
    norm_slots,
    local,
    gather_sems,
    gather_ways,
    reduce_sems,
    reduce_ways,
    across,
    norm_sem,
):
    section = lax.axis_index("section")
    first_section = section == 0
    last_section = section == 1
    ring = Ring(devices)
    me = ring.me
    micro_count, pack = tokens.shape[0], tokens.shape[1]
    width = tokens.shape[2]
    hidden_units = w_up.shape[1]
    tiles_up = hidden_units // width
    head_width = width // HEADS
    pairs = HEADS // 2
    unroll = 3
    pair_width = 2 * head_width
    head_scale = head_width ** (-0.5)
    vec_rows, vec_columns = own_vec.shape[0], own_vec.shape[2]

    def rows_of(micro):
        return pl.ds(pl.multiple_of(micro * pack, 16), pack)

    def lanes(start, count):
        return pl.ds(pl.multiple_of(start, 128), count)


    stage_attn = slope.at[pl.ds(0, own_attn.shape[1]), :]
    stage_up = slope.at[pl.ds(own_attn.shape[1], own_up.shape[1]), :]
    stage_down = middle.at[pl.ds(0, own_down.shape[1]), :]
    loads = [
        pltpu.make_async_copy(own_attn.at[0], stage_attn, local.at[0]),
        pltpu.make_async_copy(own_up.at[0], stage_up, local.at[1]),
        pltpu.make_async_copy(own_down.at[0], stage_down, local.at[2]),
        pltpu.make_async_copy(own_vec_in, own_vec, local.at[3]),
        pltpu.make_async_copy(crops_in, crops, local.at[4]),
    ]
    for load in loads:
        load.start()

    def load_tokens(micro):
        return pltpu.make_async_copy(tokens.at[micro], x_in.at[rows_of(micro), :], local.at[5 + micro])

    def load_cotangent(micro):
        return pltpu.make_async_copy(
            cotangent.at[micro], dy_in.at[rows_of(micro), :], local.at[5 + micro]
        )

    @pl.when(first_section)
    def _():
        for micro in range(micro_count):
            load_tokens(micro).start()

    @pl.when(last_section)
    def _():
        for micro in range(micro_count):
            load_cotangent(micro).start()

    barrier = pltpu.get_barrier_semaphore()
    neighbours = (ring.right(), ring.left(), ring.sibling(), (1 - section, me))
    for device in neighbours:
        pl.semaphore_signal(barrier, inc=1, device_id=device, device_id_type=MESH)

    vec_tiles[...] = jnp.zeros_like(vec_tiles)
    vec_sums[...] = jnp.zeros_like(vec_sums)
    for load in loads:
        load.wait()
    vec_tiles[0:vec_rows, 0:vec_columns] = own_vec[:, 0, :]
    tiles[pl.ds(pl.multiple_of(me * 16, 16), 16), :] = vec_tiles[0:16, :].astype(BF16)
    count = own_attn.shape[1]
    here = pl.ds(pl.multiple_of(me * count, 16), count)
    w_attn[here, :] = stage_attn[...].astype(BF16)
    count = own_up.shape[1]
    w_up[pl.ds(pl.multiple_of(me * count, 16), count), :] = stage_up[...].astype(BF16)
    count = own_down.shape[1]
    w_down[pl.ds(pl.multiple_of(me * count, 16), count), :] = stage_down[...].astype(BF16)

    pl.semaphore_wait(barrier, len(neighbours))


    def gather_of(index, shards, halves=True):
        return Gather(
            shards,
            halves,
            gather_sems.at[index, 0],
            gather_sems.at[index, 1],
            gather_ways.at[index],
        )

    down_rows = own_down.shape[1]
    get_vec = gather_of(0, Shards(ring, tiles, 16), False)
    get_attn = gather_of(1, Shards(ring, w_attn, own_attn.shape[1]))
    get_up = gather_of(2, Shards(ring, w_up, own_up.shape[1]))
    get_down = [
        gather_of(3 + part, Shards(ring, w_down, down_rows // 2, down_rows, part * down_rows // 2))
        for part in range(2)
    ]

    def down_step(step):
        for gather in get_down:
            gather.step(step)

    def down_finish():
        for gather in get_down:
            gather.finish()

    reach = ring.reach
    get_vec.begin()
    get_attn.begin()
    for step in range(1, reach + 1):
        get_vec.step(step)
        get_attn.step(step)
        if step == reach // 2:
            get_up.begin()
    get_up.step(1)
    for gather in get_down:
        gather.begin()
    get_vec.finish()
    get_attn.finish()

    late = []
    for step in range(2, reach + 1):
        late.append(partial(get_up.step, step))
        late.append(partial(down_step, step - 1))
    late.append(get_up.finish)
    late_down = [partial(down_step, reach), down_finish]

    @pl.when(last_section)
    def _():
        for call in late + late_down:
            call()

    for device in range(devices):
        params[:, device * vec_columns : (device + 1) * vec_columns] = tiles[
            device * 16 : (device + 1) * 16, 0:vec_columns
        ].astype(F32)


    for micro in range(micro_count):
        row = crops[micro : micro + 1, :].astype(F32)
        square = jnp.broadcast_to(row, (pack, pack))
        mask[micro] = jnp.where(square == square.T, 1.0, 0.0)

    lane = lax.broadcasted_iota(jnp.int32, (1, pair_width), 1)
    in_low = lane < head_width

    def of_head(value, sub):
        return jnp.where(in_low if sub == 0 else ~in_low, value, jnp.zeros_like(value))

    def forward_micro(micro, serve):
        here = rows_of(micro)
        inputs = x_in[here, :].astype(F32)
        z, _ = norm_parts(inputs)
        hidden[here, :] = (z * params[0:1, :] + params[1:2, :]).astype(BF16)
        for part in range(3):
            value = dot_nn(hidden[here, :], w_attn[:, part * width : (part + 1) * width])
            if part == 0:
                value = value + params[2:3, :]
            if part == 2:
                value = value + params[3:4, :]
            qkv[here, part * width : (part + 1) * width] = value.astype(BF16)
        serve(0)

        def pair(index, _):
            at = index * pair_width
            queries = qkv[here, lanes(at, pair_width)]
            keys = qkv[here, lanes(width + at, pair_width)]
            values = qkv[here, lanes(2 * width + at, pair_width)]
            scores = [dot_nt(keys, of_head(queries, sub)) for sub in range(2)]
            outs = []
            for sub in range(2):
                value = jnp.where(mask[micro] > 0.5, scores[sub] * head_scale, NEG_BIG)
                peak = jnp.max(value, axis=0, keepdims=True)
                exponent = jnp.exp(value - peak)
                totals = jnp.sum(exponent, axis=0, keepdims=True)
                probs = (exponent * (1.0 / totals)).astype(BF16)
                log_total[pl.ds(micro * HEADS + 2 * index + sub, 1), :] = peak + jnp.log(totals)
                outs.append(dot_tn(probs, values))
            mixed[here, lanes(at, pair_width)] = jnp.where(in_low, outs[0], outs[1]).astype(BF16)
            return 0

        lax.fori_loop(0, pairs, pair, 0, unroll=unroll)
        serve(1)
        middle_value = x_in[here, :].astype(F32) + (
            dot_nn(mixed[here, :], w_attn[:, 3 * width :]) + params[4:5, :]
        )
        middle[here, :] = middle_value
        z, _ = norm_parts(middle_value)
        hidden_two[here, :] = (z * params[5:6, :] + params[6:7, :]).astype(BF16)
        serve(2)
        for part in range(tiles_up):
            columns = slice(part * width, (part + 1) * width)
            upward = dot_nn(hidden_two[here, :], w_up[:, columns]) + params[8 + part : 9 + part, :]
            area, density = gelu_parts(upward)
            active[here, columns] = (upward * area).astype(BF16)
            slope[here, columns] = area + upward * density
        serve(3)

    def hand_over(source, target, micro):
        here = rows_of(micro)
        return remote(
            source.at[micro],
            target.at[here, :],
            across.at[0, micro],
            across.at[1, micro],
            (1 - section, me),
        )

    def forward_step(micro, _):
        @pl.when(last_section)
        def _():
            hand_over(boundary, x_in, micro).wait_recv()

        @pl.when(first_section)
        def _():
            load_tokens(micro).wait()

        def serve(point):
            @pl.when(first_section & (micro == 0))
            def _():
                split = [late[0:2], late[2:4], late[4:], []]
                for call in split[point]:
                    call()

        forward_micro(micro, serve)
        return 0

    lax.fori_loop(0, micro_count, forward_step, 0)

    @pl.when(first_section)
    def _():
        for call in late_down:
            call()

    def finish_step(micro, _):
        here = rows_of(micro)
        output = middle[here, :] + (dot_nn(active[here, :], w_down[...]) + params[7:8, :])
        boundary[micro] = output.astype(BF16)

        @pl.when(first_section)
        def _():
            hand_over(boundary, x_in, micro).start()

        return 0

    lax.fori_loop(0, micro_count, finish_step, 0)
    for gather in (get_vec, get_attn, get_up, *get_down):
        gather.drain()
    pltpu.make_async_copy(boundary, boundary_out, local.at[0]).start()


    def into(ref, first):
        def put(rows, value):
            ref[rows, pl.ds(first, value.shape[1])] = value

        return put

    def reduce_of(index, shards, put, other, slots, halves=True, block=16):
        return Reduce(
            shards,
            put,
            other,
            slots,
            halves,
            block,
            reduce_sems.at[index, 0],
            reduce_sems.at[index, pl.ds(1, 2)],
            reduce_ways.at[index],
        )

    put_down = reduce_of(
        0, Shards(ring, g_down, down_rows), into(sum_down, 0), other_down, slots_down, block=64
    )
    put_up = reduce_of(
        1, Shards(ring, w_up, own_up.shape[1]), into(sum_up, 0), other_up, slots_up
    )
    half_attn = w_attn.shape[1] // 2
    put_attn = [
        reduce_of(
            2 + part,
            Shards(ring, w_attn, own_attn.shape[1], first=part * half_attn, columns=half_attn),
            into(sum_attn, part * half_attn),
            other_attn.at[part],
            slots_attn.at[part],
        )
        for part in range(2)
    ]
    put_vec = reduce_of(
        4, Shards(ring, vec_tiles, 16), into(sum_vec, 0), other_vec, slots_vec, False
    )

    chunk = 2 * down_rows

    def weigh_down(distance):
        start = ring.device(ring.place + distance, 0) * down_rows
        columns = lanes(start, chunk)
        g_down[pl.ds(pl.multiple_of(start, 16), chunk), :] = dot_tn(
            active[:, columns], dy_in[...]
        ).astype(BF16)
        put_down.swap(distance)

    def start_down():
        for index, (distance, _) in enumerate(put_down.keys()):
            weigh_down(distance)
            if index == 1:
                put_down.first()
        put_down.step(reach - 1)

    def add_vec(row, value):
        vec_sums[row : row + 1, :] += value

    def backward_micro(micro, serve):
        here = rows_of(micro)
        add_vec(7, column_sum(dy_in[here, :].astype(F32)))
        for part in range(tiles_up):
            columns = slice(part * width, (part + 1) * width)
            back = dot_nt(dy_in[here, :], w_down[columns, :]) * slope[here, columns]
            back = back.astype(BF16)
            grad_up[here, columns] = back
            add_vec(8 + part, column_sum(back.astype(F32)))
            more = dot_nt(back, w_up[:, columns])
            if part == 0:
                flow[...] = more
            else:
                flow[...] += more
        serve(0)
        e = flow[...]
        z, scale = norm_parts(middle[here, :])
        add_vec(5, column_sum(e * z))
        add_vec(6, column_sum(e))
        back = dy_in[here, :].astype(F32) + norm_back(z, scale, e, params[5:6, :])
        flow_two[...] = back
        back = back.astype(BF16)
        grad_branch[here, :] = back
        add_vec(4, column_sum(back.astype(F32)))
        grad_heads[...] = dot_nt(back, w_attn[:, 3 * width :]).astype(BF16)
        serve(1)

        def pair(index, _):
            at = index * pair_width
            queries = qkv[here, lanes(at, pair_width)]
            keys = qkv[here, lanes(width + at, pair_width)]
            values = qkv[here, lanes(2 * width + at, pair_width)]
            back_out = grad_heads[:, lanes(at, pair_width)]
            scores = [dot_nt(keys, of_head(queries, sub)) for sub in range(2)]
            back_probs = [dot_nt(values, of_head(back_out, sub)) for sub in range(2)]
            results = []
            for sub in range(2):
                value = jnp.where(mask[micro] > 0.5, scores[sub] * head_scale, NEG_BIG)
                probs = jnp.exp(
                    value - log_total[pl.ds(micro * HEADS + 2 * index + sub, 1), :]
                )
                inner = jnp.sum(back_probs[sub] * probs, axis=0, keepdims=True)
                back_scores = (probs * (back_probs[sub] - inner)).astype(BF16)
                results.append(
                    (
                        dot_tn(back_scores, keys) * head_scale,
                        dot_nn(back_scores, queries) * head_scale,
                        dot_nn(probs.astype(BF16), back_out),
                    )
                )
            for part in range(3):
                grad_qkv[here, lanes(part * width + at, pair_width)] = jnp.where(
                    in_low, results[0][part], results[1][part]
                ).astype(BF16)
            return 0

        lax.fori_loop(0, pairs, pair, 0, unroll=unroll)
        serve(2)
        e = dot_nt(grad_qkv[here, :], w_attn[:, : 3 * width])
        z, scale = norm_parts(x_in[here, :].astype(F32))
        add_vec(0, column_sum(e * z))
        add_vec(1, column_sum(e))
        add_vec(2, column_sum(grad_qkv[here, 0:width].astype(F32)))
        add_vec(3, column_sum(grad_qkv[here, 2 * width : 3 * width].astype(F32)))
        back = flow_two[...] + norm_back(z, scale, e, params[0:1, :])
        input_grads[micro] = back.astype(BF16)
        serve(3)

    def backward_step(micro, _):
        @pl.when(first_section)
        def _():
            hand_over(input_grads, dy_in, micro).wait_recv()

        @pl.when(last_section)
        def _():
            load_cotangent(micro).wait()

        is_last = micro == micro_count - 1

        def serve(point):
            @pl.when(first_section & is_last)
            def _():
                if point == 1:
                    put_down.step(reach - 2)
                if point == 3:
                    for distance in range(reach - 3, 0, -1):
                        put_down.step(distance)

        @pl.when(first_section & is_last)
        def _():
            start_down()

        backward_micro(micro, serve)

        @pl.when(last_section)
        def _():
            hand_over(input_grads, dy_in, micro).start()

        return 0

    lax.fori_loop(0, micro_count, backward_step, 0)

    copy_input_grads = pltpu.make_async_copy(input_grads, input_grads_out, local.at[1])
    copy_input_grads.start()

    @pl.when(last_section)
    def _():
        start_down()

    third = width // 3

    def weigh(source, grad, target, first):
        def body(index, _):
            target[
                pl.ds(pl.multiple_of(index * third, 16), third),
                pl.ds(first, grad.shape[1]),
            ] = dot_tn(source[:, lanes(index * third, third)], grad[...]).astype(BF16)
            return 0

        lax.fori_loop(0, 3, body, 0)

    weigh(hidden_two, grad_up, w_up, 0)
    put_up.exchange()

    @pl.when(last_section)
    def _():
        put_down.step(reach - 2)

    put_up.first()
    vec_tiles[...] = jnp.zeros_like(vec_tiles)
    for device in range(devices):
        vec_tiles[device * 16 : (device + 1) * 16, 0:vec_columns] = vec_sums[
            :, device * vec_columns : (device + 1) * vec_columns
        ]
    put_vec.exchange()
    weigh(hidden, grad_qkv, w_attn, 0)
    put_attn[0].exchange()
    weigh(mixed, grad_branch, w_attn, 3 * width)
    put_attn[1].exchange()

    @pl.when(last_section)
    def _():
        for distance in range(reach - 3, 0, -1):
            put_down.step(distance)

    put_vec.first()
    put_up.step(reach - 1)
    put_down.last()
    for part in range(2):
        put_attn[part].first()
    put_up.step(reach - 2)
    put_vec.step(reach - 1)
    for part in range(2):
        put_attn[part].step(reach - 1)
    for distance in range(reach - 2, 0, -1):
        if distance > 1:
            put_up.step(distance - 1)
        else:
            put_up.last()
        put_vec.step(distance)
        for part in range(2):
            put_attn[part].step(distance)
    put_vec.last()
    for part in range(2):
        put_attn[part].last()


    def squares(ref):
        value = ref[...]
        value = value * value
        while value.shape[1] > 128:
            value = sum(
                value[:, start : start + 128] for start in range(0, value.shape[1], 128)
            )
        return sum(value[start : start + 8, :] for start in range(0, value.shape[0], 8))

    total_devices = sections * devices
    flat = section * devices + me

    def other_device(distance):
        other = (flat + distance) % total_devices
        return (other // devices, other % devices)

    norm_slots[0] = squares(sum_attn) + squares(sum_up) + squares(sum_down) + squares(sum_vec)

    def tell(distance, _):
        remote(
            norm_slots.at[0],
            norm_slots.at[distance],
            norm_sem.at[0],
            norm_sem.at[1],
            other_device(distance),
        ).start()
        return 0

    lax.fori_loop(1, total_devices, tell, 0)
    rest = norm_slots.at[pl.ds(1, total_devices - 1)]
    heard = remote(rest, rest, norm_sem.at[0], norm_sem.at[1], other_device(1))
    heard.wait_recv()

    def collect(device, order):
        return order + norm_slots[(flat - device + total_devices) % total_devices]

    order = lax.fori_loop(0, total_devices, collect, jnp.zeros(norm_slots.shape[1:], F32))
    total = jnp.sum(jnp.sum(order, axis=0, keepdims=True), axis=1, keepdims=True)
    norm[0, 0] = jnp.sqrt(total)[0, 0]
    heard.wait_send()


    for reduce in (put_down, put_up, *put_attn, put_vec):
        reduce.drain()
    pltpu.make_async_copy(boundary, boundary_out, local.at[0]).wait()
    copy_input_grads.wait()
    for micro in range(micro_count):

        @pl.when(first_section)
        def _():
            hand_over(boundary, x_in, micro).wait_send()

        @pl.when(last_section)
        def _():
            hand_over(input_grads, dy_in, micro).wait_send()


def run_layers(devices, sections, tokens, cotangent, crop_ids, attn, upward_w, downward_w, vectors):
    micro_count, pack, width = tokens.shape
    rows = micro_count * pack
    chips, reach = devices // 2, devices // 4
    hidden_units = upward_w.shape[2]
    attn_rows, up_rows, down_rows = attn.shape[1], upward_w.shape[1], downward_w.shape[1]
    in_hbm = pl.BlockSpec(memory_space=pl.ANY)
    in_vmem = pl.BlockSpec(memory_space=pltpu.VMEM)

    def other(rows_of_shard, columns, kind=BF16):
        return pltpu.VMEM((chips, rows_of_shard, columns), kind)

    def slots(rows_of_shard, columns, kind=BF16):
        return pltpu.VMEM((2, reach, rows_of_shard, columns), kind)

    scratch = [
        pltpu.VMEM(crop_ids.shape, jnp.int32),
        pltpu.VMEM(vectors.shape, F32),
        pltpu.VMEM(tokens.shape, BF16),
        pltpu.VMEM(tokens.shape, BF16),
        pltpu.VMEM((width, attn.shape[2]), BF16),
        pltpu.VMEM((width, hidden_units), BF16),
        pltpu.VMEM((hidden_units, width), BF16),
        pltpu.VMEM((devices * 16, 128), BF16),
        pltpu.VMEM((16, width), F32),
        pltpu.VMEM((rows, width), BF16),
        pltpu.VMEM((rows, width), BF16),
        pltpu.VMEM((rows, 3 * width), BF16),
        pltpu.VMEM((micro_count * HEADS, pack), F32),
        pltpu.VMEM((rows, width), BF16),
        pltpu.VMEM((rows, width), F32),
        pltpu.VMEM((rows, width), BF16),
        pltpu.VMEM((rows, hidden_units), F32),
        pltpu.VMEM((rows, hidden_units), BF16),
        pltpu.VMEM((micro_count, pack, pack), F32),
        pltpu.VMEM((rows, width), BF16),
        pltpu.VMEM((rows, hidden_units), BF16),
        pltpu.VMEM((rows, width), BF16),
        pltpu.VMEM((pack, width), BF16),
        pltpu.VMEM((rows, 3 * width), BF16),
        pltpu.VMEM((pack, width), F32),
        pltpu.VMEM((pack, width), F32),
        pltpu.VMEM((16, width), F32),
        pltpu.VMEM((devices * 16, 128), F32),
        pltpu.VMEM((hidden_units, width), BF16),
        other(down_rows, width),
        other(up_rows, hidden_units),
        pltpu.VMEM((2, chips, attn_rows, attn.shape[2] // 2), BF16),
        other(16, 128, F32),
        slots(down_rows, width),
        slots(up_rows, hidden_units),
        pltpu.VMEM((2, 2, reach, attn_rows, attn.shape[2] // 2), BF16),
        slots(16, 128, F32),
        pltpu.VMEM((sections * devices, 8, 128), F32),
        pltpu.SemaphoreType.DMA((5 + micro_count,)),
        pltpu.SemaphoreType.DMA((5, 2)),
        pltpu.SemaphoreType.DMA((5, 2, reach)),
        pltpu.SemaphoreType.DMA((5, 3)),
        pltpu.SemaphoreType.DMA((5, 2, reach)),
        pltpu.SemaphoreType.DMA((2, micro_count)),
        pltpu.SemaphoreType.DMA((2,)),
    ]
    return pl.pallas_call(
        partial(layer_kernel, devices, sections),
        out_shape=[
            jax.ShapeDtypeStruct(tokens.shape, BF16),
            jax.ShapeDtypeStruct(tokens.shape, BF16),
            jax.ShapeDtypeStruct(attn.shape[1:], F32),
            jax.ShapeDtypeStruct(upward_w.shape[1:], F32),
            jax.ShapeDtypeStruct(downward_w.shape[1:], F32),
            jax.ShapeDtypeStruct((16, 128), F32),
            jax.ShapeDtypeStruct((1, 1), F32),
        ],
        in_specs=[in_hbm] * 7,
        out_specs=[in_hbm] * 2 + [in_vmem] * 4 + [pl.BlockSpec(memory_space=pltpu.SMEM)],
        scratch_shapes=scratch,
        compiler_params=pltpu.CompilerParams(
            collective_id=0, has_side_effects=True, vmem_limit_bytes=VMEM_LIMIT
        ),
        name="two_layers",
    )(tokens, cotangent, crop_ids, attn, upward_w, downward_w, vectors)


def adam_kernel(boundary, input_grads, norm, *refs):
    grads, states, out_boundary, out_input, out_norm = refs[:4], refs[4:16], *refs[16:19]
    results, held, passing = refs[19:31], refs[31], refs[32]
    step = pl.program_id(0)
    take = [
        pltpu.make_async_copy(source, held.at[i], passing.at[i])
        for i, source in enumerate((boundary, input_grads))
    ]
    hand_on = [
        pltpu.make_async_copy(held.at[i], target, passing.at[i])
        for i, target in enumerate((out_boundary, out_input))
    ]

    @pl.when(step == 0)
    def _():
        for copy in take:
            copy.start()
        out_norm[0, 0] = norm[0, 0]

    @pl.when(step == 1)
    def _():
        for first, second in zip(take, hand_on):
            first.wait()
            second.start()

    clip_factor = jnp.minimum(1.0, MAX_NORM / (jnp.full((1, 1), norm[0, 0]) + 1e-06))
    for index in range(4):
        master, moment_one, moment_two = (states[index + 4 * part] for part in range(3))
        vectors = index == 3
        shape = (master.shape[0], master.shape[2]) if vectors else master.shape[1:]
        gradient = grads[index][0 : shape[0], 0 : shape[1]] * clip_factor
        old = [ref[:, 0, :] if vectors else ref[0] for ref in (master, moment_one, moment_two)]
        decay, rate = (0.0, VECTOR_RATE) if vectors else (DECAY_RATE, RATE)
        updated = adam_update(old[0], gradient, old[1], old[2], decay, rate)
        for part in range(3):
            if vectors:
                results[index + 4 * part][:, 0, :] = updated[part]
            else:
                results[index + 4 * part][0] = updated[part]

    @pl.when(step == pl.num_programs(0) - 1)
    def _():
        for copy in hand_on:
            copy.wait()


def run_adam(boundary, input_grads, attn, upward_w, downward_w, vectors, norm, states):
    grads = (attn, upward_w, downward_w, vectors)
    steps = 2

    def cut(shape):
        block = shape[:-2] + (shape[-2] // steps, shape[-1])
        lead = (0,) * (len(shape) - 2)
        return pl.BlockSpec(block, lambda i: lead + (i, 0))

    def keep(shape):
        lead = (0,) * len(shape)
        return pl.BlockSpec(shape, lambda i: lead)

    def spec(index, array):
        return keep(array.shape) if index % 4 == 3 else cut(array.shape)

    in_hbm = pl.BlockSpec(memory_space=pl.ANY)
    scalar = pl.BlockSpec(memory_space=pltpu.SMEM)
    state_specs = [spec(i, a) for i, a in enumerate(states)]
    return pl.pallas_call(
        adam_kernel,
        grid=(steps,),
        out_shape=[
            jax.ShapeDtypeStruct(boundary.shape, BF16),
            jax.ShapeDtypeStruct(input_grads.shape, BF16),
            jax.ShapeDtypeStruct((1, 1), F32),
        ]
        + [jax.ShapeDtypeStruct(a.shape, F32) for a in states],
        in_specs=[in_hbm, in_hbm, scalar] + [spec(i, a) for i, a in enumerate(grads)] + state_specs,
        out_specs=[in_hbm, in_hbm, scalar] + state_specs,
        scratch_shapes=[pltpu.VMEM((2,) + boundary.shape, BF16), pltpu.SemaphoreType.DMA((2,))],
        compiler_params=pltpu.CompilerParams(vmem_limit_bytes=VMEM_LIMIT),
        name="adam",
    )(boundary, input_grads, norm, *grads, *states)


def layer_norm(features, gain_row, shift_row):
    center = jnp.mean(features, axis=-1, keepdims=True)
    centered = features - center
    spread = jnp.mean(centered * centered, axis=-1, keepdims=True)
    return centered * lax.rsqrt(spread + LN_EPS) * gain_row + shift_row


def split_heads(packed, micro_count, model_width):
    shaped = packed.reshape(micro_count, -1, 3, HEADS, model_width // HEADS)
    return (shaped[:, :, 0], shaped[:, :, 1], shaped[:, :, 2])


def attention_scores(queries, keys_block, crop_rows):
    head_scale = queries.shape[-1] ** (-0.5)
    scores = (
        jnp.einsum("mqhd,mkhd->mhqk", queries, keys_block, preferred_element_type=F32) * head_scale
    )
    same_crop = crop_rows[:, :, None] == crop_rows[:, None, :]
    return jnp.where(same_crop[:, None], scores, NEG_BIG)


def forward_layer(inputs, crop_rows, weights):
    attn, upward_w, downward_w, vectors_b = weights
    model_width = attn.shape[0]
    rows = inputs.shape[0]
    params = vectors_b.astype(F32)
    hidden = layer_norm(inputs, params[0], params[1]).astype(BF16)
    qkv_bias = jnp.concatenate([params[2], jnp.zeros_like(params[2]), params[3]])
    packed = (
        jnp.dot(hidden, attn[:, : 3 * model_width], preferred_element_type=F32) + qkv_bias
    ).astype(BF16)
    queries, keys_block, values_block = split_heads(packed, crop_rows.shape[0], model_width)
    scores = attention_scores(queries, keys_block, crop_rows)
    row_peak = jnp.max(scores, axis=-1, keepdims=True)
    exponent = jnp.exp(scores - row_peak)
    totals = jnp.sum(exponent, axis=-1, keepdims=True)
    soft_weights = (exponent / totals).astype(BF16)
    log_total = row_peak + jnp.log(totals)
    mixed = jnp.einsum("mhqk,mkhd->mqhd", soft_weights, values_block, preferred_element_type=F32)
    mixed = mixed.reshape(rows, model_width).astype(BF16)
    middle = inputs + (
        jnp.dot(mixed, attn[:, 3 * model_width :], preferred_element_type=F32) + params[4]
    )
    hidden_two = layer_norm(middle, params[5], params[6]).astype(BF16)
    upward = jnp.dot(hidden_two, upward_w, preferred_element_type=F32) + params[8:].reshape(-1)
    active = jax.nn.gelu(upward, approximate=False).astype(BF16)
    output = middle + (jnp.dot(active, downward_w, preferred_element_type=F32) + params[7])
    return (output, (inputs, hidden, packed, log_total, mixed, middle, hidden_two, upward, active))


def backward_layer(kept, crop_rows, grad_out, weights, with_grads):
    attn, upward_w, downward_w, vectors_b = weights
    inputs, hidden, packed, log_total, mixed, middle, hidden_two, upward, active = kept
    model_width = attn.shape[0]
    rows = inputs.shape[0]
    params = vectors_b.astype(F32)
    grad_down = grad_out.astype(BF16)
    grad_active = jnp.einsum("pj,ij->pi", grad_down, downward_w, preferred_element_type=F32)
    gelu_back = jax.vjp(partial(jax.nn.gelu, approximate=False), upward)[1]
    grad_up = gelu_back(grad_active)[0].astype(BF16)
    grad_hidden_two = jnp.einsum("pj,ij->pi", grad_up, upward_w, preferred_element_type=F32)
    norm_back_two = jax.vjp(layer_norm, middle, params[5], params[6])[1]
    grad_middle_part, grad_gain_two, grad_shift_two = norm_back_two(grad_hidden_two)
    grad_middle = grad_out + grad_middle_part
    grad_branch = grad_middle.astype(BF16)
    grad_mixed = jnp.einsum(
        "pj,ij->pi", grad_branch, attn[:, 3 * model_width :], preferred_element_type=F32
    ).astype(BF16)
    micro_count = crop_rows.shape[0]
    queries, keys_block, values_block = split_heads(packed, micro_count, model_width)
    scores = attention_scores(queries, keys_block, crop_rows)
    probs = jnp.exp(scores - log_total)
    grad_heads = grad_mixed.reshape(micro_count, -1, HEADS, model_width // HEADS)
    grad_probs = jnp.einsum("mqhd,mkhd->mhqk", grad_heads, values_block, preferred_element_type=F32)
    grad_values = jnp.einsum(
        "mhqk,mqhd->mkhd", probs.astype(BF16), grad_heads, preferred_element_type=F32
    )
    grad_scores = (
        probs * (grad_probs - jnp.sum(grad_probs * probs, axis=-1, keepdims=True))
    ).astype(BF16)
    head_scale = queries.shape[-1] ** (-0.5)
    grad_queries = (
        jnp.einsum("mhqk,mkhd->mqhd", grad_scores, keys_block, preferred_element_type=F32)
        * head_scale
    )
    grad_keys = (
        jnp.einsum("mhqk,mqhd->mkhd", grad_scores, queries, preferred_element_type=F32) * head_scale
    )
    grad_packed = jnp.concatenate(
        [
            grad_queries.reshape(rows, model_width),
            grad_keys.reshape(rows, model_width),
            grad_values.reshape(rows, model_width),
        ],
        axis=1,
    ).astype(BF16)
    grad_hidden = jnp.einsum(
        "pj,ij->pi", grad_packed, attn[:, : 3 * model_width], preferred_element_type=F32
    )
    norm_back_one = jax.vjp(layer_norm, inputs, params[0], params[1])[1]
    grad_in_part, grad_gain_one, grad_shift_one = norm_back_one(grad_hidden)
    grad_inputs = grad_middle + grad_in_part
    if not with_grads:
        return (grad_inputs, None)
    grad_w_down = jnp.einsum("pi,pj->ij", active, grad_down, preferred_element_type=F32)
    grad_w_up = jnp.einsum("pi,pj->ij", hidden_two, grad_up, preferred_element_type=F32)
    grad_w_out = jnp.einsum("pi,pj->ij", mixed, grad_branch, preferred_element_type=F32)
    grad_w_qkv = jnp.einsum("pi,pj->ij", hidden, grad_packed, preferred_element_type=F32)
    packed_sums = jnp.sum(grad_packed, axis=0, dtype=F32)
    vector_rows = jnp.stack(
        [
            grad_gain_one,
            grad_shift_one,
            packed_sums[:model_width],
            packed_sums[2 * model_width :],
            jnp.sum(grad_branch, axis=0, dtype=F32),
            grad_gain_two,
            grad_shift_two,
            jnp.sum(grad_down, axis=0, dtype=F32),
        ]
    )
    up_bias_rows = jnp.sum(grad_up, axis=0, dtype=F32).reshape(-1, model_width)
    grad_vectors = jnp.concatenate([vector_rows, up_bias_rows], axis=0)
    grad_attn = jnp.concatenate([grad_w_qkv, grad_w_out], axis=1)
    return (grad_inputs, (grad_attn, grad_w_up, grad_w_down, grad_vectors))


def adam_update(master, gradient, moment_one, moment_two, decay_rate, step_rate):
    new_one = BETA_ONE * moment_one + (1.0 - BETA_ONE) * gradient
    new_two = BETA_TWO * moment_two + (1.0 - BETA_TWO) * gradient * gradient
    ratio = (
        new_one / (1.0 - BETA_ONE**STEP) / (jnp.sqrt(new_two / (1.0 - BETA_TWO**STEP)) + ADAM_EPS)
    )
    return (master - step_rate * (ratio + decay_rate * master), new_one, new_two)


def shards_by_kernels(devices, sections, tokens, cotangent, crop_ids, *states):
    states = [state.transpose(1, 0, 2) if i % 4 == 3 else state for i, state in enumerate(states)]
    sums = run_layers(devices, sections, tokens, cotangent, crop_ids, *states[:4])
    boundary, input_grads, grad_norm, *updated = run_adam(*sums, states)
    updated = [state.transpose(1, 0, 2) if i % 4 == 3 else state for i, state in enumerate(updated)]
    return (boundary[None], input_grads[None], grad_norm.reshape(())) + tuple(updated)


def shards_by_collectives(devices, sections, tokens, cotangent, crop_ids, *states):
    section_index = lax.axis_index("section")
    flat = (-1, tokens.shape[2])
    masters, firsts, seconds = states[:4], states[4:8], states[8:]
    shards = [master[0].astype(BF16) for master in masters]
    weights = tuple(
        lax.all_gather(shard, "dp", axis=axis, tiled=True) for shard, axis in zip(shards, (0, 0, 0, 1))
    )
    own_tokens = tokens.reshape(flat)
    first_output, _ = forward_layer(own_tokens.astype(F32), crop_ids, weights)
    received = lax.ppermute(first_output.astype(BF16), "section", [(0, 1)])
    layer_input = jnp.where(section_index == 0, own_tokens, received)
    output, kept = forward_layer(layer_input.astype(F32), crop_ids, weights)
    boundary = output.astype(BF16).reshape(tokens.shape)
    own_grad = cotangent.reshape(flat)
    first_back, _ = backward_layer(kept, crop_ids, own_grad.astype(F32), weights, False)
    back_received = lax.ppermute(first_back.astype(BF16), "section", [(1, 0)])
    grad_out = jnp.where(section_index == 1, own_grad, back_received).astype(F32)
    grad_inputs, gradients = backward_layer(kept, crop_ids, grad_out, weights, True)
    input_grads = grad_inputs.astype(BF16).reshape(tokens.shape)
    reduced = tuple(
        lax.psum_scatter(gradient, "dp", scatter_dimension=axis, tiled=True)
        for gradient, axis in zip(gradients, (0, 0, 0, 1))
    )
    squares = sum(jnp.sum(member * member) for member in reduced)
    grad_norm = jnp.sqrt(lax.psum(squares, ("section", "dp")))
    clip_factor = jnp.minimum(1.0, MAX_NORM / (grad_norm + 1e-06))
    decays = (DECAY_RATE, DECAY_RATE, DECAY_RATE, 0.0)
    rates = (RATE, RATE, RATE, VECTOR_RATE)
    updated = [
        adam_update(master[0], gradient * clip_factor, one[0], two[0], decay_rate, step_rate)
        for master, gradient, one, two, decay_rate, step_rate in zip(
            masters, reduced, firsts, seconds, decays, rates
        )
    ]
    new_states = tuple(entry[part][None] for part in range(3) for entry in updated)
    return (boundary[None], input_grads[None], grad_norm) + new_states


def shards(devices, sections, tokens, cotangent, crop_ids, *states):
    whole_tiles = (
        devices % 8 == 0
        and all(state.shape[1] % 16 == 0 for state in states[:3])
        and states[2].shape[1] % 64 == 0
        and states[3].shape[1] <= 16
        and states[3].shape[2] <= 128
    )
    run = shards_by_kernels if whole_tiles else shards_by_collectives
    return run(devices, sections, tokens, cotangent, crop_ids, *states)


def solution(mesh):
    token_spec = P(None, "dp", None)
    row_spec = P("section", "dp", None)
    column_spec = P("section", None, "dp")
    state = (row_spec, row_spec, row_spec, column_spec)
    micro_spec = P("section", None, "dp", None)
    return jax.shard_map(
        partial(shards, mesh.shape["dp"], mesh.shape["section"]),
        mesh=mesh,
        in_specs=(token_spec, token_spec, P(None, "dp")) + 3 * state,
        out_specs=(micro_spec, micro_spec, P()) + 3 * state,
        check_vma=False,
    )
```

```python
from functools import partial

import jax
import jax.numpy as jnp
from jax import lax
from jax.experimental import pallas as pl
from jax.experimental.pallas import tpu as pltpu
from jax.sharding import PartitionSpec as P

HEADS = 12
STEP = 10
LN_EPS = 1e-06
NEG_BIG = -1e30
BETA_ONE = 0.9
BETA_TWO = 0.999
RATE = 0.1
VECTOR_RATE = 0.5
DECAY_RATE = 0.01
ADAM_EPS = 1e-08
MAX_NORM = 1.0
MESH = pl.DeviceIdType.MESH
VMEM_LIMIT = 60 * 2**20
F32 = jnp.float32
BF16 = jnp.bfloat16


class Ring:
    def __init__(self, devices):
        self.devices = devices
        self.chips = devices // 2
        self.reach = self.chips // 2
        self.me = lax.axis_index("dp")
        self.core = self.me % 2
        chip = self.me // 2
        row, column = chip // 2, chip % 2
        self.place = row * (1 - column) + (self.chips - 1 - row) * column

    def device(self, place, core):
        place = (place + 2 * self.chips) % self.chips
        column = place // self.reach
        row = place * (1 - column) + (self.chips - 1 - place) * column
        return (row * 2 + column) * 2 + core

    def target(self, device):
        return (lax.axis_index("section"), device)

    def right(self):
        return self.target(self.device(self.place + 1, self.core))

    def left(self):
        return self.target(self.device(self.place - 1, self.core))

    def sibling(self):
        return self.target(self.device(self.place, 1 - self.core))


def remote(source, target, send, receive, device):
    return pltpu.make_async_remote_copy(
        src_ref=source,
        dst_ref=target,
        send_sem=send,
        recv_sem=receive,
        device_id=device,
        device_id_type=MESH,
    )


class Shards:
    def __init__(self, ring, whole, rows, stride=None, base=0, first=0, columns=None):
        self.ring, self.whole, self.rows = ring, whole, rows
        self.stride = rows if stride is None else stride
        self.base, self.first = base, first
        self.columns = whole.shape[1] if columns is None else columns

    def row(self, distance, core):
        device = self.ring.device(self.ring.place + distance, core)
        return pl.multiple_of(device * self.stride + self.base, 16)

    def view(self, distance, core, part=None):
        rows = pl.ds(self.row(distance, core), self.rows)
        if part is None:
            return self.whole.at[rows, pl.ds(self.first, self.columns)]
        columns = self.columns // 2
        return self.whole.at[rows, pl.ds(self.first + part * columns, columns)]

    def of_bytes(self, count):
        return self.whole.at[pl.ds(0, count * self.rows), pl.ds(self.first, self.columns)]


class Gather:
    def __init__(self, shards, halves, sent, shared, arrived):
        self.ring, self.shards, self.halves = shards.ring, shards, halves
        self.sent, self.shared, self.arrived = sent, shared, arrived

    def hop(self, way, step, came):
        ring = self.ring
        direction = 1 if way == 0 else -1
        part = None
        if step == ring.reach:
            if self.halves:
                part = way
            elif way == 1:
                return None
        view = self.shards.view(-direction * (step if came else step - 1), ring.core, part)
        device = ring.right() if way == 0 else ring.left()
        return remote(view, view, self.sent, self.arrived.at[way, step - 1], device)

    def push(self, way, step):
        copy = self.hop(way, step, False)
        if copy is not None:
            copy.start()

    def arrive(self, way, step):
        copy = self.hop(way, step, True)
        if copy is not None:
            copy.wait_recv()

    def share(self, distance):
        view = self.shards.view(distance, self.ring.core)
        remote(view, view, self.sent, self.shared, self.ring.sibling()).start()

    def begin(self):
        self.push(0, 1)
        self.push(1, 1)
        self.share(0)

    def step(self, step):
        reach = self.ring.reach
        self.arrive(0, step)
        if step < reach:
            self.push(0, step + 1)
        self.arrive(1, step)
        if step < reach:
            self.push(1, step + 1)
            self.share(-step)
            self.share(step)
        else:
            self.share(reach)

    def bytes_of(self, count):
        view = self.shards.of_bytes(count)
        return remote(view, view, self.sent, self.shared, self.ring.sibling())

    def finish(self):
        self.bytes_of(self.ring.chips).wait_recv()

    def drain(self):
        self.bytes_of(2 * self.ring.chips - 1).wait_send()


class Relay(Gather):
    def __init__(self, shards, home, away, sent, arrived, crossed):
        super().__init__(shards, True, sent, None, arrived)
        self.home, self.away, self.crossed = home, away, crossed

    def across(self, source, target, semaphore):
        section = lax.axis_index("section")
        return remote(source, target, self.sent, semaphore, (1 - section, self.ring.me))

    def lend(self):
        core = self.ring.core
        for home, away in zip(self.home, self.away):
            self.across(home.view(0, core), away.view(0, core), self.crossed.at[0]).start()

    def borrow(self):
        view = self.shards.view(0, self.ring.core)
        self.across(view, view, self.crossed.at[0]).wait_recv()

    def share(self, distance):
        if distance == 0:
            return
        core = self.ring.core
        for index, (home, away) in enumerate(zip(self.home, self.away)):
            self.across(
                away.view(distance, core), home.view(distance, core), self.crossed.at[1 + index]
            ).start()

    def take(self, index):
        view = self.home[index].of_bytes(self.ring.chips - 1)
        self.across(view, view, self.crossed.at[1 + index]).wait_recv()

    def drain(self):
        view = self.shards.of_bytes(2 * self.ring.chips - 2)
        self.across(view, view, self.crossed.at[0]).wait_send()

    def drain_lent(self):
        view = self.shards.of_bytes(1)
        self.across(view, view, self.crossed.at[0]).wait_send()


class Pieces(Gather):
    def __init__(self, shards, sent, shared):
        super().__init__(shards, True, sent, shared, None)

    def share_rest(self):
        for distance in range(1 - self.ring.reach, self.ring.reach + 1):
            if distance != 0:
                self.share(distance)

    def drain(self):
        self.bytes_of(self.ring.chips).wait_send()


class Reduce:
    def __init__(self, shards, put, other, slots, halves, block, sent, swapped, arrived):
        self.ring, self.shards, self.put = shards.ring, shards, put
        self.other, self.slots, self.halves, self.block = other, slots, halves, block
        self.sent, self.swapped, self.arrived = sent, swapped, arrived

    def keys(self):
        reach = self.ring.reach
        order = [(reach, 0)]
        for distance in range(reach - 1, 0, -1):
            order += [(distance, 2 * (reach - distance) - 1), (-distance, 2 * (reach - distance))]
        return order + [(0, 2 * reach - 1)]

    def key(self, distance):
        return dict(self.keys())[distance]

    def swap(self, distance):
        key = self.key(distance)
        remote(
            self.shards.view(distance, 1 - self.ring.core),
            self.other.at[key],
            self.sent,
            self.swapped.at[min(key, 1)],
            self.ring.sibling(),
        ).start()

    def exchange(self):
        for distance, _ in self.keys():
            self.swap(distance)

    def exchanged(self, first):
        slots = self.other.at[pl.ds(0, 1)] if first else self.other.at[pl.ds(1, self.ring.chips - 1)]
        semaphore = self.swapped.at[0 if first else 1]
        remote(slots, slots, self.sent, semaphore, self.ring.sibling()).wait_recv()

    def slot(self, way, distance):
        ref = self.slots.at[way, distance - 1]
        if distance == self.ring.reach and self.halves:
            columns = ref.shape[1] // 2
            return ref.at[:, pl.ds(way * columns, columns)]
        return ref

    def hop(self, way, distance, came):
        ring = self.ring
        if distance == ring.reach and not self.halves and way == 1:
            return None
        slot = self.slot(way, distance)
        source = slot
        if not came:
            part = way if distance == ring.reach and self.halves else None
            source = self.shards.view(distance if way == 0 else -distance, ring.core, part)
        device = ring.right() if way == 0 else ring.left()
        return remote(source, slot, self.sent, self.arrived.at[way, distance - 1], device)

    def push(self, way, distance):
        copy = self.hop(way, distance, False)
        if copy is not None:
            copy.start()

    def arrive(self, way, distance):
        copy = self.hop(way, distance, True)
        if copy is not None:
            copy.wait_recv()

    def add(self, distance, arrivals, final=False):
        ring, shards = self.ring, self.shards
        key = self.key(distance)
        base = shards.row(distance, ring.core)
        block = self.block
        half = shards.columns // 2
        columns = pl.ds(shards.first, shards.columns)

        def body(index, _):
            here = pl.ds(pl.multiple_of(base + index * block, 16), block)
            rows = pl.ds(pl.multiple_of(index * block, block), block)
            total = shards.whole[here, columns].astype(F32) + self.other[key, rows, :].astype(F32)
            for way, far in arrivals:
                if far == ring.reach and self.halves:
                    low, high = total[:, :half], total[:, half:]
                    if way == 0:
                        low = low + self.slots[way, far - 1, rows, :half].astype(F32)
                    else:
                        high = high + self.slots[way, far - 1, rows, half:].astype(F32)
                    total = jnp.concatenate([low, high], axis=1)
                elif far < ring.reach or way == 0:
                    total = total + self.slots[way, far - 1, rows, :].astype(F32)
            if final:
                self.put(index * block, total)
            else:
                shards.whole[here, columns] = total.astype(shards.whole.dtype)
            return 0

        lax.fori_loop(0, shards.rows // block, body, 0)

    def first(self):
        reach = self.ring.reach
        self.exchanged(True)
        self.add(reach, [])
        self.push(0, reach)
        self.push(1, reach)

    def step(self, distance):
        if distance == self.ring.reach - 1:
            self.exchanged(False)
        self.arrive(0, distance + 1)
        self.add(distance, [(0, distance + 1)])
        self.push(0, distance)
        self.arrive(1, distance + 1)
        self.add(-distance, [(1, distance + 1)])
        self.push(1, distance)

    def last(self):
        self.arrive(0, 1)
        self.arrive(1, 1)
        self.add(0, [(0, 1), (1, 1)], True)

    def drain(self):
        view = self.shards.of_bytes(2 * self.ring.chips - 1)
        remote(view, view, self.sent, self.swapped.at[0], self.ring.sibling()).wait_send()


def dot_nn(a, b):
    return lax.dot_general(a, b, (((1,), (0,)), ((), ())), preferred_element_type=F32)


def dot_nt(a, b):
    return lax.dot_general(a, b, (((1,), (1,)), ((), ())), preferred_element_type=F32)


def dot_tn(a, b):
    return lax.dot_general(a, b, (((0,), (0,)), ((), ())), preferred_element_type=F32)


def gelu_parts(value):
    bell = jnp.exp(-0.5 * value * value)
    t = 1.0 / (1.0 + (0.3275911 * 0.7071067811865476) * jnp.abs(value))
    tail = 0.5 * 1.061405429
    for factor in (-1.453152027, 1.421413741, -0.284496736, 0.254829592):
        tail = tail * t + 0.5 * factor
    tail = tail * t * bell
    return jnp.where(value >= 0.0, 1.0 - tail, tail), bell * 0.3989422804014327


def norm_parts(features):
    center = jnp.mean(features, axis=-1, keepdims=True)
    centered = features - center
    spread = jnp.mean(centered * centered, axis=-1, keepdims=True)
    scale = lax.rsqrt(spread + LN_EPS)
    return centered * scale, scale


def norm_back(z, scale, e, gain):
    t = e * gain
    return (
        t - jnp.mean(t, axis=-1, keepdims=True) - z * jnp.mean(t * z, axis=-1, keepdims=True)
    ) * scale


def column_sum(value):
    return jnp.sum(value, axis=0, keepdims=True)


def layer_kernel(
    devices,
    sections,
    tokens,
    cotangent,
    crops_in,
    own_attn,
    own_up,
    own_down,
    own_vec_in,
    boundary_out,
    input_grads_out,
    sum_attn,
    sum_up,
    sum_down,
    sum_vec,
    norm,
    crops,
    own_vec,
    boundary,
    input_grads,
    w_attn,
    w_up,
    w_down,
    tiles,
    params,
    x_in,
    hidden,
    qkv,
    log_total,
    mixed,
    middle,
    hidden_two,
    slope,
    active,
    mask,
    dy_in,
    grad_up,
    grad_branch,
    grad_heads,
    grad_qkv,
    flow,
    flow_two,
    vec_sums,
    vec_tiles,
    g_down,
    other_down,
    other_up,
    other_attn,
    other_vec,
    slots_down,
    slots_up,
    slots_attn,
    slots_vec,
    norm_slots,
    local,
    gather_sems,
    gather_ways,
    relay_sems,
    reduce_sems,
    reduce_ways,
    across,
    norm_sem,
):
    section = lax.axis_index("section")
    first_section = section == 0
    last_section = section == 1
    ring = Ring(devices)
    me = ring.me
    micro_count, pack = tokens.shape[0], tokens.shape[1]
    width = tokens.shape[2]
    hidden_units = w_up.shape[1]
    tiles_up = hidden_units // width
    head_width = width // HEADS
    pairs = HEADS // 2
    unroll = 3
    pair_width = 2 * head_width
    head_scale = head_width ** (-0.5)
    vec_rows, vec_columns = own_vec.shape[0], own_vec.shape[2]

    def rows_of(micro):
        return pl.ds(pl.multiple_of(micro * pack, 16), pack)

    def lanes(start, count):
        return pl.ds(pl.multiple_of(start, 128), count)


    stage_attn = slope.at[pl.ds(0, own_attn.shape[1]), :]
    stage_up = slope.at[pl.ds(own_attn.shape[1], own_up.shape[1]), :]
    stage_down = middle.at[pl.ds(0, own_down.shape[1]), :]
    loads = [
        pltpu.make_async_copy(own_attn.at[0], stage_attn, local.at[0]),
        pltpu.make_async_copy(own_up.at[0], stage_up, local.at[1]),
        pltpu.make_async_copy(own_down.at[0], stage_down, local.at[2]),
        pltpu.make_async_copy(own_vec_in, own_vec, local.at[3]),
        pltpu.make_async_copy(crops_in, crops, local.at[4]),
    ]
    for load in loads:
        load.start()

    def load_tokens(micro):
        return pltpu.make_async_copy(tokens.at[micro], x_in.at[rows_of(micro), :], local.at[5 + micro])

    def load_cotangent(micro):
        return pltpu.make_async_copy(
            cotangent.at[micro], dy_in.at[rows_of(micro), :], local.at[5 + micro]
        )

    @pl.when(first_section)
    def _():
        for micro in range(micro_count):
            load_tokens(micro).start()

    @pl.when(last_section)
    def _():
        for micro in range(micro_count):
            load_cotangent(micro).start()

    barrier = pltpu.get_barrier_semaphore()
    neighbours = (ring.right(), ring.left(), ring.sibling(), (1 - section, me))
    for device in neighbours:
        pl.semaphore_signal(barrier, inc=1, device_id=device, device_id_type=MESH)

    vec_tiles[...] = jnp.zeros_like(vec_tiles)
    vec_sums[...] = jnp.zeros_like(vec_sums)
    for load in loads:
        load.wait()
    vec_tiles[0:vec_rows, 0:vec_columns] = own_vec[:, 0, :]
    tiles[pl.ds(pl.multiple_of(me * 16, 16), 16), :] = vec_tiles[0:16, :].astype(BF16)
    count = own_attn.shape[1]
    here = pl.ds(pl.multiple_of(me * count, 16), count)
    w_attn[here, :] = stage_attn[...].astype(BF16)
    count = own_up.shape[1]
    w_up[pl.ds(pl.multiple_of(me * count, 16), count), :] = stage_up[...].astype(BF16)
    count = own_down.shape[1]
    w_down[pl.ds(pl.multiple_of(me * count, 16), count), :] = stage_down[...].astype(BF16)

    pl.semaphore_wait(barrier, len(neighbours))


    def gather_of(index, shards, halves=True):
        return Gather(
            shards,
            halves,
            gather_sems.at[index, 0],
            gather_sems.at[index, 1],
            gather_ways.at[index],
        )

    attn_rows, up_rows, down_rows = own_attn.shape[1], own_up.shape[1], own_down.shape[1]
    reach = ring.reach
    get_vec = gather_of(0, Shards(ring, tiles, 16), False)
    get_attn = gather_of(1, Shards(ring, w_attn, attn_rows))

    lent_rows = up_rows
    kept_up = hidden_units - width
    kept_down = down_rows - lent_rows
    home = (
        Shards(ring, w_up, lent_rows, first=kept_up, columns=width),
        Shards(ring, w_down, lent_rows, down_rows, kept_down),
    )
    relay = Relay(
        Shards(ring, g_down, 2 * lent_rows),
        home,
        [Shards(ring, g_down, lent_rows, 2 * lent_rows, part * lent_rows) for part in range(2)],
        gather_sems.at[5, 0],
        gather_ways.at[5],
        relay_sems,
    )
    pieces = [Pieces(home[part], gather_sems.at[6, part], gather_sems.at[7, part]) for part in range(2)]

    def gathers_of(rows, columns):
        cut = (rows // 2 + 15) // 16 * 16
        up = gather_of(2, Shards(ring, w_up, up_rows, columns=columns))
        down = [
            gather_of(3, Shards(ring, w_down, cut, down_rows)),
            gather_of(4, Shards(ring, w_down, rows - cut, down_rows, cut)),
        ]
        return up, down

    first_up, first_down = gathers_of(kept_down, kept_up)
    last_up, last_down = gathers_of(down_rows, hidden_units)

    def each(gathers, call, *values):
        for gather in gathers:
            getattr(gather, call)(*values)

    get_vec.begin()
    get_attn.begin()

    @pl.when(first_section)
    def _():
        relay.lend()
        first_up.begin()
        for part in range(2):
            pieces[part].share(0)
        for step in range(1, reach + 1):
            get_vec.step(step)
            get_attn.step(step)
            if step < reach:
                first_up.step(step)
            if step == reach - 1:
                each(first_down, "begin")

    @pl.when(last_section)
    def _():
        relay.borrow()
        relay.begin()
        for step in range(1, reach + 1):
            get_vec.step(step)
            get_attn.step(step)
            if step == reach - 1:
                last_up.begin()
            relay.step(step)

    get_vec.finish()
    get_attn.finish()

    @pl.when(last_section)
    def _():
        last_up.step(1)
        each(last_down, "begin")
        for step in range(2, reach + 1):
            last_up.step(step)
            if step < reach:
                each(last_down, "step", step - 1)
        last_up.finish()

    def first_up_done():
        first_up.step(reach)
        relay.take(0)
        pieces[0].share_rest()
        first_up.finish()
        pieces[0].finish()

    def first_pieces():
        relay.take(1)
        pieces[1].share_rest()

    for device in range(devices):
        params[:, device * vec_columns : (device + 1) * vec_columns] = tiles[
            device * 16 : (device + 1) * 16, 0:vec_columns
        ].astype(F32)


    for micro in range(micro_count):
        row = crops[micro : micro + 1, :].astype(F32)
        square = jnp.broadcast_to(row, (pack, pack))
        mask[micro] = jnp.where(square == square.T, 1.0, 0.0)

    lane = lax.broadcasted_iota(jnp.int32, (1, pair_width), 1)
    in_low = lane < head_width

    def of_head(value, sub):
        return jnp.where(in_low if sub == 0 else ~in_low, value, jnp.zeros_like(value))

    def forward_micro(micro, serve):
        here = rows_of(micro)
        inputs = x_in[here, :].astype(F32)
        z, _ = norm_parts(inputs)
        hidden[here, :] = (z * params[0:1, :] + params[1:2, :]).astype(BF16)
        for part in range(3):
            value = dot_nn(hidden[here, :], w_attn[:, part * width : (part + 1) * width])
            if part == 0:
                value = value + params[2:3, :]
            if part == 2:
                value = value + params[3:4, :]
            qkv[here, part * width : (part + 1) * width] = value.astype(BF16)
        serve(0)

        def pair(index, _):
            at = index * pair_width
            queries = qkv[here, lanes(at, pair_width)]
            keys = qkv[here, lanes(width + at, pair_width)]
            values = qkv[here, lanes(2 * width + at, pair_width)]
            scores = [dot_nt(keys, of_head(queries, sub)) for sub in range(2)]
            outs = []
            for sub in range(2):
                value = jnp.where(mask[micro] > 0.5, scores[sub] * head_scale, NEG_BIG)
                peak = jnp.max(value, axis=0, keepdims=True)
                exponent = jnp.exp(value - peak)
                totals = jnp.sum(exponent, axis=0, keepdims=True)
                probs = (exponent * (1.0 / totals)).astype(BF16)
                log_total[pl.ds(micro * HEADS + 2 * index + sub, 1), :] = peak + jnp.log(totals)
                outs.append(dot_tn(probs, values))
            mixed[here, lanes(at, pair_width)] = jnp.where(in_low, outs[0], outs[1]).astype(BF16)
            return 0

        lax.fori_loop(0, pairs, pair, 0, unroll=unroll)
        serve(1)
        middle_value = x_in[here, :].astype(F32) + (
            dot_nn(mixed[here, :], w_attn[:, 3 * width :]) + params[4:5, :]
        )
        middle[here, :] = middle_value
        z, _ = norm_parts(middle_value)
        hidden_two[here, :] = (z * params[5:6, :] + params[6:7, :]).astype(BF16)
        serve(2)
        for part in range(tiles_up):
            columns = slice(part * width, (part + 1) * width)
            upward = dot_nn(hidden_two[here, :], w_up[:, columns]) + params[8 + part : 9 + part, :]
            area, density = gelu_parts(upward)
            active[here, columns] = (upward * area).astype(BF16)
            slope[here, columns] = area + upward * density
        serve(3)

    def hand_over(source, target, micro):
        here = rows_of(micro)
        return remote(
            source.at[micro],
            target.at[here, :],
            across.at[0, micro],
            across.at[1, micro],
            (1 - section, me),
        )

    def forward_step(micro, _):
        @pl.when(last_section)
        def _():
            hand_over(boundary, x_in, micro).wait_recv()

        @pl.when(first_section)
        def _():
            load_tokens(micro).wait()

        def serve(point):
            first_of, last_of = micro == 0, micro == micro_count - 1

            @pl.when(first_section & first_of)
            def _():
                if point == 0:
                    first_up_done()
                if point == 2:
                    for step in range(1, reach - 2):
                        each(first_down, "step", step)
                    first_pieces()

            @pl.when(first_section & last_of)
            def _():
                if point == 0:
                    each(first_down, "step", reach - 2)
                if point == 2:
                    each(first_down, "step", reach - 1)
                if point == 3:
                    each(first_down, "step", reach)

            @pl.when(last_section & first_of)
            def _():
                if point == 2:
                    each(last_down, "step", reach - 1)

            @pl.when(last_section & last_of)
            def _():
                if point == 0:
                    each(last_down, "step", reach)

        forward_micro(micro, serve)
        return 0

    lax.fori_loop(0, micro_count, forward_step, 0)

    @pl.when(first_section)
    def _():
        each(first_down, "finish")
        pieces[1].finish()

    @pl.when(last_section)
    def _():
        each(last_down, "finish")

    def finish_step(micro, _):
        here = rows_of(micro)
        output = middle[here, :] + (dot_nn(active[here, :], w_down[...]) + params[7:8, :])
        boundary[micro] = output.astype(BF16)

        @pl.when(first_section)
        def _():
            hand_over(boundary, x_in, micro).start()

        return 0

    lax.fori_loop(0, micro_count, finish_step, 0)
    each((get_vec, get_attn), "drain")

    @pl.when(first_section)
    def _():
        each((first_up, *first_down, *pieces), "drain")
        relay.drain_lent()

    @pl.when(last_section)
    def _():
        each((last_up, *last_down, relay), "drain")

    pltpu.make_async_copy(boundary, boundary_out, local.at[0]).start()


    def into(ref, first=0, row=0):
        def put(start, value):
            rows = pl.ds(pl.multiple_of(row + start, 8), value.shape[0])
            ref[rows, pl.ds(first, value.shape[1])] = value

        return put

    def reduce_of(index, shards, put, other, slots, halves=True, block=16):
        return Reduce(
            shards,
            put,
            other,
            slots,
            halves,
            block,
            reduce_sems.at[index, 0],
            reduce_sems.at[index, pl.ds(1, 2)],
            reduce_ways.at[index],
        )

    half_down = down_rows // 2
    put_down = [
        reduce_of(
            part,
            Shards(ring, g_down, half_down, down_rows, part * half_down),
            into(sum_down, row=part * half_down),
            other_down.at[part],
            slots_down.at[part],
            block=half_down // 2,
        )
        for part in range(2)
    ]
    half_up, half_attn = hidden_units // 2, w_attn.shape[1] // 2
    put_up = [
        reduce_of(
            2 + part,
            Shards(ring, w_up, up_rows, first=part * half_up, columns=half_up),
            into(sum_up, part * half_up),
            other_up.at[part],
            slots_up.at[part],
        )
        for part in range(2)
    ]
    put_attn = [
        reduce_of(
            4 + part,
            Shards(ring, w_attn, attn_rows, first=part * half_attn, columns=half_attn),
            into(sum_attn, part * half_attn),
            other_attn.at[part],
            slots_attn.at[part],
        )
        for part in range(2)
    ]
    put_vec = reduce_of(
        6, Shards(ring, vec_tiles, 16), into(sum_vec), other_vec, slots_vec, False
    )

    chunk = 2 * down_rows

    def weigh_down(distance):
        start = ring.device(ring.place + distance, 0) * down_rows
        columns = lanes(start, chunk)
        g_down[pl.ds(pl.multiple_of(start, 16), chunk), :] = dot_tn(
            active[:, columns], dy_in[...]
        ).astype(BF16)
        each(put_down, "swap", distance)

    def start_down():
        for index, (distance, _) in enumerate(put_down[0].keys()):
            weigh_down(distance)
            if index == 1:
                each(put_down, "first")
        each(put_down, "step", reach - 1)

    def add_vec(row, value):
        vec_sums[row : row + 1, :] += value

    def backward_micro(micro, serve):
        here = rows_of(micro)
        add_vec(7, column_sum(dy_in[here, :].astype(F32)))
        for part in range(tiles_up):
            columns = slice(part * width, (part + 1) * width)
            back = dot_nt(dy_in[here, :], w_down[columns, :]) * slope[here, columns]
            back = back.astype(BF16)
            grad_up[here, columns] = back
            add_vec(8 + part, column_sum(back.astype(F32)))
            more = dot_nt(back, w_up[:, columns])
            if part == 0:
                flow[...] = more
            else:
                flow[...] += more
        serve(0)
        e = flow[...]
        z, scale = norm_parts(middle[here, :])
        add_vec(5, column_sum(e * z))
        add_vec(6, column_sum(e))
        back = dy_in[here, :].astype(F32) + norm_back(z, scale, e, params[5:6, :])
        flow_two[...] = back
        back = back.astype(BF16)
        grad_branch[here, :] = back
        add_vec(4, column_sum(back.astype(F32)))
        grad_heads[...] = dot_nt(back, w_attn[:, 3 * width :]).astype(BF16)
        serve(1)

        def pair(index, _):
            at = index * pair_width
            queries = qkv[here, lanes(at, pair_width)]
            keys = qkv[here, lanes(width + at, pair_width)]
            values = qkv[here, lanes(2 * width + at, pair_width)]
            back_out = grad_heads[:, lanes(at, pair_width)]
            scores = [dot_nt(keys, of_head(queries, sub)) for sub in range(2)]
            back_probs = [dot_nt(values, of_head(back_out, sub)) for sub in range(2)]
            results = []
            for sub in range(2):
                value = jnp.where(mask[micro] > 0.5, scores[sub] * head_scale, NEG_BIG)
                probs = jnp.exp(
                    value - log_total[pl.ds(micro * HEADS + 2 * index + sub, 1), :]
                )
                inner = jnp.sum(back_probs[sub] * probs, axis=0, keepdims=True)
                back_scores = (probs * (back_probs[sub] - inner)).astype(BF16)
                results.append(
                    (
                        dot_tn(back_scores, keys) * head_scale,
                        dot_nn(back_scores, queries) * head_scale,
                        dot_nn(probs.astype(BF16), back_out),
                    )
                )
            for part in range(3):
                grad_qkv[here, lanes(part * width + at, pair_width)] = jnp.where(
                    in_low, results[0][part], results[1][part]
                ).astype(BF16)
            return 0

        lax.fori_loop(0, pairs, pair, 0, unroll=unroll)
        serve(2)
        e = dot_nt(grad_qkv[here, :], w_attn[:, : 3 * width])
        z, scale = norm_parts(x_in[here, :].astype(F32))
        add_vec(0, column_sum(e * z))
        add_vec(1, column_sum(e))
        add_vec(2, column_sum(grad_qkv[here, 0:width].astype(F32)))
        add_vec(3, column_sum(grad_qkv[here, 2 * width : 3 * width].astype(F32)))
        back = flow_two[...] + norm_back(z, scale, e, params[0:1, :])
        input_grads[micro] = back.astype(BF16)
        serve(3)

    def backward_step(micro, _):
        @pl.when(first_section)
        def _():
            hand_over(input_grads, dy_in, micro).wait_recv()

        @pl.when(last_section)
        def _():
            load_cotangent(micro).wait()

        is_last = micro == micro_count - 1

        def serve(point):
            @pl.when(first_section & is_last)
            def _():
                if point == 1:
                    each(put_down, "step", reach - 2)
                if point == 3:
                    for distance in range(reach - 3, 0, -1):
                        each(put_down, "step", distance)

        @pl.when(first_section & is_last)
        def _():
            start_down()

        backward_micro(micro, serve)

        @pl.when(last_section)
        def _():
            hand_over(input_grads, dy_in, micro).start()

        return 0

    lax.fori_loop(0, micro_count, backward_step, 0)

    copy_input_grads = pltpu.make_async_copy(input_grads, input_grads_out, local.at[1])
    copy_input_grads.start()

    @pl.when(last_section)
    def _():
        start_down()

    def squares(ref):
        value = ref[...]
        value = value * value
        while value.shape[1] > 128:
            value = sum(
                value[:, start : start + 128] for start in range(0, value.shape[1], 128)
            )
        return sum(value[start : start + 8, :] for start in range(0, value.shape[0], 8))

    third = width // 3

    def weigh(source, grad, target, first):
        def body(index, _):
            target[
                pl.ds(pl.multiple_of(index * third, 16), third),
                pl.ds(first, grad.shape[1]),
            ] = dot_tn(source[:, lanes(index * third, third)], grad[...]).astype(BF16)
            return 0

        lax.fori_loop(0, 3, body, 0)

    weigh(hidden_two, grad_up, w_up, 0)
    each(put_up, "exchange")

    @pl.when(last_section)
    def _():
        each(put_down, "step", reach - 2)

    each(put_up, "first")
    vec_tiles[...] = jnp.zeros_like(vec_tiles)
    for device in range(devices):
        vec_tiles[device * 16 : (device + 1) * 16, 0:vec_columns] = vec_sums[
            :, device * vec_columns : (device + 1) * vec_columns
        ]
    put_vec.exchange()
    weigh(hidden, grad_qkv, w_attn, 0)
    put_attn[0].exchange()
    weigh(mixed, grad_branch, w_attn, 3 * width)
    put_attn[1].exchange()

    @pl.when(last_section)
    def _():
        for distance in range(reach - 3, 0, -1):
            each(put_down, "step", distance)

    put_vec.first()
    each(put_up, "step", reach - 1)
    each(put_down, "last")
    each(put_attn, "first")
    put_vec.step(reach - 1)
    each(put_up, "step", reach - 2)
    each(put_attn, "step", reach - 1)
    for distance in range(reach - 2, 0, -1):
        put_vec.step(distance)
        if distance > 1:
            each(put_up, "step", distance - 1)
        else:
            each(put_up, "last")
        each(put_attn, "step", distance)
    put_vec.last()
    norm_slots[0] = squares(sum_up) + squares(sum_down) + squares(sum_vec)
    each(put_attn, "last")


    total_devices = sections * devices
    flat = section * devices + me

    def other_device(distance):
        other = (flat + distance) % total_devices
        return (other // devices, other % devices)

    norm_slots[0] += squares(sum_attn)

    def tell(distance, _):
        remote(
            norm_slots.at[0],
            norm_slots.at[distance],
            norm_sem.at[0],
            norm_sem.at[1],
            other_device(distance),
        ).start()
        return 0

    lax.fori_loop(1, total_devices, tell, 0)
    rest = norm_slots.at[pl.ds(1, total_devices - 1)]
    heard = remote(rest, rest, norm_sem.at[0], norm_sem.at[1], other_device(1))
    heard.wait_recv()

    def collect(device, order):
        return order + norm_slots[(flat - device + total_devices) % total_devices]

    order = lax.fori_loop(0, total_devices, collect, jnp.zeros(norm_slots.shape[1:], F32))
    total = jnp.sum(jnp.sum(order, axis=0, keepdims=True), axis=1, keepdims=True)
    norm[0, 0] = jnp.sqrt(total)[0, 0]
    heard.wait_send()


    each((*put_down, *put_up, *put_attn, put_vec), "drain")
    pltpu.make_async_copy(boundary, boundary_out, local.at[0]).wait()
    copy_input_grads.wait()
    for micro in range(micro_count):

        @pl.when(first_section)
        def _():
            hand_over(boundary, x_in, micro).wait_send()

        @pl.when(last_section)
        def _():
            hand_over(input_grads, dy_in, micro).wait_send()


def run_layers(devices, sections, tokens, cotangent, crop_ids, attn, upward_w, downward_w, vectors):
    micro_count, pack, width = tokens.shape
    rows = micro_count * pack
    chips, reach = devices // 2, devices // 4
    hidden_units = upward_w.shape[2]
    attn_rows, up_rows, down_rows = attn.shape[1], upward_w.shape[1], downward_w.shape[1]
    in_hbm = pl.BlockSpec(memory_space=pl.ANY)
    in_vmem = pl.BlockSpec(memory_space=pltpu.VMEM)

    def other(rows_of_shard, columns, kind=BF16):
        return pltpu.VMEM((chips, rows_of_shard, columns), kind)

    def slots(rows_of_shard, columns, kind=BF16):
        return pltpu.VMEM((2, reach, rows_of_shard, columns), kind)

    scratch = [
        pltpu.VMEM(crop_ids.shape, jnp.int32),
        pltpu.VMEM(vectors.shape, F32),
        pltpu.VMEM(tokens.shape, BF16),
        pltpu.VMEM(tokens.shape, BF16),
        pltpu.VMEM((width, attn.shape[2]), BF16),
        pltpu.VMEM((width, hidden_units), BF16),
        pltpu.VMEM((hidden_units, width), BF16),
        pltpu.VMEM((devices * 16, 128), BF16),
        pltpu.VMEM((16, width), F32),
        pltpu.VMEM((rows, width), BF16),
        pltpu.VMEM((rows, width), BF16),
        pltpu.VMEM((rows, 3 * width), BF16),
        pltpu.VMEM((micro_count * HEADS, pack), F32),
        pltpu.VMEM((rows, width), BF16),
        pltpu.VMEM((rows, width), F32),
        pltpu.VMEM((rows, width), BF16),
        pltpu.VMEM((rows, hidden_units), F32),
        pltpu.VMEM((rows, hidden_units), BF16),
        pltpu.VMEM((micro_count, pack, pack), F32),
        pltpu.VMEM((rows, width), BF16),
        pltpu.VMEM((rows, hidden_units), BF16),
        pltpu.VMEM((rows, width), BF16),
        pltpu.VMEM((pack, width), BF16),
        pltpu.VMEM((rows, 3 * width), BF16),
        pltpu.VMEM((pack, width), F32),
        pltpu.VMEM((pack, width), F32),
        pltpu.VMEM((16, width), F32),
        pltpu.VMEM((devices * 16, 128), F32),
        pltpu.VMEM((hidden_units, width), BF16),
        pltpu.VMEM((2, chips, down_rows // 2, width), BF16),
        pltpu.VMEM((2, chips, up_rows, hidden_units // 2), BF16),
        pltpu.VMEM((2, chips, attn_rows, attn.shape[2] // 2), BF16),
        other(16, 128, F32),
        pltpu.VMEM((2, 2, reach, down_rows // 2, width), BF16),
        pltpu.VMEM((2, 2, reach, up_rows, hidden_units // 2), BF16),
        pltpu.VMEM((2, 2, reach, attn_rows, attn.shape[2] // 2), BF16),
        slots(16, 128, F32),
        pltpu.VMEM((sections * devices, 8, 128), F32),
        pltpu.SemaphoreType.DMA((5 + micro_count,)),
        pltpu.SemaphoreType.DMA((8, 2)),
        pltpu.SemaphoreType.DMA((6, 2, reach)),
        pltpu.SemaphoreType.DMA((3,)),
        pltpu.SemaphoreType.DMA((7, 3)),
        pltpu.SemaphoreType.DMA((7, 2, reach)),
        pltpu.SemaphoreType.DMA((2, micro_count)),
        pltpu.SemaphoreType.DMA((2,)),
    ]
    return pl.pallas_call(
        partial(layer_kernel, devices, sections),
        out_shape=[
            jax.ShapeDtypeStruct(tokens.shape, BF16),
            jax.ShapeDtypeStruct(tokens.shape, BF16),
            jax.ShapeDtypeStruct(attn.shape[1:], F32),
            jax.ShapeDtypeStruct(upward_w.shape[1:], F32),
            jax.ShapeDtypeStruct(downward_w.shape[1:], F32),
            jax.ShapeDtypeStruct((16, 128), F32),
            jax.ShapeDtypeStruct((1, 1), F32),
        ],
        in_specs=[in_hbm] * 7,
        out_specs=[in_hbm] * 2 + [in_vmem] * 4 + [pl.BlockSpec(memory_space=pltpu.SMEM)],
        scratch_shapes=scratch,
        compiler_params=pltpu.CompilerParams(
            collective_id=0, has_side_effects=True, vmem_limit_bytes=VMEM_LIMIT
        ),
        name="two_layers",
    )(tokens, cotangent, crop_ids, attn, upward_w, downward_w, vectors)


def adam_kernel(boundary, input_grads, norm, *refs):
    grads, states, out_boundary, out_input, out_norm = refs[:4], refs[4:16], *refs[16:19]
    results, held, passing = refs[19:31], refs[31], refs[32]
    step = pl.program_id(0)
    take = [
        pltpu.make_async_copy(source, held.at[i], passing.at[i])
        for i, source in enumerate((boundary, input_grads))
    ]
    hand_on = [
        pltpu.make_async_copy(held.at[i], target, passing.at[i])
        for i, target in enumerate((out_boundary, out_input))
    ]

    @pl.when(step == 0)
    def _():
        for copy in take:
            copy.start()
        out_norm[0, 0] = norm[0, 0]

    @pl.when(step == 1)
    def _():
        for first, second in zip(take, hand_on):
            first.wait()
            second.start()

    clip_factor = jnp.minimum(1.0, MAX_NORM / (jnp.full((1, 1), norm[0, 0]) + 1e-06))
    for index in range(4):
        master, moment_one, moment_two = (states[index + 4 * part] for part in range(3))
        vectors = index == 3
        shape = (master.shape[0], master.shape[2]) if vectors else master.shape[1:]
        gradient = grads[index][0 : shape[0], 0 : shape[1]] * clip_factor
        old = [ref[:, 0, :] if vectors else ref[0] for ref in (master, moment_one, moment_two)]
        decay, rate = (0.0, VECTOR_RATE) if vectors else (DECAY_RATE, RATE)
        updated = adam_update(old[0], gradient, old[1], old[2], decay, rate)
        for part in range(3):
            if vectors:
                results[index + 4 * part][:, 0, :] = updated[part]
            else:
                results[index + 4 * part][0] = updated[part]

    @pl.when(step == pl.num_programs(0) - 1)
    def _():
        for copy in hand_on:
            copy.wait()


def run_adam(boundary, input_grads, attn, upward_w, downward_w, vectors, norm, states):
    grads = (attn, upward_w, downward_w, vectors)
    steps = 2

    def cut(shape):
        block = shape[:-2] + (shape[-2] // steps, shape[-1])
        lead = (0,) * (len(shape) - 2)
        return pl.BlockSpec(block, lambda i: lead + (i, 0))

    def keep(shape):
        lead = (0,) * len(shape)
        return pl.BlockSpec(shape, lambda i: lead)

    def spec(index, array):
        return keep(array.shape) if index % 4 == 3 else cut(array.shape)

    in_hbm = pl.BlockSpec(memory_space=pl.ANY)
    scalar = pl.BlockSpec(memory_space=pltpu.SMEM)
    state_specs = [spec(i, a) for i, a in enumerate(states)]
    return pl.pallas_call(
        adam_kernel,
        grid=(steps,),
        out_shape=[
            jax.ShapeDtypeStruct(boundary.shape, BF16),
            jax.ShapeDtypeStruct(input_grads.shape, BF16),
            jax.ShapeDtypeStruct((1, 1), F32),
        ]
        + [jax.ShapeDtypeStruct(a.shape, F32) for a in states],
        in_specs=[in_hbm, in_hbm, scalar] + [spec(i, a) for i, a in enumerate(grads)] + state_specs,
        out_specs=[in_hbm, in_hbm, scalar] + state_specs,
        scratch_shapes=[pltpu.VMEM((2,) + boundary.shape, BF16), pltpu.SemaphoreType.DMA((2,))],
        compiler_params=pltpu.CompilerParams(vmem_limit_bytes=VMEM_LIMIT),
        name="adam",
    )(boundary, input_grads, norm, *grads, *states)


def layer_norm(features, gain_row, shift_row):
    center = jnp.mean(features, axis=-1, keepdims=True)
    centered = features - center
    spread = jnp.mean(centered * centered, axis=-1, keepdims=True)
    return centered * lax.rsqrt(spread + LN_EPS) * gain_row + shift_row


def split_heads(packed, micro_count, model_width):
    shaped = packed.reshape(micro_count, -1, 3, HEADS, model_width // HEADS)
    return (shaped[:, :, 0], shaped[:, :, 1], shaped[:, :, 2])


def attention_scores(queries, keys_block, crop_rows):
    head_scale = queries.shape[-1] ** (-0.5)
    scores = (
        jnp.einsum("mqhd,mkhd->mhqk", queries, keys_block, preferred_element_type=F32) * head_scale
    )
    same_crop = crop_rows[:, :, None] == crop_rows[:, None, :]
    return jnp.where(same_crop[:, None], scores, NEG_BIG)


def forward_layer(inputs, crop_rows, weights):
    attn, upward_w, downward_w, vectors_b = weights
    model_width = attn.shape[0]
    rows = inputs.shape[0]
    params = vectors_b.astype(F32)
    hidden = layer_norm(inputs, params[0], params[1]).astype(BF16)
    qkv_bias = jnp.concatenate([params[2], jnp.zeros_like(params[2]), params[3]])
    packed = (
        jnp.dot(hidden, attn[:, : 3 * model_width], preferred_element_type=F32) + qkv_bias
    ).astype(BF16)
    queries, keys_block, values_block = split_heads(packed, crop_rows.shape[0], model_width)
    scores = attention_scores(queries, keys_block, crop_rows)
    row_peak = jnp.max(scores, axis=-1, keepdims=True)
    exponent = jnp.exp(scores - row_peak)
    totals = jnp.sum(exponent, axis=-1, keepdims=True)
    soft_weights = (exponent / totals).astype(BF16)
    log_total = row_peak + jnp.log(totals)
    mixed = jnp.einsum("mhqk,mkhd->mqhd", soft_weights, values_block, preferred_element_type=F32)
    mixed = mixed.reshape(rows, model_width).astype(BF16)
    middle = inputs + (
        jnp.dot(mixed, attn[:, 3 * model_width :], preferred_element_type=F32) + params[4]
    )
    hidden_two = layer_norm(middle, params[5], params[6]).astype(BF16)
    upward = jnp.dot(hidden_two, upward_w, preferred_element_type=F32) + params[8:].reshape(-1)
    active = jax.nn.gelu(upward, approximate=False).astype(BF16)
    output = middle + (jnp.dot(active, downward_w, preferred_element_type=F32) + params[7])
    return (output, (inputs, hidden, packed, log_total, mixed, middle, hidden_two, upward, active))


def backward_layer(kept, crop_rows, grad_out, weights, with_grads):
    attn, upward_w, downward_w, vectors_b = weights
    inputs, hidden, packed, log_total, mixed, middle, hidden_two, upward, active = kept
    model_width = attn.shape[0]
    rows = inputs.shape[0]
    params = vectors_b.astype(F32)
    grad_down = grad_out.astype(BF16)
    grad_active = jnp.einsum("pj,ij->pi", grad_down, downward_w, preferred_element_type=F32)
    gelu_back = jax.vjp(partial(jax.nn.gelu, approximate=False), upward)[1]
    grad_up = gelu_back(grad_active)[0].astype(BF16)
    grad_hidden_two = jnp.einsum("pj,ij->pi", grad_up, upward_w, preferred_element_type=F32)
    norm_back_two = jax.vjp(layer_norm, middle, params[5], params[6])[1]
    grad_middle_part, grad_gain_two, grad_shift_two = norm_back_two(grad_hidden_two)
    grad_middle = grad_out + grad_middle_part
    grad_branch = grad_middle.astype(BF16)
    grad_mixed = jnp.einsum(
        "pj,ij->pi", grad_branch, attn[:, 3 * model_width :], preferred_element_type=F32
    ).astype(BF16)
    micro_count = crop_rows.shape[0]
    queries, keys_block, values_block = split_heads(packed, micro_count, model_width)
    scores = attention_scores(queries, keys_block, crop_rows)
    probs = jnp.exp(scores - log_total)
    grad_heads = grad_mixed.reshape(micro_count, -1, HEADS, model_width // HEADS)
    grad_probs = jnp.einsum("mqhd,mkhd->mhqk", grad_heads, values_block, preferred_element_type=F32)
    grad_values = jnp.einsum(
        "mhqk,mqhd->mkhd", probs.astype(BF16), grad_heads, preferred_element_type=F32
    )
    grad_scores = (
        probs * (grad_probs - jnp.sum(grad_probs * probs, axis=-1, keepdims=True))
    ).astype(BF16)
    head_scale = queries.shape[-1] ** (-0.5)
    grad_queries = (
        jnp.einsum("mhqk,mkhd->mqhd", grad_scores, keys_block, preferred_element_type=F32)
        * head_scale
    )
    grad_keys = (
        jnp.einsum("mhqk,mqhd->mkhd", grad_scores, queries, preferred_element_type=F32) * head_scale
    )
    grad_packed = jnp.concatenate(
        [
            grad_queries.reshape(rows, model_width),
            grad_keys.reshape(rows, model_width),
            grad_values.reshape(rows, model_width),
        ],
        axis=1,
    ).astype(BF16)
    grad_hidden = jnp.einsum(
        "pj,ij->pi", grad_packed, attn[:, : 3 * model_width], preferred_element_type=F32
    )
    norm_back_one = jax.vjp(layer_norm, inputs, params[0], params[1])[1]
    grad_in_part, grad_gain_one, grad_shift_one = norm_back_one(grad_hidden)
    grad_inputs = grad_middle + grad_in_part
    if not with_grads:
        return (grad_inputs, None)
    grad_w_down = jnp.einsum("pi,pj->ij", active, grad_down, preferred_element_type=F32)
    grad_w_up = jnp.einsum("pi,pj->ij", hidden_two, grad_up, preferred_element_type=F32)
    grad_w_out = jnp.einsum("pi,pj->ij", mixed, grad_branch, preferred_element_type=F32)
    grad_w_qkv = jnp.einsum("pi,pj->ij", hidden, grad_packed, preferred_element_type=F32)
    packed_sums = jnp.sum(grad_packed, axis=0, dtype=F32)
    vector_rows = jnp.stack(
        [
            grad_gain_one,
            grad_shift_one,
            packed_sums[:model_width],
            packed_sums[2 * model_width :],
            jnp.sum(grad_branch, axis=0, dtype=F32),
            grad_gain_two,
            grad_shift_two,
            jnp.sum(grad_down, axis=0, dtype=F32),
        ]
    )
    up_bias_rows = jnp.sum(grad_up, axis=0, dtype=F32).reshape(-1, model_width)
    grad_vectors = jnp.concatenate([vector_rows, up_bias_rows], axis=0)
    grad_attn = jnp.concatenate([grad_w_qkv, grad_w_out], axis=1)
    return (grad_inputs, (grad_attn, grad_w_up, grad_w_down, grad_vectors))


def adam_update(master, gradient, moment_one, moment_two, decay_rate, step_rate):
    new_one = BETA_ONE * moment_one + (1.0 - BETA_ONE) * gradient
    new_two = BETA_TWO * moment_two + (1.0 - BETA_TWO) * gradient * gradient
    ratio = (
        new_one / (1.0 - BETA_ONE**STEP) / (jnp.sqrt(new_two / (1.0 - BETA_TWO**STEP)) + ADAM_EPS)
    )
    return (master - step_rate * (ratio + decay_rate * master), new_one, new_two)


def shards_by_kernels(devices, sections, tokens, cotangent, crop_ids, *states):
    states = [state.transpose(1, 0, 2) if i % 4 == 3 else state for i, state in enumerate(states)]
    sums = run_layers(devices, sections, tokens, cotangent, crop_ids, *states[:4])
    boundary, input_grads, grad_norm, *updated = run_adam(*sums, states)
    updated = [state.transpose(1, 0, 2) if i % 4 == 3 else state for i, state in enumerate(updated)]
    return (boundary[None], input_grads[None], grad_norm.reshape(())) + tuple(updated)


def shards_by_collectives(devices, sections, tokens, cotangent, crop_ids, *states):
    section_index = lax.axis_index("section")
    flat = (-1, tokens.shape[2])
    masters, firsts, seconds = states[:4], states[4:8], states[8:]
    shards = [master[0].astype(BF16) for master in masters]
    weights = tuple(
        lax.all_gather(shard, "dp", axis=axis, tiled=True) for shard, axis in zip(shards, (0, 0, 0, 1))
    )
    own_tokens = tokens.reshape(flat)
    first_output, _ = forward_layer(own_tokens.astype(F32), crop_ids, weights)
    received = lax.ppermute(first_output.astype(BF16), "section", [(0, 1)])
    layer_input = jnp.where(section_index == 0, own_tokens, received)
    output, kept = forward_layer(layer_input.astype(F32), crop_ids, weights)
    boundary = output.astype(BF16).reshape(tokens.shape)
    own_grad = cotangent.reshape(flat)
    first_back, _ = backward_layer(kept, crop_ids, own_grad.astype(F32), weights, False)
    back_received = lax.ppermute(first_back.astype(BF16), "section", [(1, 0)])
    grad_out = jnp.where(section_index == 1, own_grad, back_received).astype(F32)
    grad_inputs, gradients = backward_layer(kept, crop_ids, grad_out, weights, True)
    input_grads = grad_inputs.astype(BF16).reshape(tokens.shape)
    reduced = tuple(
        lax.psum_scatter(gradient, "dp", scatter_dimension=axis, tiled=True)
        for gradient, axis in zip(gradients, (0, 0, 0, 1))
    )
    squares = sum(jnp.sum(member * member) for member in reduced)
    grad_norm = jnp.sqrt(lax.psum(squares, ("section", "dp")))
    clip_factor = jnp.minimum(1.0, MAX_NORM / (grad_norm + 1e-06))
    decays = (DECAY_RATE, DECAY_RATE, DECAY_RATE, 0.0)
    rates = (RATE, RATE, RATE, VECTOR_RATE)
    updated = [
        adam_update(master[0], gradient * clip_factor, one[0], two[0], decay_rate, step_rate)
        for master, gradient, one, two, decay_rate, step_rate in zip(
            masters, reduced, firsts, seconds, decays, rates
        )
    ]
    new_states = tuple(entry[part][None] for part in range(3) for entry in updated)
    return (boundary[None], input_grads[None], grad_norm) + new_states


def shards(devices, sections, tokens, cotangent, crop_ids, *states):
    whole_tiles = (
        devices % 8 == 0
        and all(state.shape[1] % 16 == 0 for state in states[:3])
        and states[2].shape[1] % 64 == 0
        and states[3].shape[1] <= 16
        and states[3].shape[2] <= 128
    )
    run = shards_by_kernels if whole_tiles else shards_by_collectives
    return run(devices, sections, tokens, cotangent, crop_ids, *states)


def solution(mesh):
    token_spec = P(None, "dp", None)
    row_spec = P("section", "dp", None)
    column_spec = P("section", None, "dp")
    state = (row_spec, row_spec, row_spec, column_spec)
    micro_spec = P("section", None, "dp", None)
    return jax.shard_map(
        partial(shards, mesh.shape["dp"], mesh.shape["section"]),
        mesh=mesh,
        in_specs=(token_spec, token_spec, P(None, "dp")) + 3 * state,
        out_specs=(micro_spec, micro_spec, P()) + 3 * state,
        check_vma=False,
    )
```

```python
from functools import partial

import jax
import jax.numpy as jnp
from jax import lax
from jax.experimental import pallas as pl
from jax.experimental.pallas import tpu as pltpu
from jax.sharding import PartitionSpec as P

HEADS = 12
STEP = 10
LN_EPS = 1e-06
NEG_BIG = -1e30
BETA_ONE = 0.9
BETA_TWO = 0.999
RATE = 0.1
VECTOR_RATE = 0.5
DECAY_RATE = 0.01
ADAM_EPS = 1e-08
MAX_NORM = 1.0
MESH = pl.DeviceIdType.MESH
VMEM_LIMIT = 61 * 2**20
F32 = jnp.float32
BF16 = jnp.bfloat16


class Ring:
    def __init__(self, devices):
        self.devices = devices
        self.chips = devices // 2
        self.reach = self.chips // 2
        self.me = lax.axis_index("dp")
        self.core = self.me % 2
        chip = self.me // 2
        row, column = chip // 2, chip % 2
        self.place = row * (1 - column) + (self.chips - 1 - row) * column

    def device(self, place, core):
        place = (place + 2 * self.chips) % self.chips
        column = place // self.reach
        row = place * (1 - column) + (self.chips - 1 - place) * column
        return (row * 2 + column) * 2 + core

    def target(self, device):
        return (lax.axis_index("section"), device)

    def right(self):
        return self.target(self.device(self.place + 1, self.core))

    def left(self):
        return self.target(self.device(self.place - 1, self.core))

    def sibling(self):
        return self.target(self.device(self.place, 1 - self.core))


def remote(source, target, send, receive, device):
    return pltpu.make_async_remote_copy(
        src_ref=source,
        dst_ref=target,
        send_sem=send,
        recv_sem=receive,
        device_id=device,
        device_id_type=MESH,
    )


class Shards:
    def __init__(self, ring, whole, rows, stride=None, base=0, first=0, columns=None):
        self.ring, self.whole, self.rows = ring, whole, rows
        self.stride = rows if stride is None else stride
        self.base, self.first = base, first
        self.columns = whole.shape[1] if columns is None else columns

    def row(self, distance, core):
        device = self.ring.device(self.ring.place + distance, core)
        return pl.multiple_of(device * self.stride + self.base, 16)

    def view(self, distance, core, part=None):
        rows = pl.ds(self.row(distance, core), self.rows)
        if part is None:
            return self.whole.at[rows, pl.ds(self.first, self.columns)]
        columns = self.columns // 2
        return self.whole.at[rows, pl.ds(self.first + part * columns, columns)]

    def of_bytes(self, count):
        return self.whole.at[pl.ds(0, count * self.rows), pl.ds(self.first, self.columns)]


class Gather:
    def __init__(self, shards, halves, sent, shared, arrived):
        self.ring, self.shards, self.halves = shards.ring, shards, halves
        self.sent, self.shared, self.arrived = sent, shared, arrived

    def hop(self, way, step, came):
        ring = self.ring
        direction = 1 if way == 0 else -1
        part = None
        if step == ring.reach:
            if self.halves:
                part = way
            elif way == 1:
                return None
        view = self.shards.view(-direction * (step if came else step - 1), ring.core, part)
        device = ring.right() if way == 0 else ring.left()
        return remote(view, view, self.sent, self.arrived.at[way, step - 1], device)

    def push(self, way, step):
        copy = self.hop(way, step, False)
        if copy is not None:
            copy.start()

    def arrive(self, way, step):
        copy = self.hop(way, step, True)
        if copy is not None:
            copy.wait_recv()

    def share(self, distance):
        view = self.shards.view(distance, self.ring.core)
        remote(view, view, self.sent, self.shared, self.ring.sibling()).start()

    def begin(self):
        self.push(0, 1)
        self.push(1, 1)
        self.share(0)

    def step(self, step):
        reach = self.ring.reach
        self.arrive(0, step)
        if step < reach:
            self.push(0, step + 1)
        self.arrive(1, step)
        if step < reach:
            self.push(1, step + 1)
            self.share(-step)
            self.share(step)
        else:
            self.share(reach)

    def bytes_of(self, count):
        view = self.shards.of_bytes(count)
        return remote(view, view, self.sent, self.shared, self.ring.sibling())

    def finish(self):
        self.bytes_of(self.ring.chips).wait_recv()

    def drain(self):
        self.bytes_of(2 * self.ring.chips - 1).wait_send()


class Relay(Gather):
    def __init__(self, shards, home, away, sent, arrived, crossed):
        super().__init__(shards, True, sent, None, arrived)
        self.home, self.away, self.crossed = home, away, crossed

    def across(self, source, target, semaphore):
        section = lax.axis_index("section")
        return remote(source, target, self.sent, semaphore, (1 - section, self.ring.me))

    def lend(self):
        core = self.ring.core
        for home, away in zip(self.home, self.away):
            self.across(home.view(0, core), away.view(0, core), self.crossed.at[0]).start()

    def borrow(self):
        view = self.shards.view(0, self.ring.core)
        self.across(view, view, self.crossed.at[0]).wait_recv()

    def share(self, distance):
        if distance == 0:
            return
        core = self.ring.core
        for index, (home, away) in enumerate(zip(self.home, self.away)):
            self.across(
                away.view(distance, core), home.view(distance, core), self.crossed.at[1 + index]
            ).start()

    def take(self, index):
        view = self.home[index].of_bytes(self.ring.chips - 1)
        self.across(view, view, self.crossed.at[1 + index]).wait_recv()

    def drain(self):
        view = self.shards.of_bytes(2 * self.ring.chips - 2)
        self.across(view, view, self.crossed.at[0]).wait_send()

    def drain_lent(self):
        view = self.shards.of_bytes(1)
        self.across(view, view, self.crossed.at[0]).wait_send()


class Pieces(Gather):
    def __init__(self, shards, sent, shared):
        super().__init__(shards, True, sent, shared, None)

    def share_rest(self):
        for distance in range(1 - self.ring.reach, self.ring.reach + 1):
            if distance != 0:
                self.share(distance)

    def drain(self):
        self.bytes_of(self.ring.chips).wait_send()


class Reduce:
    def __init__(self, shards, put, other, slots, halves, block, sent, swapped, arrived):
        self.ring, self.shards, self.put = shards.ring, shards, put
        self.other, self.slots, self.halves, self.block = other, slots, halves, block
        self.sent, self.swapped, self.arrived = sent, swapped, arrived

    def keys(self):
        reach = self.ring.reach
        order = [(reach, 0)]
        for distance in range(reach - 1, 0, -1):
            order += [(distance, 2 * (reach - distance) - 1), (-distance, 2 * (reach - distance))]
        return order + [(0, 2 * reach - 1)]

    def key(self, distance):
        return dict(self.keys())[distance]

    def swap(self, distance):
        key = self.key(distance)
        remote(
            self.shards.view(distance, 1 - self.ring.core),
            self.other.at[key],
            self.sent,
            self.swapped.at[min(key, 1)],
            self.ring.sibling(),
        ).start()

    def exchange(self):
        for distance, _ in self.keys():
            self.swap(distance)

    def exchanged(self, first):
        slots = self.other.at[pl.ds(0, 1)] if first else self.other.at[pl.ds(1, self.ring.chips - 1)]
        semaphore = self.swapped.at[0 if first else 1]
        remote(slots, slots, self.sent, semaphore, self.ring.sibling()).wait_recv()

    def slot_number(self, way, distance):
        reach = self.ring.reach
        return distance - 1 if way == 0 or distance == reach else reach + distance - 1

    def slot(self, way, distance):
        ref = self.slots.at[self.slot_number(way, distance)]
        if distance == self.ring.reach and self.halves:
            columns = ref.shape[1] // 2
            return ref.at[:, pl.ds(way * columns, columns)]
        return ref

    def hop(self, way, distance, came):
        ring = self.ring
        if distance == ring.reach and not self.halves and way == 1:
            return None
        slot = self.slot(way, distance)
        source = slot
        if not came:
            part = way if distance == ring.reach and self.halves else None
            source = self.shards.view(distance if way == 0 else -distance, ring.core, part)
        device = ring.right() if way == 0 else ring.left()
        return remote(source, slot, self.sent, self.arrived.at[way, distance - 1], device)

    def push(self, way, distance):
        copy = self.hop(way, distance, False)
        if copy is not None:
            copy.start()

    def arrive(self, way, distance):
        copy = self.hop(way, distance, True)
        if copy is not None:
            copy.wait_recv()

    def add(self, distance, arrivals, final=False):
        ring, shards = self.ring, self.shards
        key = self.key(distance)
        base = shards.row(distance, ring.core)
        block = self.block
        half = shards.columns // 2
        columns = pl.ds(shards.first, shards.columns)

        def body(index, _):
            here = pl.ds(pl.multiple_of(base + index * block, 16), block)
            rows = pl.ds(pl.multiple_of(index * block, block), block)
            total = shards.whole[here, columns].astype(F32) + self.other[key, rows, :].astype(F32)
            for way, far in arrivals:
                slot = self.slot_number(way, far)
                if far == ring.reach and self.halves:
                    low, high = total[:, :half], total[:, half:]
                    if way == 0:
                        low = low + self.slots[slot, rows, :half].astype(F32)
                    else:
                        high = high + self.slots[slot, rows, half:].astype(F32)
                    total = jnp.concatenate([low, high], axis=1)
                elif far < ring.reach or way == 0:
                    total = total + self.slots[slot, rows, :].astype(F32)
            if final:
                self.put(index * block, total)
            else:
                shards.whole[here, columns] = total.astype(shards.whole.dtype)
            return 0

        lax.fori_loop(0, shards.rows // block, body, 0)

    def first(self):
        reach = self.ring.reach
        self.exchanged(True)
        self.add(reach, [])
        self.push(0, reach)
        self.push(1, reach)

    def step(self, distance):
        if distance == self.ring.reach - 1:
            self.exchanged(False)
        self.arrive(0, distance + 1)
        self.add(distance, [(0, distance + 1)])
        self.push(0, distance)
        self.arrive(1, distance + 1)
        self.add(-distance, [(1, distance + 1)])
        self.push(1, distance)

    def last(self):
        self.arrive(0, 1)
        self.arrive(1, 1)
        self.add(0, [(0, 1), (1, 1)], True)

    def drain(self):
        view = self.shards.of_bytes(2 * self.ring.chips - 1)
        remote(view, view, self.sent, self.swapped.at[0], self.ring.sibling()).wait_send()


def dot_nn(a, b):
    return lax.dot_general(a, b, (((1,), (0,)), ((), ())), preferred_element_type=F32)


def dot_nt(a, b):
    return lax.dot_general(a, b, (((1,), (1,)), ((), ())), preferred_element_type=F32)


def dot_tn(a, b):
    return lax.dot_general(a, b, (((0,), (0,)), ((), ())), preferred_element_type=F32)


def gelu_parts(value):
    bell = jnp.exp(-0.5 * value * value)
    t = 1.0 / (1.0 + (0.3275911 * 0.7071067811865476) * jnp.abs(value))
    tail = 0.5 * 1.061405429
    for factor in (-1.453152027, 1.421413741, -0.284496736, 0.254829592):
        tail = tail * t + 0.5 * factor
    tail = tail * t * bell
    return jnp.where(value >= 0.0, 1.0 - tail, tail), bell * 0.3989422804014327


def norm_parts(features):
    center = jnp.mean(features, axis=-1, keepdims=True)
    centered = features - center
    spread = jnp.mean(centered * centered, axis=-1, keepdims=True)
    scale = lax.rsqrt(spread + LN_EPS)
    return centered * scale, scale


def norm_back(z, scale, e, gain):
    t = e * gain
    return (
        t - jnp.mean(t, axis=-1, keepdims=True) - z * jnp.mean(t * z, axis=-1, keepdims=True)
    ) * scale


def column_sum(value):
    return jnp.sum(value, axis=0, keepdims=True)


def layer_kernel(
    devices,
    sections,
    tokens,
    cotangent,
    crops_in,
    own_attn,
    own_up,
    own_down,
    own_vec_in,
    boundary_out,
    input_grads_out,
    sum_attn_out,
    sum_up_out,
    sum_down_out,
    sum_vec_out,
    norm,
    sum_attn,
    sum_up,
    sum_down,
    sum_vec,
    crops,
    own_vec,
    boundary,
    input_grads,
    w_attn,
    w_up,
    w_down,
    tiles,
    params,
    x_in,
    hidden,
    qkv,
    log_total,
    mixed,
    middle,
    hidden_two,
    slope,
    active,
    mask,
    dy_in,
    grad_up,
    grad_branch,
    grad_heads,
    grad_qkv,
    flow,
    flow_two,
    vec_sums,
    vec_tiles,
    g_down,
    other_down,
    other_up,
    other_attn,
    other_vec,
    slots_down,
    slots_up,
    slots_attn,
    slots_vec,
    norm_slots,
    local,
    gather_sems,
    gather_ways,
    relay_sems,
    reduce_sems,
    reduce_ways,
    across,
    norm_sem,
):
    section = lax.axis_index("section")
    first_section = section == 0
    last_section = section == 1
    ring = Ring(devices)
    me = ring.me
    micro_count, pack = tokens.shape[0], tokens.shape[1]
    width = tokens.shape[2]
    hidden_units = w_up.shape[1]
    tiles_up = hidden_units // width
    head_width = width // HEADS
    pair_width = 2 * head_width
    head_scale = head_width ** (-0.5)
    vec_rows, vec_columns = own_vec.shape[0], own_vec.shape[2]

    def rows_of(micro):
        return pl.ds(pl.multiple_of(micro * pack, 16), pack)

    def lanes(start, count):
        return pl.ds(pl.multiple_of(start, 128), count)


    stage_attn = slope.at[pl.ds(0, own_attn.shape[1]), :]
    stage_up = slope.at[pl.ds(own_attn.shape[1], own_up.shape[1]), :]
    stage_down = middle.at[pl.ds(0, own_down.shape[1]), :]
    loads = [
        pltpu.make_async_copy(own_attn.at[0], stage_attn, local.at[0]),
        pltpu.make_async_copy(own_up.at[0], stage_up, local.at[1]),
        pltpu.make_async_copy(own_down.at[0], stage_down, local.at[2]),
        pltpu.make_async_copy(own_vec_in, own_vec, local.at[3]),
        pltpu.make_async_copy(crops_in, crops, local.at[4]),
    ]
    for load in loads:
        load.start()

    def load_tokens(micro):
        return pltpu.make_async_copy(tokens.at[micro], x_in.at[rows_of(micro), :], local.at[5 + micro])

    def load_cotangent(micro):
        return pltpu.make_async_copy(
            cotangent.at[micro], dy_in.at[rows_of(micro), :], local.at[5 + micro]
        )

    @pl.when(first_section)
    def _():
        for micro in range(micro_count):
            load_tokens(micro).start()

    @pl.when(last_section)
    def _():
        for micro in range(micro_count):
            load_cotangent(micro).start()

    barrier = pltpu.get_barrier_semaphore()
    neighbours = (ring.right(), ring.left(), ring.sibling(), (1 - section, me))
    for device in neighbours:
        pl.semaphore_signal(barrier, inc=1, device_id=device, device_id_type=MESH)

    vec_tiles[...] = jnp.zeros_like(vec_tiles)
    vec_sums[...] = jnp.zeros_like(vec_sums)
    load_attn, load_up, load_down, load_vec, load_crops = loads
    load_vec.wait()
    vec_tiles[0:vec_rows, 0:vec_columns] = own_vec[:, 0, :]
    tiles[pl.ds(pl.multiple_of(me * 16, 16), 16), :] = vec_tiles[0:16, :].astype(BF16)
    load_attn.wait()
    count = own_attn.shape[1]
    w_attn[pl.ds(pl.multiple_of(me * count, 16), count), :] = stage_attn[...].astype(BF16)
    pl.semaphore_wait(barrier, len(neighbours))


    def gather_of(index, shards, halves=True):
        return Gather(
            shards,
            halves,
            gather_sems.at[index, 0],
            gather_sems.at[index, 1],
            gather_ways.at[index],
        )

    attn_rows, up_rows, down_rows = own_attn.shape[1], own_up.shape[1], own_down.shape[1]
    reach = ring.reach
    get_vec = gather_of(0, Shards(ring, tiles, 16), False)
    get_attn = gather_of(1, Shards(ring, w_attn, attn_rows))

    lent_rows = up_rows
    kept_up = hidden_units - width
    kept_down = down_rows - lent_rows
    home = (
        Shards(ring, w_up, lent_rows, first=kept_up, columns=width),
        Shards(ring, w_down, lent_rows, down_rows, kept_down),
    )
    relay = Relay(
        Shards(ring, g_down, 2 * lent_rows),
        home,
        [Shards(ring, g_down, lent_rows, 2 * lent_rows, part * lent_rows) for part in range(2)],
        gather_sems.at[5, 0],
        gather_ways.at[5],
        relay_sems,
    )
    pieces = [Pieces(home[part], gather_sems.at[6, part], gather_sems.at[7, part]) for part in range(2)]

    def gathers_of(rows, columns):
        cut = (rows // 2 + 15) // 16 * 16
        up = gather_of(2, Shards(ring, w_up, up_rows, columns=columns))
        down = [
            gather_of(3, Shards(ring, w_down, cut, down_rows)),
            gather_of(4, Shards(ring, w_down, rows - cut, down_rows, cut)),
        ]
        return up, down

    first_up, first_down = gathers_of(kept_down, kept_up)
    last_up, last_down = gathers_of(down_rows, hidden_units)

    def each(gathers, call, *values):
        for gather in gathers:
            getattr(gather, call)(*values)

    get_vec.begin()
    get_attn.begin()
    load_up.wait()
    count = own_up.shape[1]
    w_up[pl.ds(pl.multiple_of(me * count, 16), count), :] = stage_up[...].astype(BF16)
    load_down.wait()
    count = own_down.shape[1]
    w_down[pl.ds(pl.multiple_of(me * count, 16), count), :] = stage_down[...].astype(BF16)
    load_crops.wait()

    @pl.when(first_section)
    def _():
        relay.lend()
        first_up.begin()
        for part in range(2):
            pieces[part].share(0)
        for step in range(1, reach + 1):
            get_vec.step(step)
            get_attn.step(step)
            if step < reach:
                first_up.step(step)
            if step == reach - 1:
                each(first_down, "begin")

    @pl.when(last_section)
    def _():
        relay.borrow()
        relay.begin()
        for step in range(1, reach + 1):
            get_vec.step(step)
            get_attn.step(step)
            if step == reach - 1:
                last_up.begin()
            relay.step(step)

    get_vec.finish()
    get_attn.finish()

    @pl.when(last_section)
    def _():
        last_up.step(1)
        each(last_down, "begin")
        for step in range(2, reach + 1):
            last_up.step(step)
            if step < reach:
                each(last_down, "step", step - 1)
        last_up.finish()

    def first_up_done():
        first_up.step(reach)
        relay.take(0)
        pieces[0].share_rest()
        first_up.finish()
        pieces[0].finish()

    def first_pieces():
        relay.take(1)
        pieces[1].share_rest()

    for device in range(devices):
        params[:, device * vec_columns : (device + 1) * vec_columns] = tiles[
            device * 16 : (device + 1) * 16, 0:vec_columns
        ].astype(F32)


    for micro in range(micro_count):
        row = crops[micro : micro + 1, :].astype(F32)
        square = jnp.broadcast_to(row, (pack, pack))
        mask[micro] = jnp.where(square == square.T, 1.0, 0.0)

    lane = lax.broadcasted_iota(jnp.int32, (1, pair_width), 1)
    in_low = lane < head_width

    def of_head(value, sub):
        return jnp.where(in_low if sub == 0 else ~in_low, value, jnp.zeros_like(value))

    def forward_micro(micro, serve):
        here = rows_of(micro)
        inputs = x_in[here, :].astype(F32)
        z, _ = norm_parts(inputs)
        hidden[here, :] = (z * params[0:1, :] + params[1:2, :]).astype(BF16)
        for part in range(3):
            value = dot_nn(hidden[here, :], w_attn[:, part * width : (part + 1) * width])
            if part == 0:
                value = value + params[2:3, :]
            if part == 2:
                value = value + params[3:4, :]
            qkv[here, part * width : (part + 1) * width] = value.astype(BF16)
        serve(0)

        same = mask[micro] > 0.5
        loaded, scores, probs, outs = [], [], [], []
        for at in range(0, width, pair_width):
            loaded.append([qkv[here, part * width + at : part * width + at + pair_width] for part in range(3)])
        for queries, keys, _ in loaded:
            scores.append([dot_nt(keys, of_head(queries, sub)) for sub in range(2)])
        for head in range(HEADS):
            value = jnp.where(same, scores[head // 2][head % 2] * head_scale, NEG_BIG)
            peak = jnp.max(value, axis=0, keepdims=True)
            exponent = jnp.exp(value - peak)
            totals = jnp.sum(exponent, axis=0, keepdims=True)
            probs.append((exponent * (1.0 / totals)).astype(BF16))
            log_total[micro, head : head + 1, :] = peak + jnp.log(totals)
        for index in range(HEADS // 2):
            low, high = (dot_tn(probs[2 * index + sub], loaded[index][2]) for sub in range(2))
            outs.append(jnp.where(in_low, low, high).astype(BF16))
        for index, value in enumerate(outs):
            mixed[here, index * pair_width : (index + 1) * pair_width] = value
        serve(1)
        middle_value = x_in[here, :].astype(F32) + (
            dot_nn(mixed[here, :], w_attn[:, 3 * width :]) + params[4:5, :]
        )
        middle[here, :] = middle_value
        z, _ = norm_parts(middle_value)
        hidden_two[here, :] = (z * params[5:6, :] + params[6:7, :]).astype(BF16)
        serve(2)
        for part in range(tiles_up):
            columns = slice(part * width, (part + 1) * width)
            upward = dot_nn(hidden_two[here, :], w_up[:, columns]) + params[8 + part : 9 + part, :]
            area, density = gelu_parts(upward)
            active[here, columns] = (upward * area).astype(BF16)
            slope[here, columns] = area + upward * density
        serve(3)

    def hand_over(source, target, micro):
        here = rows_of(micro)
        return remote(
            source.at[micro],
            target.at[here, :],
            across.at[0, micro],
            across.at[1, micro],
            (1 - section, me),
        )

    def forward_step(micro, _):
        @pl.when(last_section)
        def _():
            hand_over(boundary, x_in, micro).wait_recv()

        @pl.when(first_section)
        def _():
            load_tokens(micro).wait()

        def serve(point):
            first_of, last_of = micro == 0, micro == micro_count - 1

            @pl.when(first_section & first_of)
            def _():
                if point == 0:
                    first_up_done()
                if point == 2:
                    for step in range(1, reach - 2):
                        each(first_down, "step", step)
                    first_pieces()

            @pl.when(first_section & last_of)
            def _():
                if point == 0:
                    each(first_down, "step", reach - 2)
                if point == 2:
                    each(first_down, "step", reach - 1)
                if point == 3:
                    each(first_down, "step", reach)

            @pl.when(last_section & first_of)
            def _():
                if point == 2:
                    each(last_down, "step", reach - 1)

            @pl.when(last_section & last_of)
            def _():
                if point == 0:
                    each(last_down, "step", reach)

        forward_micro(micro, serve)
        return 0

    lax.fori_loop(0, micro_count, forward_step, 0)

    @pl.when(first_section)
    def _():
        each(first_down, "finish")
        pieces[1].finish()

    @pl.when(last_section)
    def _():
        each(last_down, "finish")

    def finish_step(micro, _):
        here = rows_of(micro)
        output = middle[here, :] + (dot_nn(active[here, :], w_down[...]) + params[7:8, :])
        boundary[micro] = output.astype(BF16)

        @pl.when(first_section)
        def _():
            hand_over(boundary, x_in, micro).start()

        return 0

    lax.fori_loop(0, micro_count, finish_step, 0)
    each((get_vec, get_attn), "drain")

    @pl.when(first_section)
    def _():
        each((first_up, *first_down, *pieces), "drain")
        relay.drain_lent()

    @pl.when(last_section)
    def _():
        each((last_up, *last_down, relay), "drain")

    pltpu.make_async_copy(boundary, boundary_out, local.at[0]).start()


    def into(ref, first=0, row=0):
        def put(start, value):
            rows = pl.ds(pl.multiple_of(row + start, 8), value.shape[0])
            ref[rows, pl.ds(first, value.shape[1])] = value

        return put

    def reduce_of(index, shards, put, other, slots, halves=True, block=16):
        return Reduce(
            shards,
            put,
            other,
            slots,
            halves,
            block,
            reduce_sems.at[index, 0],
            reduce_sems.at[index, pl.ds(1, 2)],
            reduce_ways.at[index],
        )

    half_down = down_rows // 2
    put_down = [
        reduce_of(
            part,
            Shards(ring, g_down, half_down, down_rows, part * half_down),
            into(sum_down, row=part * half_down),
            other_down.at[part],
            slots_down.at[part],
            block=half_down // 2,
        )
        for part in range(2)
    ]
    half_up, half_attn = hidden_units // 2, w_attn.shape[1] // 2
    put_up = [
        reduce_of(
            2 + part,
            Shards(ring, w_up, up_rows, first=part * half_up, columns=half_up),
            into(sum_up, part * half_up),
            other_up.at[part],
            slots_up.at[part],
        )
        for part in range(2)
    ]
    put_attn = [
        reduce_of(
            4 + part,
            Shards(ring, w_attn, attn_rows, first=part * half_attn, columns=half_attn),
            into(sum_attn, part * half_attn),
            other_attn.at[part],
            slots_attn.at[part],
        )
        for part in range(2)
    ]
    put_vec = reduce_of(
        6, Shards(ring, vec_tiles, 16), into(sum_vec), other_vec, slots_vec, False
    )

    chunk = 2 * down_rows

    def weigh_down(distance):
        start = ring.device(ring.place + distance, 0) * down_rows
        columns = lanes(start, chunk)
        g_down[pl.ds(pl.multiple_of(start, 16), chunk), :] = dot_tn(
            active[:, columns], dy_in[...]
        ).astype(BF16)
        each(put_down, "swap", distance)

    def start_down():
        for index, (distance, _) in enumerate(put_down[0].keys()):
            weigh_down(distance)
            if index == 1:
                each(put_down, "first")
        each(put_down, "step", reach - 1)

    def add_vec(row, value):
        vec_sums[row : row + 1, :] += value

    def backward_micro(micro, serve):
        here = rows_of(micro)
        add_vec(7, column_sum(dy_in[here, :].astype(F32)))
        for part in range(tiles_up):
            columns = slice(part * width, (part + 1) * width)
            back = dot_nt(dy_in[here, :], w_down[columns, :]) * slope[here, columns]
            back = back.astype(BF16)
            grad_up[here, columns] = back
            add_vec(8 + part, column_sum(back.astype(F32)))
            more = dot_nt(back, w_up[:, columns])
            if part == 0:
                flow[...] = more
            else:
                flow[...] += more
        serve(0)
        e = flow[...]
        z, scale = norm_parts(middle[here, :])
        add_vec(5, column_sum(e * z))
        add_vec(6, column_sum(e))
        back = dy_in[here, :].astype(F32) + norm_back(z, scale, e, params[5:6, :])
        flow_two[...] = back
        back = back.astype(BF16)
        grad_branch[here, :] = back
        add_vec(4, column_sum(back.astype(F32)))
        grad_heads[...] = dot_nt(back, w_attn[:, 3 * width :]).astype(BF16)
        serve(1)

        same = mask[micro] > 0.5
        loaded, scores, back_probs, mids, results = [], [], [], [], []
        for at in range(0, width, pair_width):
            loaded.append(
                [qkv[here, part * width + at : part * width + at + pair_width] for part in range(3)]
                + [grad_heads[:, at : at + pair_width]]
            )
        for queries, keys, values, back_out in loaded:
            scores.append([dot_nt(keys, of_head(queries, sub)) for sub in range(2)])
            back_probs.append([dot_nt(values, of_head(back_out, sub)) for sub in range(2)])
        for head in range(HEADS):
            value = jnp.where(same, scores[head // 2][head % 2] * head_scale, NEG_BIG)
            probs = jnp.exp(value - log_total[micro, head : head + 1, :])
            back = back_probs[head // 2][head % 2]
            inner = jnp.sum(back * probs, axis=0, keepdims=True)
            mids.append(((probs * (back - inner)).astype(BF16), probs.astype(BF16)))
        for index, (queries, keys, _, back_out) in enumerate(loaded):
            heads = [
                (
                    dot_tn(back_scores, keys) * head_scale,
                    dot_nn(back_scores, queries) * head_scale,
                    dot_nn(probs, back_out),
                )
                for back_scores, probs in mids[2 * index : 2 * index + 2]
            ]
            results.append(
                [jnp.where(in_low, heads[0][part], heads[1][part]).astype(BF16) for part in range(3)]
            )
        for index, values in enumerate(results):
            for part in range(3):
                at = part * width + index * pair_width
                grad_qkv[here, at : at + pair_width] = values[part]
        serve(2)
        e = dot_nt(grad_qkv[here, :], w_attn[:, : 3 * width])
        z, scale = norm_parts(x_in[here, :].astype(F32))
        back = flow_two[...] + norm_back(z, scale, e, params[0:1, :])
        input_grads[micro] = back.astype(BF16)

        @pl.when(last_section)
        def _():
            hand_over(input_grads, dy_in, micro).start()

        add_vec(0, column_sum(e * z))
        add_vec(1, column_sum(e))
        add_vec(2, column_sum(grad_qkv[here, 0:width].astype(F32)))
        add_vec(3, column_sum(grad_qkv[here, 2 * width : 3 * width].astype(F32)))
        serve(3)

    def backward_step(micro, _):
        @pl.when(first_section)
        def _():
            hand_over(input_grads, dy_in, micro).wait_recv()

        @pl.when(last_section)
        def _():
            load_cotangent(micro).wait()

        is_last = micro == micro_count - 1

        def serve(point):
            @pl.when(first_section & is_last)
            def _():
                if point == 1:
                    each(put_down, "step", reach - 2)
                if point == 3:
                    for distance in range(reach - 3, 0, -1):
                        each(put_down, "step", distance)

        @pl.when(first_section & is_last)
        def _():
            start_down()

        backward_micro(micro, serve)
        return 0

    lax.fori_loop(0, micro_count, backward_step, 0)

    copy_input_grads = pltpu.make_async_copy(input_grads, input_grads_out, local.at[1])
    copy_input_grads.start()

    @pl.when(last_section)
    def _():
        start_down()

    def squares(ref):
        value = ref[...]
        value = value * value
        while value.shape[1] > 128:
            value = sum(
                value[:, start : start + 128] for start in range(0, value.shape[1], 128)
            )
        return sum(value[start : start + 8, :] for start in range(0, value.shape[0], 8))

    third = width // 3

    def weigh(source, grad, target, first):
        def body(index, _):
            target[
                pl.ds(pl.multiple_of(index * third, 16), third),
                pl.ds(first, grad.shape[1]),
            ] = dot_tn(source[:, lanes(index * third, third)], grad[...]).astype(BF16)
            return 0

        lax.fori_loop(0, 3, body, 0)

    weigh(hidden_two, grad_up, w_up, 0)
    each(put_up, "exchange")

    @pl.when(last_section)
    def _():
        each(put_down, "step", reach - 2)

    each(put_up, "first")
    vec_tiles[...] = jnp.zeros_like(vec_tiles)
    for device in range(devices):
        vec_tiles[device * 16 : (device + 1) * 16, 0:vec_columns] = vec_sums[
            :, device * vec_columns : (device + 1) * vec_columns
        ]
    put_vec.exchange()
    weigh(hidden, grad_qkv, w_attn, 0)
    put_attn[0].exchange()
    weigh(mixed, grad_branch, w_attn, 3 * width)
    put_attn[1].exchange()

    @pl.when(last_section)
    def _():
        for distance in range(reach - 3, 0, -1):
            each(put_down, "step", distance)

    put_vec.first()
    each(put_up, "step", reach - 1)
    each(put_down, "last")
    each(put_attn, "first")
    put_vec.step(reach - 1)
    each(put_up, "step", reach - 2)
    each(put_attn, "step", reach - 1)
    for distance in range(reach - 2, 0, -1):
        put_vec.step(distance)
        if distance > 1:
            each(put_up, "step", distance - 1)
        else:
            each(put_up, "last")
        each(put_attn, "step", distance)
    put_vec.last()
    leaving = [
        pltpu.make_async_copy(source, target, local.at[2 + index])
        for index, (source, target) in enumerate(
            ((sum_up, sum_up_out), (sum_down, sum_down_out), (sum_vec, sum_vec_out))
        )
    ]
    for copy in leaving:
        copy.start()
    norm_slots[0] = squares(sum_up) + squares(sum_down) + squares(sum_vec)
    each(put_attn, "last")


    total_devices = sections * devices
    flat = section * devices + me

    def other_device(distance):
        other = (flat + distance) % total_devices
        return (other // devices, other % devices)

    norm_slots[0] += squares(sum_attn)

    def tell(distance, _):
        remote(
            norm_slots.at[0],
            norm_slots.at[distance],
            norm_sem.at[0],
            norm_sem.at[1],
            other_device(distance),
        ).start()
        return 0

    lax.fori_loop(1, total_devices, tell, 0)
    leaving.append(pltpu.make_async_copy(sum_attn, sum_attn_out, local.at[5]))
    leaving[-1].start()
    rest = norm_slots.at[pl.ds(1, total_devices - 1)]
    heard = remote(rest, rest, norm_sem.at[0], norm_sem.at[1], other_device(1))
    heard.wait_recv()

    def collect(device, order):
        return order + norm_slots[(flat - device + total_devices) % total_devices]

    order = lax.fori_loop(0, total_devices, collect, jnp.zeros(norm_slots.shape[1:], F32))
    total = jnp.sum(jnp.sum(order, axis=0, keepdims=True), axis=1, keepdims=True)
    norm[0, 0] = jnp.sqrt(total)[0, 0]
    heard.wait_send()


    each((*put_down, *put_up, *put_attn, put_vec), "drain")
    pltpu.make_async_copy(boundary, boundary_out, local.at[0]).wait()
    copy_input_grads.wait()
    for copy in leaving:
        copy.wait()
    for micro in range(micro_count):

        @pl.when(first_section)
        def _():
            hand_over(boundary, x_in, micro).wait_send()

        @pl.when(last_section)
        def _():
            hand_over(input_grads, dy_in, micro).wait_send()


def run_layers(devices, sections, tokens, cotangent, crop_ids, attn, upward_w, downward_w, vectors):
    micro_count, pack, width = tokens.shape
    rows = micro_count * pack
    chips, reach = devices // 2, devices // 4
    hidden_units = upward_w.shape[2]
    attn_rows, up_rows, down_rows = attn.shape[1], upward_w.shape[1], downward_w.shape[1]
    in_hbm = pl.BlockSpec(memory_space=pl.ANY)

    def other(rows_of_shard, columns, kind=BF16):
        return pltpu.VMEM((chips, rows_of_shard, columns), kind)

    def slots(rows_of_shard, columns, kind=BF16):
        return pltpu.VMEM((2 * reach - 1, rows_of_shard, columns), kind)

    scratch = [
        pltpu.VMEM(attn.shape[1:], F32),
        pltpu.VMEM(upward_w.shape[1:], F32),
        pltpu.VMEM(downward_w.shape[1:], F32),
        pltpu.VMEM((16, 128), F32),
        pltpu.VMEM(crop_ids.shape, jnp.int32),
        pltpu.VMEM(vectors.shape, F32),
        pltpu.VMEM(tokens.shape, BF16),
        pltpu.VMEM(tokens.shape, BF16),
        pltpu.VMEM((width, attn.shape[2]), BF16),
        pltpu.VMEM((width, hidden_units), BF16),
        pltpu.VMEM((hidden_units, width), BF16),
        pltpu.VMEM((devices * 16, 128), BF16),
        pltpu.VMEM((16, width), F32),
        pltpu.VMEM((rows, width), BF16),
        pltpu.VMEM((rows, width), BF16),
        pltpu.VMEM((rows, 3 * width), BF16),
        pltpu.VMEM((micro_count, HEADS, pack), F32),
        pltpu.VMEM((rows, width), BF16),
        pltpu.VMEM((rows, width), F32),
        pltpu.VMEM((rows, width), BF16),
        pltpu.VMEM((rows, hidden_units), F32),
        pltpu.VMEM((rows, hidden_units), BF16),
        pltpu.VMEM((micro_count, pack, pack), F32),
        pltpu.VMEM((rows, width), BF16),
        pltpu.VMEM((rows, hidden_units), BF16),
        pltpu.VMEM((rows, width), BF16),
        pltpu.VMEM((pack, width), BF16),
        pltpu.VMEM((rows, 3 * width), BF16),
        pltpu.VMEM((pack, width), F32),
        pltpu.VMEM((pack, width), F32),
        pltpu.VMEM((16, width), F32),
        pltpu.VMEM((devices * 16, 128), F32),
        pltpu.VMEM((hidden_units, width), BF16),
        pltpu.VMEM((2, chips, down_rows // 2, width), BF16),
        pltpu.VMEM((2, chips, up_rows, hidden_units // 2), BF16),
        pltpu.VMEM((2, chips, attn_rows, attn.shape[2] // 2), BF16),
        other(16, 128, F32),
        pltpu.VMEM((2, 2 * reach - 1, down_rows // 2, width), BF16),
        pltpu.VMEM((2, 2 * reach - 1, up_rows, hidden_units // 2), BF16),
        pltpu.VMEM((2, 2 * reach - 1, attn_rows, attn.shape[2] // 2), BF16),
        slots(16, 128, F32),
        pltpu.VMEM((sections * devices, 8, 128), F32),
        pltpu.SemaphoreType.DMA((5 + micro_count,)),
        pltpu.SemaphoreType.DMA((8, 2)),
        pltpu.SemaphoreType.DMA((6, 2, reach)),
        pltpu.SemaphoreType.DMA((3,)),
        pltpu.SemaphoreType.DMA((7, 3)),
        pltpu.SemaphoreType.DMA((7, 2, reach)),
        pltpu.SemaphoreType.DMA((2, micro_count)),
        pltpu.SemaphoreType.DMA((2,)),
    ]
    return pl.pallas_call(
        partial(layer_kernel, devices, sections),
        out_shape=[
            jax.ShapeDtypeStruct(tokens.shape, BF16),
            jax.ShapeDtypeStruct(tokens.shape, BF16),
            jax.ShapeDtypeStruct(attn.shape[1:], F32),
            jax.ShapeDtypeStruct(upward_w.shape[1:], F32),
            jax.ShapeDtypeStruct(downward_w.shape[1:], F32),
            jax.ShapeDtypeStruct((16, 128), F32),
            jax.ShapeDtypeStruct((1, 1), F32),
        ],
        in_specs=[in_hbm] * 7,
        out_specs=[in_hbm] * 6 + [pl.BlockSpec(memory_space=pltpu.SMEM)],
        scratch_shapes=scratch,
        compiler_params=pltpu.CompilerParams(
            collective_id=0, has_side_effects=True, vmem_limit_bytes=VMEM_LIMIT
        ),
        name="two_layers",
    )(tokens, cotangent, crop_ids, attn, upward_w, downward_w, vectors)


def adam_kernel(boundary, input_grads, norm, *refs):
    grads, states, out_boundary, out_input, out_norm = refs[:4], refs[4:16], *refs[16:19]
    results, held, held_grads, held_states = refs[19:31], refs[31], refs[32:36], refs[36:48]
    fetching, leaving = refs[48:]
    take = [
        pltpu.make_async_copy(source, held.at[i], fetching.at[i])
        for i, source in enumerate((boundary, input_grads))
    ]
    hand_on = [
        pltpu.make_async_copy(held.at[i], target, leaving.at[i])
        for i, target in enumerate((out_boundary, out_input))
    ]
    order = (0, 1, 2, 3)

    def fetches(index):
        copies = [pltpu.make_async_copy(grads[index], held_grads[index], fetching.at[2 + index])]
        for part in range(3):
            at = index + 4 * part
            copies.append(pltpu.make_async_copy(states[at], held_states[at], fetching.at[6 + at]))
        return copies

    def leave(at):
        return pltpu.make_async_copy(held_states[at], results[at], leaving.at[2 + at])

    for index in order:
        for copy in fetches(index):
            copy.start()
    for copy in take:
        copy.start()
    out_norm[0, 0] = norm[0, 0]
    clip_factor = jnp.minimum(1.0, MAX_NORM / (jnp.full((1, 1), norm[0, 0]) + 1e-06))
    for index in order:
        for copy in fetches(index):
            copy.wait()
        master, moment_one, moment_two = (held_states[index + 4 * part] for part in range(3))
        vectors = index == 3
        shape = (master.shape[0], master.shape[2]) if vectors else master.shape[1:]
        gradient = held_grads[index][0 : shape[0], 0 : shape[1]] * clip_factor
        old = [ref[:, 0, :] if vectors else ref[0] for ref in (master, moment_one, moment_two)]
        decay, rate = (0.0, VECTOR_RATE) if vectors else (DECAY_RATE, RATE)
        updated = adam_update(old[0], gradient, old[1], old[2], decay, rate)
        for part in range(3):
            at = index + 4 * part
            if vectors:
                held_states[at][:, 0, :] = updated[part]
            else:
                held_states[at][0] = updated[part]
            leave(at).start()
    for first, second in zip(take, hand_on):
        first.wait()
        second.start()
    for at in range(12):
        leave(at).wait()
    for copy in hand_on:
        copy.wait()


def run_adam(boundary, input_grads, attn, upward_w, downward_w, vectors, norm, states):
    grads = (attn, upward_w, downward_w, vectors)
    in_hbm = pl.BlockSpec(memory_space=pl.ANY)
    scalar = pl.BlockSpec(memory_space=pltpu.SMEM)
    return pl.pallas_call(
        adam_kernel,
        out_shape=[
            jax.ShapeDtypeStruct(boundary.shape, BF16),
            jax.ShapeDtypeStruct(input_grads.shape, BF16),
            jax.ShapeDtypeStruct((1, 1), F32),
        ]
        + [jax.ShapeDtypeStruct(a.shape, F32) for a in states],
        in_specs=[in_hbm, in_hbm, scalar] + [in_hbm] * 16,
        out_specs=[in_hbm, in_hbm, scalar] + [in_hbm] * 12,
        scratch_shapes=[pltpu.VMEM((2,) + boundary.shape, BF16)]
        + [pltpu.VMEM(a.shape, F32) for a in grads]
        + [pltpu.VMEM(a.shape, F32) for a in states]
        + [pltpu.SemaphoreType.DMA((18,)), pltpu.SemaphoreType.DMA((14,))],
        compiler_params=pltpu.CompilerParams(vmem_limit_bytes=VMEM_LIMIT),
        name="adam",
    )(boundary, input_grads, norm, *grads, *states)


def layer_norm(features, gain_row, shift_row):
    center = jnp.mean(features, axis=-1, keepdims=True)
    centered = features - center
    spread = jnp.mean(centered * centered, axis=-1, keepdims=True)
    return centered * lax.rsqrt(spread + LN_EPS) * gain_row + shift_row


def split_heads(packed, micro_count, model_width):
    shaped = packed.reshape(micro_count, -1, 3, HEADS, model_width // HEADS)
    return (shaped[:, :, 0], shaped[:, :, 1], shaped[:, :, 2])


def attention_scores(queries, keys_block, crop_rows):
    head_scale = queries.shape[-1] ** (-0.5)
    scores = (
        jnp.einsum("mqhd,mkhd->mhqk", queries, keys_block, preferred_element_type=F32) * head_scale
    )
    same_crop = crop_rows[:, :, None] == crop_rows[:, None, :]
    return jnp.where(same_crop[:, None], scores, NEG_BIG)


def forward_layer(inputs, crop_rows, weights):
    attn, upward_w, downward_w, vectors_b = weights
    model_width = attn.shape[0]
    rows = inputs.shape[0]
    params = vectors_b.astype(F32)
    hidden = layer_norm(inputs, params[0], params[1]).astype(BF16)
    qkv_bias = jnp.concatenate([params[2], jnp.zeros_like(params[2]), params[3]])
    packed = (
        jnp.dot(hidden, attn[:, : 3 * model_width], preferred_element_type=F32) + qkv_bias
    ).astype(BF16)
    queries, keys_block, values_block = split_heads(packed, crop_rows.shape[0], model_width)
    scores = attention_scores(queries, keys_block, crop_rows)
    row_peak = jnp.max(scores, axis=-1, keepdims=True)
    exponent = jnp.exp(scores - row_peak)
    totals = jnp.sum(exponent, axis=-1, keepdims=True)
    soft_weights = (exponent / totals).astype(BF16)
    log_total = row_peak + jnp.log(totals)
    mixed = jnp.einsum("mhqk,mkhd->mqhd", soft_weights, values_block, preferred_element_type=F32)
    mixed = mixed.reshape(rows, model_width).astype(BF16)
    middle = inputs + (
        jnp.dot(mixed, attn[:, 3 * model_width :], preferred_element_type=F32) + params[4]
    )
    hidden_two = layer_norm(middle, params[5], params[6]).astype(BF16)
    upward = jnp.dot(hidden_two, upward_w, preferred_element_type=F32) + params[8:].reshape(-1)
    active = jax.nn.gelu(upward, approximate=False).astype(BF16)
    output = middle + (jnp.dot(active, downward_w, preferred_element_type=F32) + params[7])
    return (output, (inputs, hidden, packed, log_total, mixed, middle, hidden_two, upward, active))


def backward_layer(kept, crop_rows, grad_out, weights, with_grads):
    attn, upward_w, downward_w, vectors_b = weights
    inputs, hidden, packed, log_total, mixed, middle, hidden_two, upward, active = kept
    model_width = attn.shape[0]
    rows = inputs.shape[0]
    params = vectors_b.astype(F32)
    grad_down = grad_out.astype(BF16)
    grad_active = jnp.einsum("pj,ij->pi", grad_down, downward_w, preferred_element_type=F32)
    gelu_back = jax.vjp(partial(jax.nn.gelu, approximate=False), upward)[1]
    grad_up = gelu_back(grad_active)[0].astype(BF16)
    grad_hidden_two = jnp.einsum("pj,ij->pi", grad_up, upward_w, preferred_element_type=F32)
    norm_back_two = jax.vjp(layer_norm, middle, params[5], params[6])[1]
    grad_middle_part, grad_gain_two, grad_shift_two = norm_back_two(grad_hidden_two)
    grad_middle = grad_out + grad_middle_part
    grad_branch = grad_middle.astype(BF16)
    grad_mixed = jnp.einsum(
        "pj,ij->pi", grad_branch, attn[:, 3 * model_width :], preferred_element_type=F32
    ).astype(BF16)
    micro_count = crop_rows.shape[0]
    queries, keys_block, values_block = split_heads(packed, micro_count, model_width)
    scores = attention_scores(queries, keys_block, crop_rows)
    probs = jnp.exp(scores - log_total)
    grad_heads = grad_mixed.reshape(micro_count, -1, HEADS, model_width // HEADS)
    grad_probs = jnp.einsum("mqhd,mkhd->mhqk", grad_heads, values_block, preferred_element_type=F32)
    grad_values = jnp.einsum(
        "mhqk,mqhd->mkhd", probs.astype(BF16), grad_heads, preferred_element_type=F32
    )
    grad_scores = (
        probs * (grad_probs - jnp.sum(grad_probs * probs, axis=-1, keepdims=True))
    ).astype(BF16)
    head_scale = queries.shape[-1] ** (-0.5)
    grad_queries = (
        jnp.einsum("mhqk,mkhd->mqhd", grad_scores, keys_block, preferred_element_type=F32)
        * head_scale
    )
    grad_keys = (
        jnp.einsum("mhqk,mqhd->mkhd", grad_scores, queries, preferred_element_type=F32) * head_scale
    )
    grad_packed = jnp.concatenate(
        [
            grad_queries.reshape(rows, model_width),
            grad_keys.reshape(rows, model_width),
            grad_values.reshape(rows, model_width),
        ],
        axis=1,
    ).astype(BF16)
    grad_hidden = jnp.einsum(
        "pj,ij->pi", grad_packed, attn[:, : 3 * model_width], preferred_element_type=F32
    )
    norm_back_one = jax.vjp(layer_norm, inputs, params[0], params[1])[1]
    grad_in_part, grad_gain_one, grad_shift_one = norm_back_one(grad_hidden)
    grad_inputs = grad_middle + grad_in_part
    if not with_grads:
        return (grad_inputs, None)
    grad_w_down = jnp.einsum("pi,pj->ij", active, grad_down, preferred_element_type=F32)
    grad_w_up = jnp.einsum("pi,pj->ij", hidden_two, grad_up, preferred_element_type=F32)
    grad_w_out = jnp.einsum("pi,pj->ij", mixed, grad_branch, preferred_element_type=F32)
    grad_w_qkv = jnp.einsum("pi,pj->ij", hidden, grad_packed, preferred_element_type=F32)
    packed_sums = jnp.sum(grad_packed, axis=0, dtype=F32)
    vector_rows = jnp.stack(
        [
            grad_gain_one,
            grad_shift_one,
            packed_sums[:model_width],
            packed_sums[2 * model_width :],
            jnp.sum(grad_branch, axis=0, dtype=F32),
            grad_gain_two,
            grad_shift_two,
            jnp.sum(grad_down, axis=0, dtype=F32),
        ]
    )
    up_bias_rows = jnp.sum(grad_up, axis=0, dtype=F32).reshape(-1, model_width)
    grad_vectors = jnp.concatenate([vector_rows, up_bias_rows], axis=0)
    grad_attn = jnp.concatenate([grad_w_qkv, grad_w_out], axis=1)
    return (grad_inputs, (grad_attn, grad_w_up, grad_w_down, grad_vectors))


def adam_update(master, gradient, moment_one, moment_two, decay_rate, step_rate):
    new_one = BETA_ONE * moment_one + (1.0 - BETA_ONE) * gradient
    new_two = BETA_TWO * moment_two + (1.0 - BETA_TWO) * gradient * gradient
    ratio = (
        new_one / (1.0 - BETA_ONE**STEP) / (jnp.sqrt(new_two / (1.0 - BETA_TWO**STEP)) + ADAM_EPS)
    )
    return (master - step_rate * (ratio + decay_rate * master), new_one, new_two)


def shards_by_kernels(devices, sections, tokens, cotangent, crop_ids, *states):
    states = [state.transpose(1, 0, 2) if i % 4 == 3 else state for i, state in enumerate(states)]
    sums = run_layers(devices, sections, tokens, cotangent, crop_ids, *states[:4])
    boundary, input_grads, grad_norm, *updated = run_adam(*sums, states)
    updated = [state.transpose(1, 0, 2) if i % 4 == 3 else state for i, state in enumerate(updated)]
    return (boundary[None], input_grads[None], grad_norm.reshape(())) + tuple(updated)


def shards_by_collectives(devices, sections, tokens, cotangent, crop_ids, *states):
    section_index = lax.axis_index("section")
    flat = (-1, tokens.shape[2])
    masters, firsts, seconds = states[:4], states[4:8], states[8:]
    shards = [master[0].astype(BF16) for master in masters]
    weights = tuple(
        lax.all_gather(shard, "dp", axis=axis, tiled=True) for shard, axis in zip(shards, (0, 0, 0, 1))
    )
    own_tokens = tokens.reshape(flat)
    first_output, _ = forward_layer(own_tokens.astype(F32), crop_ids, weights)
    received = lax.ppermute(first_output.astype(BF16), "section", [(0, 1)])
    layer_input = jnp.where(section_index == 0, own_tokens, received)
    output, kept = forward_layer(layer_input.astype(F32), crop_ids, weights)
    boundary = output.astype(BF16).reshape(tokens.shape)
    own_grad = cotangent.reshape(flat)
    first_back, _ = backward_layer(kept, crop_ids, own_grad.astype(F32), weights, False)
    back_received = lax.ppermute(first_back.astype(BF16), "section", [(1, 0)])
    grad_out = jnp.where(section_index == 1, own_grad, back_received).astype(F32)
    grad_inputs, gradients = backward_layer(kept, crop_ids, grad_out, weights, True)
    input_grads = grad_inputs.astype(BF16).reshape(tokens.shape)
    reduced = tuple(
        lax.psum_scatter(gradient, "dp", scatter_dimension=axis, tiled=True)
        for gradient, axis in zip(gradients, (0, 0, 0, 1))
    )
    squares = sum(jnp.sum(member * member) for member in reduced)
    grad_norm = jnp.sqrt(lax.psum(squares, ("section", "dp")))
    clip_factor = jnp.minimum(1.0, MAX_NORM / (grad_norm + 1e-06))
    decays = (DECAY_RATE, DECAY_RATE, DECAY_RATE, 0.0)
    rates = (RATE, RATE, RATE, VECTOR_RATE)
    updated = [
        adam_update(master[0], gradient * clip_factor, one[0], two[0], decay_rate, step_rate)
        for master, gradient, one, two, decay_rate, step_rate in zip(
            masters, reduced, firsts, seconds, decays, rates
        )
    ]
    new_states = tuple(entry[part][None] for part in range(3) for entry in updated)
    return (boundary[None], input_grads[None], grad_norm) + new_states


def shards(devices, sections, tokens, cotangent, crop_ids, *states):
    whole_tiles = (
        devices % 8 == 0
        and tokens.shape[1] % 32 == 0
        and all(state.shape[1] % 16 == 0 for state in states[:3])
        and states[2].shape[1] % 64 == 0
        and states[3].shape[1] <= 16
        and states[3].shape[2] <= 128
    )
    run = shards_by_kernels if whole_tiles else shards_by_collectives
    return run(devices, sections, tokens, cotangent, crop_ids, *states)


def solution(mesh):
    token_spec = P(None, "dp", None)
    row_spec = P("section", "dp", None)
    column_spec = P("section", None, "dp")
    state = (row_spec, row_spec, row_spec, column_spec)
    micro_spec = P("section", None, "dp", None)
    return jax.shard_map(
        partial(shards, mesh.shape["dp"], mesh.shape["section"]),
        mesh=mesh,
        in_specs=(token_spec, token_spec, P(None, "dp")) + 3 * state,
        out_specs=(micro_spec, micro_spec, P()) + 3 * state,
        check_vma=False,
    )
```

```python
from functools import partial

import jax
import jax.numpy as jnp
from jax import lax
from jax.experimental import pallas as pl
from jax.experimental.pallas import tpu as pltpu
from jax.sharding import PartitionSpec as P

HEADS = 12
STEP = 10
LN_EPS = 1e-06
NEG_BIG = -1e30
BETA_ONE = 0.9
BETA_TWO = 0.999
RATE = 0.1
VECTOR_RATE = 0.5
DECAY_RATE = 0.01
ADAM_EPS = 1e-08
MAX_NORM = 1.0
MESH = pl.DeviceIdType.MESH
VMEM_LIMIT = 61 * 2**20
F32 = jnp.float32
BF16 = jnp.bfloat16


class Ring:
    def __init__(self, devices):
        self.devices = devices
        self.chips = devices // 2
        self.reach = self.chips // 2
        self.me = lax.axis_index("dp")
        self.core = self.me % 2
        chip = self.me // 2
        row, column = chip // 2, chip % 2
        self.place = row * (1 - column) + (self.chips - 1 - row) * column

    def device(self, place, core):
        place = (place + 2 * self.chips) % self.chips
        column = place // self.reach
        row = place * (1 - column) + (self.chips - 1 - place) * column
        return (row * 2 + column) * 2 + core

    def target(self, device):
        return (lax.axis_index("section"), device)

    def right(self):
        return self.target(self.device(self.place + 1, self.core))

    def left(self):
        return self.target(self.device(self.place - 1, self.core))

    def sibling(self):
        return self.target(self.device(self.place, 1 - self.core))


def remote(source, target, send, receive, device):
    return pltpu.make_async_remote_copy(
        src_ref=source,
        dst_ref=target,
        send_sem=send,
        recv_sem=receive,
        device_id=device,
        device_id_type=MESH,
    )


class Shards:
    def __init__(self, ring, whole, rows, stride=None, base=0, first=0, columns=None):
        self.ring, self.whole, self.rows = ring, whole, rows
        self.stride = rows if stride is None else stride
        self.base, self.first = base, first
        self.columns = whole.shape[1] if columns is None else columns

    def row(self, distance, core):
        device = self.ring.device(self.ring.place + distance, core)
        return pl.multiple_of(device * self.stride + self.base, 16)

    def view(self, distance, core, part=None):
        rows = pl.ds(self.row(distance, core), self.rows)
        if part is None:
            return self.whole.at[rows, pl.ds(self.first, self.columns)]
        columns = self.columns // 2
        return self.whole.at[rows, pl.ds(self.first + part * columns, columns)]

    def of_bytes(self, count):
        return self.whole.at[pl.ds(0, count * self.rows), pl.ds(self.first, self.columns)]


class Gather:
    def __init__(self, shards, halves, sent, shared, arrived):
        self.ring, self.shards, self.halves = shards.ring, shards, halves
        self.sent, self.shared, self.arrived = sent, shared, arrived

    def hop(self, way, step, came):
        ring = self.ring
        direction = 1 if way == 0 else -1
        part = None
        if step == ring.reach:
            if self.halves:
                part = way
            elif way == 1:
                return None
        view = self.shards.view(-direction * (step if came else step - 1), ring.core, part)
        device = ring.right() if way == 0 else ring.left()
        return remote(view, view, self.sent, self.arrived.at[way, step - 1], device)

    def push(self, way, step):
        copy = self.hop(way, step, False)
        if copy is not None:
            copy.start()

    def arrive(self, way, step):
        copy = self.hop(way, step, True)
        if copy is not None:
            copy.wait_recv()

    def share(self, distance):
        view = self.shards.view(distance, self.ring.core)
        remote(view, view, self.sent, self.shared, self.ring.sibling()).start()

    def begin(self):
        self.push(0, 1)
        self.push(1, 1)
        self.share(0)

    def step(self, step):
        reach = self.ring.reach
        self.arrive(0, step)
        if step < reach:
            self.push(0, step + 1)
        self.arrive(1, step)
        if step < reach:
            self.push(1, step + 1)
            self.share(-step)
            self.share(step)
        else:
            self.share(reach)

    def bytes_of(self, count):
        view = self.shards.of_bytes(count)
        return remote(view, view, self.sent, self.shared, self.ring.sibling())

    def finish(self):
        self.bytes_of(self.ring.chips).wait_recv()

    def drain(self):
        self.bytes_of(2 * self.ring.chips - 1).wait_send()


class Relay(Gather):
    def __init__(self, shards, home, away, sent, arrived, crossed):
        super().__init__(shards, True, sent, None, arrived)
        self.home, self.away, self.crossed = home, away, crossed

    def across(self, source, target, semaphore):
        section = lax.axis_index("section")
        return remote(source, target, self.sent, semaphore, (1 - section, self.ring.me))

    def lend(self):
        core = self.ring.core
        for home, away in zip(self.home, self.away):
            self.across(home.view(0, core), away.view(0, core), self.crossed.at[0]).start()

    def borrow(self):
        view = self.shards.view(0, self.ring.core)
        self.across(view, view, self.crossed.at[0]).wait_recv()

    def share(self, distance):
        if distance == 0:
            return
        core = self.ring.core
        for index, (home, away) in enumerate(zip(self.home, self.away)):
            self.across(
                away.view(distance, core), home.view(distance, core), self.crossed.at[1 + index]
            ).start()

    def take(self, index):
        view = self.home[index].of_bytes(self.ring.chips - 1)
        self.across(view, view, self.crossed.at[1 + index]).wait_recv()

    def drain(self):
        view = self.shards.of_bytes(2 * self.ring.chips - 2)
        self.across(view, view, self.crossed.at[0]).wait_send()

    def drain_lent(self):
        view = self.shards.of_bytes(1)
        self.across(view, view, self.crossed.at[0]).wait_send()


class Pieces(Gather):
    def __init__(self, shards, sent, shared):
        super().__init__(shards, True, sent, shared, None)

    def share_rest(self):
        for distance in range(1 - self.ring.reach, self.ring.reach + 1):
            if distance != 0:
                self.share(distance)

    def drain(self):
        self.bytes_of(self.ring.chips).wait_send()


class Reduce:
    def __init__(self, shards, put, other, slots, halves, block, sent, swapped, arrived):
        self.ring, self.shards, self.put = shards.ring, shards, put
        self.other, self.slots, self.halves, self.block = other, slots, halves, block
        self.sent, self.swapped, self.arrived = sent, swapped, arrived

    def keys(self):
        reach = self.ring.reach
        order = [(reach, 0)]
        for distance in range(reach - 1, 0, -1):
            order += [(distance, 2 * (reach - distance) - 1), (-distance, 2 * (reach - distance))]
        return order + [(0, 2 * reach - 1)]

    def key(self, distance):
        return dict(self.keys())[distance]

    def swap(self, distance):
        key = self.key(distance)
        remote(
            self.shards.view(distance, 1 - self.ring.core),
            self.other.at[key],
            self.sent,
            self.swapped.at[min(key, 1)],
            self.ring.sibling(),
        ).start()

    def exchange(self):
        for distance, _ in self.keys():
            self.swap(distance)

    def exchanged(self, first):
        slots = self.other.at[pl.ds(0, 1)] if first else self.other.at[pl.ds(1, self.ring.chips - 1)]
        semaphore = self.swapped.at[0 if first else 1]
        remote(slots, slots, self.sent, semaphore, self.ring.sibling()).wait_recv()

    def slot_number(self, way, distance):
        reach = self.ring.reach
        return distance - 1 if way == 0 or distance == reach else reach + distance - 1

    def slot(self, way, distance):
        ref = self.slots.at[self.slot_number(way, distance)]
        if distance == self.ring.reach and self.halves:
            columns = ref.shape[1] // 2
            return ref.at[:, pl.ds(way * columns, columns)]
        return ref

    def hop(self, way, distance, came):
        ring = self.ring
        if distance == ring.reach and not self.halves and way == 1:
            return None
        slot = self.slot(way, distance)
        source = slot
        if not came:
            part = way if distance == ring.reach and self.halves else None
            source = self.shards.view(distance if way == 0 else -distance, ring.core, part)
        device = ring.right() if way == 0 else ring.left()
        return remote(source, slot, self.sent, self.arrived.at[way, distance - 1], device)

    def push(self, way, distance):
        copy = self.hop(way, distance, False)
        if copy is not None:
            copy.start()

    def arrive(self, way, distance):
        copy = self.hop(way, distance, True)
        if copy is not None:
            copy.wait_recv()

    def add(self, distance, arrivals, final=False):
        ring, shards = self.ring, self.shards
        key = self.key(distance)
        base = shards.row(distance, ring.core)
        block = self.block
        half = shards.columns // 2
        columns = pl.ds(shards.first, shards.columns)

        def body(index, _):
            here = pl.ds(pl.multiple_of(base + index * block, 16), block)
            rows = pl.ds(pl.multiple_of(index * block, block), block)
            total = shards.whole[here, columns].astype(F32) + self.other[key, rows, :].astype(F32)
            for way, far in arrivals:
                slot = self.slot_number(way, far)
                if far == ring.reach and self.halves:
                    low, high = total[:, :half], total[:, half:]
                    if way == 0:
                        low = low + self.slots[slot, rows, :half].astype(F32)
                    else:
                        high = high + self.slots[slot, rows, half:].astype(F32)
                    total = jnp.concatenate([low, high], axis=1)
                elif far < ring.reach or way == 0:
                    total = total + self.slots[slot, rows, :].astype(F32)
            if final:
                self.put(index * block, total)
            else:
                shards.whole[here, columns] = total.astype(shards.whole.dtype)
            return 0

        lax.fori_loop(0, shards.rows // block, body, 0)

    def first(self):
        reach = self.ring.reach
        self.exchanged(True)
        self.add(reach, [])
        self.push(0, reach)
        self.push(1, reach)

    def step(self, distance):
        if distance == self.ring.reach - 1:
            self.exchanged(False)
        self.arrive(0, distance + 1)
        self.add(distance, [(0, distance + 1)])
        self.push(0, distance)
        self.arrive(1, distance + 1)
        self.add(-distance, [(1, distance + 1)])
        self.push(1, distance)

    def last(self):
        self.arrive(0, 1)
        self.arrive(1, 1)
        self.add(0, [(0, 1), (1, 1)], True)

    def drain(self):
        view = self.shards.of_bytes(2 * self.ring.chips - 1)
        remote(view, view, self.sent, self.swapped.at[0], self.ring.sibling()).wait_send()


def dot_nn(a, b):
    return lax.dot_general(a, b, (((1,), (0,)), ((), ())), preferred_element_type=F32)


def dot_nt(a, b):
    return lax.dot_general(a, b, (((1,), (1,)), ((), ())), preferred_element_type=F32)


def dot_tn(a, b):
    return lax.dot_general(a, b, (((0,), (0,)), ((), ())), preferred_element_type=F32)


def gelu_parts(value):
    area = 0.5 + 0.5 * lax.erf(value * 0.7071067811865476)
    return area, jnp.exp(-0.5 * value * value) * 0.3989422804014327


def norm_parts(features):
    center = jnp.mean(features, axis=-1, keepdims=True)
    centered = features - center
    spread = jnp.mean(centered * centered, axis=-1, keepdims=True)
    scale = lax.rsqrt(spread + LN_EPS)
    return centered * scale, scale


def norm_back(z, scale, e, gain):
    t = e * gain
    return (
        t - jnp.mean(t, axis=-1, keepdims=True) - z * jnp.mean(t * z, axis=-1, keepdims=True)
    ) * scale


def column_sum(value):
    return jnp.sum(value, axis=0, keepdims=True)


def layer_kernel(
    devices,
    sections,
    tokens,
    cotangent,
    crops_in,
    own_attn,
    own_up,
    own_down,
    own_vec_in,
    boundary_out,
    input_grads_out,
    sum_attn_out,
    sum_up_out,
    sum_down_out,
    sum_vec_out,
    norm,
    sum_attn,
    sum_up,
    sum_down,
    sum_vec,
    crops,
    own_vec,
    boundary,
    input_grads,
    w_attn,
    w_up,
    w_down,
    tiles,
    params,
    x_in,
    hidden,
    qkv,
    log_total,
    mixed,
    middle,
    hidden_two,
    slope,
    active,
    mask,
    dy_in,
    grad_up,
    grad_branch,
    grad_heads,
    grad_qkv,
    flow,
    flow_two,
    vec_sums,
    vec_tiles,
    g_down,
    other_down,
    other_up,
    other_attn,
    other_vec,
    slots_down,
    slots_up,
    slots_attn,
    slots_vec,
    norm_slots,
    local,
    gather_sems,
    gather_ways,
    relay_sems,
    reduce_sems,
    reduce_ways,
    across,
    norm_sem,
):
    section = lax.axis_index("section")
    first_section = section == 0
    last_section = section == 1
    ring = Ring(devices)
    me = ring.me
    micro_count, pack = tokens.shape[0], tokens.shape[1]
    width = tokens.shape[2]
    hidden_units = w_up.shape[1]
    tiles_up = hidden_units // width
    head_width = width // HEADS
    pair_width = 2 * head_width
    head_scale = head_width ** (-0.5)
    vec_rows, vec_columns = own_vec.shape[0], own_vec.shape[2]

    def rows_of(micro):
        return pl.ds(pl.multiple_of(micro * pack, 16), pack)

    def lanes(start, count):
        return pl.ds(pl.multiple_of(start, 128), count)


    stage_attn = slope.at[pl.ds(0, own_attn.shape[1]), :]
    stage_up = slope.at[pl.ds(own_attn.shape[1], own_up.shape[1]), :]
    stage_down = middle.at[pl.ds(0, own_down.shape[1]), :]
    loads = [
        pltpu.make_async_copy(own_attn.at[0], stage_attn, local.at[0]),
        pltpu.make_async_copy(own_up.at[0], stage_up, local.at[1]),
        pltpu.make_async_copy(own_down.at[0], stage_down, local.at[2]),
        pltpu.make_async_copy(own_vec_in, own_vec, local.at[3]),
        pltpu.make_async_copy(crops_in, crops, local.at[4]),
    ]
    for load in loads:
        load.start()

    def load_tokens(micro):
        return pltpu.make_async_copy(tokens.at[micro], x_in.at[rows_of(micro), :], local.at[5 + micro])

    def load_cotangent(micro):
        return pltpu.make_async_copy(
            cotangent.at[micro], dy_in.at[rows_of(micro), :], local.at[5 + micro]
        )

    @pl.when(first_section)
    def _():
        for micro in range(micro_count):
            load_tokens(micro).start()

    @pl.when(last_section)
    def _():
        for micro in range(micro_count):
            load_cotangent(micro).start()

    barrier = pltpu.get_barrier_semaphore()
    neighbours = (ring.right(), ring.left(), ring.sibling(), (1 - section, me))
    for device in neighbours:
        pl.semaphore_signal(barrier, inc=1, device_id=device, device_id_type=MESH)

    vec_tiles[...] = jnp.zeros_like(vec_tiles)
    vec_sums[...] = jnp.zeros_like(vec_sums)
    load_attn, load_up, load_down, load_vec, load_crops = loads
    load_vec.wait()
    vec_tiles[0:vec_rows, 0:vec_columns] = own_vec[:, 0, :]
    tiles[pl.ds(pl.multiple_of(me * 16, 16), 16), :] = vec_tiles[0:16, :].astype(BF16)
    load_attn.wait()
    count = own_attn.shape[1]
    w_attn[pl.ds(pl.multiple_of(me * count, 16), count), :] = stage_attn[...].astype(BF16)
    pl.semaphore_wait(barrier, len(neighbours))


    def gather_of(index, shards, halves=True):
        return Gather(
            shards,
            halves,
            gather_sems.at[index, 0],
            gather_sems.at[index, 1],
            gather_ways.at[index],
        )

    attn_rows, up_rows, down_rows = own_attn.shape[1], own_up.shape[1], own_down.shape[1]
    reach = ring.reach
    get_vec = gather_of(0, Shards(ring, tiles, 16), False)
    get_attn = gather_of(1, Shards(ring, w_attn, attn_rows))

    lent_rows = up_rows
    kept_up = hidden_units - width
    kept_down = down_rows - lent_rows
    home = (
        Shards(ring, w_up, lent_rows, first=kept_up, columns=width),
        Shards(ring, w_down, lent_rows, down_rows, kept_down),
    )
    relay = Relay(
        Shards(ring, g_down, 2 * lent_rows),
        home,
        [Shards(ring, g_down, lent_rows, 2 * lent_rows, part * lent_rows) for part in range(2)],
        gather_sems.at[5, 0],
        gather_ways.at[5],
        relay_sems,
    )
    pieces = [Pieces(home[part], gather_sems.at[6, part], gather_sems.at[7, part]) for part in range(2)]

    def gathers_of(rows, columns):
        cut = (rows // 2 + 15) // 16 * 16
        up = gather_of(2, Shards(ring, w_up, up_rows, columns=columns))
        down = [
            gather_of(3, Shards(ring, w_down, cut, down_rows)),
            gather_of(4, Shards(ring, w_down, rows - cut, down_rows, cut)),
        ]
        return up, down

    first_up, first_down = gathers_of(kept_down, kept_up)
    last_up, last_down = gathers_of(down_rows, hidden_units)

    def each(gathers, call, *values):
        for gather in gathers:
            getattr(gather, call)(*values)

    get_vec.begin()
    get_attn.begin()
    load_up.wait()
    count = own_up.shape[1]
    w_up[pl.ds(pl.multiple_of(me * count, 16), count), :] = stage_up[...].astype(BF16)
    load_down.wait()
    count = own_down.shape[1]
    w_down[pl.ds(pl.multiple_of(me * count, 16), count), :] = stage_down[...].astype(BF16)
    load_crops.wait()

    @pl.when(first_section)
    def _():
        relay.lend()
        first_up.begin()
        for part in range(2):
            pieces[part].share(0)
        for step in range(1, reach + 1):
            get_vec.step(step)
            get_attn.step(step)
            if step < reach:
                first_up.step(step)
            if step == reach - 1:
                each(first_down, "begin")

    @pl.when(last_section)
    def _():
        relay.borrow()
        relay.begin()
        for step in range(1, reach + 1):
            get_vec.step(step)
            get_attn.step(step)
            if step == reach - 1:
                last_up.begin()
            relay.step(step)

    get_vec.finish()
    get_attn.finish()

    @pl.when(last_section)
    def _():
        last_up.step(1)
        each(last_down, "begin")
        for step in range(2, reach + 1):
            last_up.step(step)
            if step < reach:
                each(last_down, "step", step - 1)
        last_up.finish()

    def first_up_done():
        first_up.step(reach)
        relay.take(0)
        pieces[0].share_rest()
        first_up.finish()
        pieces[0].finish()

    def first_pieces():
        relay.take(1)
        pieces[1].share_rest()

    for device in range(devices):
        params[:, device * vec_columns : (device + 1) * vec_columns] = tiles[
            device * 16 : (device + 1) * 16, 0:vec_columns
        ].astype(F32)


    for micro in range(micro_count):
        row = crops[micro : micro + 1, :].astype(F32)
        square = jnp.broadcast_to(row, (pack, pack))
        mask[micro] = jnp.where(square == square.T, 1.0, 0.0)

    lane = lax.broadcasted_iota(jnp.int32, (1, pair_width), 1)
    in_low = lane < head_width

    def of_head(value, sub):
        return jnp.where(in_low if sub == 0 else ~in_low, value, jnp.zeros_like(value))

    def forward_micro(micro, serve):
        here = rows_of(micro)
        inputs = x_in[here, :].astype(F32)
        z, _ = norm_parts(inputs)
        hidden[here, :] = (z * params[0:1, :] + params[1:2, :]).astype(BF16)
        for part in range(3):
            value = dot_nn(hidden[here, :], w_attn[:, part * width : (part + 1) * width])
            if part == 0:
                value = value + params[2:3, :]
            if part == 2:
                value = value + params[3:4, :]
            qkv[here, part * width : (part + 1) * width] = value.astype(BF16)
        serve(0)

        same = mask[micro] > 0.5
        loaded, scores, probs, outs = [], [], [], []
        for at in range(0, width, pair_width):
            loaded.append([qkv[here, part * width + at : part * width + at + pair_width] for part in range(3)])
        for queries, keys, _ in loaded:
            scores.append([dot_nt(keys, of_head(queries, sub)) for sub in range(2)])
        for head in range(HEADS):
            value = jnp.where(same, scores[head // 2][head % 2] * head_scale, NEG_BIG)
            peak = jnp.max(value, axis=0, keepdims=True)
            exponent = jnp.exp(value - peak)
            totals = jnp.sum(exponent, axis=0, keepdims=True)
            probs.append((exponent * (1.0 / totals)).astype(BF16))
            log_total[micro, head : head + 1, :] = peak + jnp.log(totals)
        for index in range(HEADS // 2):
            low, high = (dot_tn(probs[2 * index + sub], loaded[index][2]) for sub in range(2))
            outs.append(jnp.where(in_low, low, high).astype(BF16))
        for index, value in enumerate(outs):
            mixed[here, index * pair_width : (index + 1) * pair_width] = value
        serve(1)
        middle_value = x_in[here, :].astype(F32) + (
            dot_nn(mixed[here, :], w_attn[:, 3 * width :]) + params[4:5, :]
        )
        middle[here, :] = middle_value
        z, _ = norm_parts(middle_value)
        hidden_two[here, :] = (z * params[5:6, :] + params[6:7, :]).astype(BF16)
        serve(2)
        for part in range(tiles_up):
            columns = slice(part * width, (part + 1) * width)
            upward = dot_nn(hidden_two[here, :], w_up[:, columns]) + params[8 + part : 9 + part, :]
            area, density = gelu_parts(upward)
            active[here, columns] = (upward * area).astype(BF16)
            slope[here, columns] = area + upward * density
        serve(3)

    def hand_over(source, target, micro):
        here = rows_of(micro)
        return remote(
            source.at[micro],
            target.at[here, :],
            across.at[0, micro],
            across.at[1, micro],
            (1 - section, me),
        )

    def forward_step(micro, _):
        @pl.when(last_section)
        def _():
            hand_over(boundary, x_in, micro).wait_recv()

        @pl.when(first_section)
        def _():
            load_tokens(micro).wait()

        def serve(point):
            first_of, last_of = micro == 0, micro == micro_count - 1

            @pl.when(first_section & first_of)
            def _():
                if point == 0:
                    first_up_done()
                if point == 2:
                    for step in range(1, reach - 2):
                        each(first_down, "step", step)
                    first_pieces()

            @pl.when(first_section & last_of)
            def _():
                if point == 0:
                    each(first_down, "step", reach - 2)
                if point == 2:
                    each(first_down, "step", reach - 1)
                if point == 3:
                    each(first_down, "step", reach)

            @pl.when(last_section & first_of)
            def _():
                if point == 2:
                    each(last_down, "step", reach - 1)

            @pl.when(last_section & last_of)
            def _():
                if point == 0:
                    each(last_down, "step", reach)

        forward_micro(micro, serve)
        return 0

    lax.fori_loop(0, micro_count, forward_step, 0)

    @pl.when(first_section)
    def _():
        each(first_down, "finish")
        pieces[1].finish()

    @pl.when(last_section)
    def _():
        each(last_down, "finish")

    def finish_step(micro, _):
        here = rows_of(micro)
        output = middle[here, :] + (dot_nn(active[here, :], w_down[...]) + params[7:8, :])
        boundary[micro] = output.astype(BF16)

        @pl.when(first_section)
        def _():
            hand_over(boundary, x_in, micro).start()

        return 0

    lax.fori_loop(0, micro_count, finish_step, 0)
    each((get_vec, get_attn), "drain")

    @pl.when(first_section)
    def _():
        each((first_up, *first_down, *pieces), "drain")
        relay.drain_lent()

    @pl.when(last_section)
    def _():
        each((last_up, *last_down, relay), "drain")

    pltpu.make_async_copy(boundary, boundary_out, local.at[0]).start()


    def into(ref, first=0, row=0):
        def put(start, value):
            rows = pl.ds(pl.multiple_of(row + start, 8), value.shape[0])
            ref[rows, pl.ds(first, value.shape[1])] = value

        return put

    def reduce_of(index, shards, put, other, slots, halves=True, block=16):
        return Reduce(
            shards,
            put,
            other,
            slots,
            halves,
            block,
            reduce_sems.at[index, 0],
            reduce_sems.at[index, pl.ds(1, 2)],
            reduce_ways.at[index],
        )

    half_down = down_rows // 2
    put_down = [
        reduce_of(
            part,
            Shards(ring, g_down, half_down, down_rows, part * half_down),
            into(sum_down, row=part * half_down),
            other_down.at[part],
            slots_down.at[part],
            block=half_down // 2,
        )
        for part in range(2)
    ]
    half_up, half_attn = hidden_units // 2, w_attn.shape[1] // 2
    put_up = [
        reduce_of(
            2 + part,
            Shards(ring, w_up, up_rows, first=part * half_up, columns=half_up),
            into(sum_up, part * half_up),
            other_up.at[part],
            slots_up.at[part],
        )
        for part in range(2)
    ]
    put_attn = [
        reduce_of(
            4 + part,
            Shards(ring, w_attn, attn_rows, first=part * half_attn, columns=half_attn),
            into(sum_attn, part * half_attn),
            other_attn.at[part],
            slots_attn.at[part],
        )
        for part in range(2)
    ]
    put_vec = reduce_of(
        6, Shards(ring, vec_tiles, 16), into(sum_vec), other_vec, slots_vec, False
    )

    chunk = 2 * down_rows

    def weigh_down(distance):
        start = ring.device(ring.place + distance, 0) * down_rows
        columns = lanes(start, chunk)
        g_down[pl.ds(pl.multiple_of(start, 16), chunk), :] = dot_tn(
            active[:, columns], dy_in[...]
        ).astype(BF16)
        each(put_down, "swap", distance)

    def start_down():
        for index, (distance, _) in enumerate(put_down[0].keys()):
            weigh_down(distance)
            if index == 1:
                each(put_down, "first")
        each(put_down, "step", reach - 1)

    def add_vec(row, value):
        vec_sums[row : row + 1, :] += value

    def backward_micro(micro, serve):
        here = rows_of(micro)
        add_vec(7, column_sum(dy_in[here, :].astype(F32)))
        for part in range(tiles_up):
            columns = slice(part * width, (part + 1) * width)
            back = dot_nt(dy_in[here, :], w_down[columns, :]) * slope[here, columns]
            back = back.astype(BF16)
            grad_up[here, columns] = back
            add_vec(8 + part, column_sum(back.astype(F32)))
            more = dot_nt(back, w_up[:, columns])
            if part == 0:
                flow[...] = more
            else:
                flow[...] += more
        serve(0)
        e = flow[...]
        z, scale = norm_parts(middle[here, :])
        add_vec(5, column_sum(e * z))
        add_vec(6, column_sum(e))
        back = dy_in[here, :].astype(F32) + norm_back(z, scale, e, params[5:6, :])
        flow_two[...] = back
        back = back.astype(BF16)
        grad_branch[here, :] = back
        add_vec(4, column_sum(back.astype(F32)))
        grad_heads[...] = dot_nt(back, w_attn[:, 3 * width :]).astype(BF16)
        serve(1)

        same = mask[micro] > 0.5
        loaded, scores, back_probs, mids, results = [], [], [], [], []
        for at in range(0, width, pair_width):
            loaded.append(
                [qkv[here, part * width + at : part * width + at + pair_width] for part in range(3)]
                + [grad_heads[:, at : at + pair_width]]
            )
        for queries, keys, values, back_out in loaded:
            scores.append([dot_nt(keys, of_head(queries, sub)) for sub in range(2)])
            back_probs.append([dot_nt(values, of_head(back_out, sub)) for sub in range(2)])
        for head in range(HEADS):
            value = jnp.where(same, scores[head // 2][head % 2] * head_scale, NEG_BIG)
            probs = jnp.exp(value - log_total[micro, head : head + 1, :])
            back = back_probs[head // 2][head % 2]
            inner = jnp.sum(back * probs, axis=0, keepdims=True)
            mids.append(((probs * (back - inner)).astype(BF16), probs.astype(BF16)))
        for index, (queries, keys, _, back_out) in enumerate(loaded):
            heads = [
                (
                    dot_tn(back_scores, keys) * head_scale,
                    dot_nn(back_scores, queries) * head_scale,
                    dot_nn(probs, back_out),
                )
                for back_scores, probs in mids[2 * index : 2 * index + 2]
            ]
            results.append(
                [jnp.where(in_low, heads[0][part], heads[1][part]).astype(BF16) for part in range(3)]
            )
        for index, values in enumerate(results):
            for part in range(3):
                at = part * width + index * pair_width
                grad_qkv[here, at : at + pair_width] = values[part]
        serve(2)
        e = dot_nt(grad_qkv[here, :], w_attn[:, : 3 * width])
        z, scale = norm_parts(x_in[here, :].astype(F32))
        back = flow_two[...] + norm_back(z, scale, e, params[0:1, :])
        input_grads[micro] = back.astype(BF16)

        @pl.when(last_section)
        def _():
            hand_over(input_grads, dy_in, micro).start()

        add_vec(0, column_sum(e * z))
        add_vec(1, column_sum(e))
        add_vec(2, column_sum(grad_qkv[here, 0:width].astype(F32)))
        add_vec(3, column_sum(grad_qkv[here, 2 * width : 3 * width].astype(F32)))
        serve(3)

    def backward_step(micro, _):
        @pl.when(first_section)
        def _():
            hand_over(input_grads, dy_in, micro).wait_recv()

        @pl.when(last_section)
        def _():
            load_cotangent(micro).wait()

        is_last = micro == micro_count - 1

        def serve(point):
            @pl.when(first_section & is_last)
            def _():
                if point == 1:
                    each(put_down, "step", reach - 2)
                if point == 3:
                    for distance in range(reach - 3, 0, -1):
                        each(put_down, "step", distance)

        @pl.when(first_section & is_last)
        def _():
            start_down()

        backward_micro(micro, serve)
        return 0

    lax.fori_loop(0, micro_count, backward_step, 0)

    copy_input_grads = pltpu.make_async_copy(input_grads, input_grads_out, local.at[1])
    copy_input_grads.start()

    @pl.when(last_section)
    def _():
        start_down()

    def squares(ref):
        value = ref[...]
        value = value * value
        while value.shape[1] > 128:
            value = sum(
                value[:, start : start + 128] for start in range(0, value.shape[1], 128)
            )
        return sum(value[start : start + 8, :] for start in range(0, value.shape[0], 8))

    third = width // 3

    def weigh(source, grad, target, first):
        def body(index, _):
            target[
                pl.ds(pl.multiple_of(index * third, 16), third),
                pl.ds(first, grad.shape[1]),
            ] = dot_tn(source[:, lanes(index * third, third)], grad[...]).astype(BF16)
            return 0

        lax.fori_loop(0, 3, body, 0)

    weigh(hidden_two, grad_up, w_up, 0)
    each(put_up, "exchange")

    @pl.when(last_section)
    def _():
        each(put_down, "step", reach - 2)

    each(put_up, "first")
    vec_tiles[...] = jnp.zeros_like(vec_tiles)
    for device in range(devices):
        vec_tiles[device * 16 : (device + 1) * 16, 0:vec_columns] = vec_sums[
            :, device * vec_columns : (device + 1) * vec_columns
        ]
    put_vec.exchange()
    weigh(hidden, grad_qkv, w_attn, 0)
    put_attn[0].exchange()
    weigh(mixed, grad_branch, w_attn, 3 * width)
    put_attn[1].exchange()

    @pl.when(last_section)
    def _():
        for distance in range(reach - 3, 0, -1):
            each(put_down, "step", distance)

    put_vec.first()
    each(put_up, "step", reach - 1)
    each(put_down, "last")
    each(put_attn, "first")
    put_vec.step(reach - 1)
    each(put_up, "step", reach - 2)
    each(put_attn, "step", reach - 1)
    for distance in range(reach - 2, 0, -1):
        put_vec.step(distance)
        if distance > 1:
            each(put_up, "step", distance - 1)
        else:
            each(put_up, "last")
        each(put_attn, "step", distance)
    put_vec.last()
    leaving = [
        pltpu.make_async_copy(source, target, local.at[2 + index])
        for index, (source, target) in enumerate(
            ((sum_up, sum_up_out), (sum_down, sum_down_out), (sum_vec, sum_vec_out))
        )
    ]
    for copy in leaving:
        copy.start()
    norm_slots[0] = squares(sum_up) + squares(sum_down) + squares(sum_vec)
    each(put_attn, "last")


    total_devices = sections * devices
    flat = section * devices + me

    def other_device(distance):
        other = (flat + distance) % total_devices
        return (other // devices, other % devices)

    norm_slots[0] += squares(sum_attn)

    def tell(distance, _):
        remote(
            norm_slots.at[0],
            norm_slots.at[distance],
            norm_sem.at[0],
            norm_sem.at[1],
            other_device(distance),
        ).start()
        return 0

    lax.fori_loop(1, total_devices, tell, 0)
    leaving.append(pltpu.make_async_copy(sum_attn, sum_attn_out, local.at[5]))
    leaving[-1].start()
    rest = norm_slots.at[pl.ds(1, total_devices - 1)]
    heard = remote(rest, rest, norm_sem.at[0], norm_sem.at[1], other_device(1))
    heard.wait_recv()

    def collect(device, order):
        return order + norm_slots[(flat - device + total_devices) % total_devices]

    order = lax.fori_loop(0, total_devices, collect, jnp.zeros(norm_slots.shape[1:], F32))
    total = jnp.sum(jnp.sum(order, axis=0, keepdims=True), axis=1, keepdims=True)
    norm[0, 0] = jnp.sqrt(total)[0, 0]
    heard.wait_send()


    each((*put_down, *put_up, *put_attn, put_vec), "drain")
    pltpu.make_async_copy(boundary, boundary_out, local.at[0]).wait()
    copy_input_grads.wait()
    for copy in leaving:
        copy.wait()
    for micro in range(micro_count):

        @pl.when(first_section)
        def _():
            hand_over(boundary, x_in, micro).wait_send()

        @pl.when(last_section)
        def _():
            hand_over(input_grads, dy_in, micro).wait_send()


def run_layers(devices, sections, tokens, cotangent, crop_ids, attn, upward_w, downward_w, vectors):
    micro_count, pack, width = tokens.shape
    rows = micro_count * pack
    chips, reach = devices // 2, devices // 4
    hidden_units = upward_w.shape[2]
    attn_rows, up_rows, down_rows = attn.shape[1], upward_w.shape[1], downward_w.shape[1]
    in_hbm = pl.BlockSpec(memory_space=pl.ANY)

    def other(rows_of_shard, columns, kind=BF16):
        return pltpu.VMEM((chips, rows_of_shard, columns), kind)

    def slots(rows_of_shard, columns, kind=BF16):
        return pltpu.VMEM((2 * reach - 1, rows_of_shard, columns), kind)

    scratch = [
        pltpu.VMEM(attn.shape[1:], F32),
        pltpu.VMEM(upward_w.shape[1:], F32),
        pltpu.VMEM(downward_w.shape[1:], F32),
        pltpu.VMEM((16, 128), F32),
        pltpu.VMEM(crop_ids.shape, jnp.int32),
        pltpu.VMEM(vectors.shape, F32),
        pltpu.VMEM(tokens.shape, BF16),
        pltpu.VMEM(tokens.shape, BF16),
        pltpu.VMEM((width, attn.shape[2]), BF16),
        pltpu.VMEM((width, hidden_units), BF16),
        pltpu.VMEM((hidden_units, width), BF16),
        pltpu.VMEM((devices * 16, 128), BF16),
        pltpu.VMEM((16, width), F32),
        pltpu.VMEM((rows, width), BF16),
        pltpu.VMEM((rows, width), BF16),
        pltpu.VMEM((rows, 3 * width), BF16),
        pltpu.VMEM((micro_count, HEADS, pack), F32),
        pltpu.VMEM((rows, width), BF16),
        pltpu.VMEM((rows, width), F32),
        pltpu.VMEM((rows, width), BF16),
        pltpu.VMEM((rows, hidden_units), F32),
        pltpu.VMEM((rows, hidden_units), BF16),
        pltpu.VMEM((micro_count, pack, pack), F32),
        pltpu.VMEM((rows, width), BF16),
        pltpu.VMEM((rows, hidden_units), BF16),
        pltpu.VMEM((rows, width), BF16),
        pltpu.VMEM((pack, width), BF16),
        pltpu.VMEM((rows, 3 * width), BF16),
        pltpu.VMEM((pack, width), F32),
        pltpu.VMEM((pack, width), F32),
        pltpu.VMEM((16, width), F32),
        pltpu.VMEM((devices * 16, 128), F32),
        pltpu.VMEM((hidden_units, width), BF16),
        pltpu.VMEM((2, chips, down_rows // 2, width), BF16),
        pltpu.VMEM((2, chips, up_rows, hidden_units // 2), BF16),
        pltpu.VMEM((2, chips, attn_rows, attn.shape[2] // 2), BF16),
        other(16, 128, F32),
        pltpu.VMEM((2, 2 * reach - 1, down_rows // 2, width), BF16),
        pltpu.VMEM((2, 2 * reach - 1, up_rows, hidden_units // 2), BF16),
        pltpu.VMEM((2, 2 * reach - 1, attn_rows, attn.shape[2] // 2), BF16),
        slots(16, 128, F32),
        pltpu.VMEM((sections * devices, 8, 128), F32),
        pltpu.SemaphoreType.DMA((5 + micro_count,)),
        pltpu.SemaphoreType.DMA((8, 2)),
        pltpu.SemaphoreType.DMA((6, 2, reach)),
        pltpu.SemaphoreType.DMA((3,)),
        pltpu.SemaphoreType.DMA((7, 3)),
        pltpu.SemaphoreType.DMA((7, 2, reach)),
        pltpu.SemaphoreType.DMA((2, micro_count)),
        pltpu.SemaphoreType.DMA((2,)),
    ]
    return pl.pallas_call(
        partial(layer_kernel, devices, sections),
        out_shape=[
            jax.ShapeDtypeStruct(tokens.shape, BF16),
            jax.ShapeDtypeStruct(tokens.shape, BF16),
            jax.ShapeDtypeStruct(attn.shape[1:], F32),
            jax.ShapeDtypeStruct(upward_w.shape[1:], F32),
            jax.ShapeDtypeStruct(downward_w.shape[1:], F32),
            jax.ShapeDtypeStruct((16, 128), F32),
            jax.ShapeDtypeStruct((1, 1), F32),
        ],
        in_specs=[in_hbm] * 7,
        out_specs=[in_hbm] * 6 + [pl.BlockSpec(memory_space=pltpu.SMEM)],
        scratch_shapes=scratch,
        compiler_params=pltpu.CompilerParams(
            collective_id=0, has_side_effects=True, vmem_limit_bytes=VMEM_LIMIT
        ),
        name="two_layers",
    )(tokens, cotangent, crop_ids, attn, upward_w, downward_w, vectors)


def adam_kernel(boundary, input_grads, norm, *refs):
    grads, states, out_boundary, out_input, out_norm = refs[:4], refs[4:16], *refs[16:19]
    results, held, held_grads, held_states = refs[19:31], refs[31], refs[32:36], refs[36:48]
    fetching, leaving = refs[48:]
    take = [
        pltpu.make_async_copy(source, held.at[i], fetching.at[i])
        for i, source in enumerate((boundary, input_grads))
    ]
    hand_on = [
        pltpu.make_async_copy(held.at[i], target, leaving.at[i])
        for i, target in enumerate((out_boundary, out_input))
    ]
    order = (0, 1, 2, 3)

    def fetches(index):
        copies = [pltpu.make_async_copy(grads[index], held_grads[index], fetching.at[2 + index])]
        for part in range(3):
            at = index + 4 * part
            copies.append(pltpu.make_async_copy(states[at], held_states[at], fetching.at[6 + at]))
        return copies

    def leave(at):
        return pltpu.make_async_copy(held_states[at], results[at], leaving.at[2 + at])

    for index in order:
        for copy in fetches(index):
            copy.start()
    for copy in take:
        copy.start()
    out_norm[0, 0] = norm[0, 0]
    clip_factor = jnp.minimum(1.0, MAX_NORM / (jnp.full((1, 1), norm[0, 0]) + 1e-06))
    for index in order:
        for copy in fetches(index):
            copy.wait()
        master, moment_one, moment_two = (held_states[index + 4 * part] for part in range(3))
        vectors = index == 3
        shape = (master.shape[0], master.shape[2]) if vectors else master.shape[1:]
        gradient = held_grads[index][0 : shape[0], 0 : shape[1]] * clip_factor
        old = [ref[:, 0, :] if vectors else ref[0] for ref in (master, moment_one, moment_two)]
        decay, rate = (0.0, VECTOR_RATE) if vectors else (DECAY_RATE, RATE)
        updated = adam_update(old[0], gradient, old[1], old[2], decay, rate)
        for part in range(3):
            at = index + 4 * part
            if vectors:
                held_states[at][:, 0, :] = updated[part]
            else:
                held_states[at][0] = updated[part]
            leave(at).start()
    for first, second in zip(take, hand_on):
        first.wait()
        second.start()
    for at in range(12):
        leave(at).wait()
    for copy in hand_on:
        copy.wait()


def run_adam(boundary, input_grads, attn, upward_w, downward_w, vectors, norm, states):
    grads = (attn, upward_w, downward_w, vectors)
    in_hbm = pl.BlockSpec(memory_space=pl.ANY)
    scalar = pl.BlockSpec(memory_space=pltpu.SMEM)
    return pl.pallas_call(
        adam_kernel,
        out_shape=[
            jax.ShapeDtypeStruct(boundary.shape, BF16),
            jax.ShapeDtypeStruct(input_grads.shape, BF16),
            jax.ShapeDtypeStruct((1, 1), F32),
        ]
        + [jax.ShapeDtypeStruct(a.shape, F32) for a in states],
        in_specs=[in_hbm, in_hbm, scalar] + [in_hbm] * 16,
        out_specs=[in_hbm, in_hbm, scalar] + [in_hbm] * 12,
        scratch_shapes=[pltpu.VMEM((2,) + boundary.shape, BF16)]
        + [pltpu.VMEM(a.shape, F32) for a in grads]
        + [pltpu.VMEM(a.shape, F32) for a in states]
        + [pltpu.SemaphoreType.DMA((18,)), pltpu.SemaphoreType.DMA((14,))],
        compiler_params=pltpu.CompilerParams(vmem_limit_bytes=VMEM_LIMIT),
        name="adam",
    )(boundary, input_grads, norm, *grads, *states)


def layer_norm(features, gain_row, shift_row):
    center = jnp.mean(features, axis=-1, keepdims=True)
    centered = features - center
    spread = jnp.mean(centered * centered, axis=-1, keepdims=True)
    return centered * lax.rsqrt(spread + LN_EPS) * gain_row + shift_row


def split_heads(packed, micro_count, model_width):
    shaped = packed.reshape(micro_count, -1, 3, HEADS, model_width // HEADS)
    return (shaped[:, :, 0], shaped[:, :, 1], shaped[:, :, 2])


def attention_scores(queries, keys_block, crop_rows):
    head_scale = queries.shape[-1] ** (-0.5)
    scores = (
        jnp.einsum("mqhd,mkhd->mhqk", queries, keys_block, preferred_element_type=F32) * head_scale
    )
    same_crop = crop_rows[:, :, None] == crop_rows[:, None, :]
    return jnp.where(same_crop[:, None], scores, NEG_BIG)


def forward_layer(inputs, crop_rows, weights):
    attn, upward_w, downward_w, vectors_b = weights
    model_width = attn.shape[0]
    rows = inputs.shape[0]
    params = vectors_b.astype(F32)
    hidden = layer_norm(inputs, params[0], params[1]).astype(BF16)
    qkv_bias = jnp.concatenate([params[2], jnp.zeros_like(params[2]), params[3]])
    packed = (
        jnp.dot(hidden, attn[:, : 3 * model_width], preferred_element_type=F32) + qkv_bias
    ).astype(BF16)
    queries, keys_block, values_block = split_heads(packed, crop_rows.shape[0], model_width)
    scores = attention_scores(queries, keys_block, crop_rows)
    row_peak = jnp.max(scores, axis=-1, keepdims=True)
    exponent = jnp.exp(scores - row_peak)
    totals = jnp.sum(exponent, axis=-1, keepdims=True)
    soft_weights = (exponent / totals).astype(BF16)
    log_total = row_peak + jnp.log(totals)
    mixed = jnp.einsum("mhqk,mkhd->mqhd", soft_weights, values_block, preferred_element_type=F32)
    mixed = mixed.reshape(rows, model_width).astype(BF16)
    middle = inputs + (
        jnp.dot(mixed, attn[:, 3 * model_width :], preferred_element_type=F32) + params[4]
    )
    hidden_two = layer_norm(middle, params[5], params[6]).astype(BF16)
    upward = jnp.dot(hidden_two, upward_w, preferred_element_type=F32) + params[8:].reshape(-1)
    active = jax.nn.gelu(upward, approximate=False).astype(BF16)
    output = middle + (jnp.dot(active, downward_w, preferred_element_type=F32) + params[7])
    return (output, (inputs, hidden, packed, log_total, mixed, middle, hidden_two, upward, active))


def backward_layer(kept, crop_rows, grad_out, weights, with_grads):
    attn, upward_w, downward_w, vectors_b = weights
    inputs, hidden, packed, log_total, mixed, middle, hidden_two, upward, active = kept
    model_width = attn.shape[0]
    rows = inputs.shape[0]
    params = vectors_b.astype(F32)
    grad_down = grad_out.astype(BF16)
    grad_active = jnp.einsum("pj,ij->pi", grad_down, downward_w, preferred_element_type=F32)
    gelu_back = jax.vjp(partial(jax.nn.gelu, approximate=False), upward)[1]
    grad_up = gelu_back(grad_active)[0].astype(BF16)
    grad_hidden_two = jnp.einsum("pj,ij->pi", grad_up, upward_w, preferred_element_type=F32)
    norm_back_two = jax.vjp(layer_norm, middle, params[5], params[6])[1]
    grad_middle_part, grad_gain_two, grad_shift_two = norm_back_two(grad_hidden_two)
    grad_middle = grad_out + grad_middle_part
    grad_branch = grad_middle.astype(BF16)
    grad_mixed = jnp.einsum(
        "pj,ij->pi", grad_branch, attn[:, 3 * model_width :], preferred_element_type=F32
    ).astype(BF16)
    micro_count = crop_rows.shape[0]
    queries, keys_block, values_block = split_heads(packed, micro_count, model_width)
    scores = attention_scores(queries, keys_block, crop_rows)
    probs = jnp.exp(scores - log_total)
    grad_heads = grad_mixed.reshape(micro_count, -1, HEADS, model_width // HEADS)
    grad_probs = jnp.einsum("mqhd,mkhd->mhqk", grad_heads, values_block, preferred_element_type=F32)
    grad_values = jnp.einsum(
        "mhqk,mqhd->mkhd", probs.astype(BF16), grad_heads, preferred_element_type=F32
    )
    grad_scores = (
        probs * (grad_probs - jnp.sum(grad_probs * probs, axis=-1, keepdims=True))
    ).astype(BF16)
    head_scale = queries.shape[-1] ** (-0.5)
    grad_queries = (
        jnp.einsum("mhqk,mkhd->mqhd", grad_scores, keys_block, preferred_element_type=F32)
        * head_scale
    )
    grad_keys = (
        jnp.einsum("mhqk,mqhd->mkhd", grad_scores, queries, preferred_element_type=F32) * head_scale
    )
    grad_packed = jnp.concatenate(
        [
            grad_queries.reshape(rows, model_width),
            grad_keys.reshape(rows, model_width),
            grad_values.reshape(rows, model_width),
        ],
        axis=1,
    ).astype(BF16)
    grad_hidden = jnp.einsum(
        "pj,ij->pi", grad_packed, attn[:, : 3 * model_width], preferred_element_type=F32
    )
    norm_back_one = jax.vjp(layer_norm, inputs, params[0], params[1])[1]
    grad_in_part, grad_gain_one, grad_shift_one = norm_back_one(grad_hidden)
    grad_inputs = grad_middle + grad_in_part
    if not with_grads:
        return (grad_inputs, None)
    grad_w_down = jnp.einsum("pi,pj->ij", active, grad_down, preferred_element_type=F32)
    grad_w_up = jnp.einsum("pi,pj->ij", hidden_two, grad_up, preferred_element_type=F32)
    grad_w_out = jnp.einsum("pi,pj->ij", mixed, grad_branch, preferred_element_type=F32)
    grad_w_qkv = jnp.einsum("pi,pj->ij", hidden, grad_packed, preferred_element_type=F32)
    packed_sums = jnp.sum(grad_packed, axis=0, dtype=F32)
    vector_rows = jnp.stack(
        [
            grad_gain_one,
            grad_shift_one,
            packed_sums[:model_width],
            packed_sums[2 * model_width :],
            jnp.sum(grad_branch, axis=0, dtype=F32),
            grad_gain_two,
            grad_shift_two,
            jnp.sum(grad_down, axis=0, dtype=F32),
        ]
    )
    up_bias_rows = jnp.sum(grad_up, axis=0, dtype=F32).reshape(-1, model_width)
    grad_vectors = jnp.concatenate([vector_rows, up_bias_rows], axis=0)
    grad_attn = jnp.concatenate([grad_w_qkv, grad_w_out], axis=1)
    return (grad_inputs, (grad_attn, grad_w_up, grad_w_down, grad_vectors))


def adam_update(master, gradient, moment_one, moment_two, decay_rate, step_rate):
    new_one = BETA_ONE * moment_one + (1.0 - BETA_ONE) * gradient
    new_two = BETA_TWO * moment_two + (1.0 - BETA_TWO) * gradient * gradient
    ratio = (
        new_one / (1.0 - BETA_ONE**STEP) / (jnp.sqrt(new_two / (1.0 - BETA_TWO**STEP)) + ADAM_EPS)
    )
    return (master - step_rate * (ratio + decay_rate * master), new_one, new_two)


def shards_by_kernels(devices, sections, tokens, cotangent, crop_ids, *states):
    states = [state.transpose(1, 0, 2) if i % 4 == 3 else state for i, state in enumerate(states)]
    sums = run_layers(devices, sections, tokens, cotangent, crop_ids, *states[:4])
    boundary, input_grads, grad_norm, *updated = run_adam(*sums, states)
    updated = [state.transpose(1, 0, 2) if i % 4 == 3 else state for i, state in enumerate(updated)]
    return (boundary[None], input_grads[None], grad_norm.reshape(())) + tuple(updated)


def shards_by_collectives(devices, sections, tokens, cotangent, crop_ids, *states):
    section_index = lax.axis_index("section")
    flat = (-1, tokens.shape[2])
    masters, firsts, seconds = states[:4], states[4:8], states[8:]
    shards = [master[0].astype(BF16) for master in masters]
    weights = tuple(
        lax.all_gather(shard, "dp", axis=axis, tiled=True) for shard, axis in zip(shards, (0, 0, 0, 1))
    )
    own_tokens = tokens.reshape(flat)
    first_output, _ = forward_layer(own_tokens.astype(F32), crop_ids, weights)
    received = lax.ppermute(first_output.astype(BF16), "section", [(0, 1)])
    layer_input = jnp.where(section_index == 0, own_tokens, received)
    output, kept = forward_layer(layer_input.astype(F32), crop_ids, weights)
    boundary = output.astype(BF16).reshape(tokens.shape)
    own_grad = cotangent.reshape(flat)
    first_back, _ = backward_layer(kept, crop_ids, own_grad.astype(F32), weights, False)
    back_received = lax.ppermute(first_back.astype(BF16), "section", [(1, 0)])
    grad_out = jnp.where(section_index == 1, own_grad, back_received).astype(F32)
    grad_inputs, gradients = backward_layer(kept, crop_ids, grad_out, weights, True)
    input_grads = grad_inputs.astype(BF16).reshape(tokens.shape)
    reduced = tuple(
        lax.psum_scatter(gradient, "dp", scatter_dimension=axis, tiled=True)
        for gradient, axis in zip(gradients, (0, 0, 0, 1))
    )
    squares = sum(jnp.sum(member * member) for member in reduced)
    grad_norm = jnp.sqrt(lax.psum(squares, ("section", "dp")))
    clip_factor = jnp.minimum(1.0, MAX_NORM / (grad_norm + 1e-06))
    decays = (DECAY_RATE, DECAY_RATE, DECAY_RATE, 0.0)
    rates = (RATE, RATE, RATE, VECTOR_RATE)
    updated = [
        adam_update(master[0], gradient * clip_factor, one[0], two[0], decay_rate, step_rate)
        for master, gradient, one, two, decay_rate, step_rate in zip(
            masters, reduced, firsts, seconds, decays, rates
        )
    ]
    new_states = tuple(entry[part][None] for part in range(3) for entry in updated)
    return (boundary[None], input_grads[None], grad_norm) + new_states


def shards(devices, sections, tokens, cotangent, crop_ids, *states):
    whole_tiles = (
        devices % 8 == 0
        and tokens.shape[1] % 32 == 0
        and all(state.shape[1] % 16 == 0 for state in states[:3])
        and states[2].shape[1] % 64 == 0
        and states[3].shape[1] <= 16
        and states[3].shape[2] <= 128
    )
    run = shards_by_kernels if whole_tiles else shards_by_collectives
    return run(devices, sections, tokens, cotangent, crop_ids, *states)


def solution(mesh):
    token_spec = P(None, "dp", None)
    row_spec = P("section", "dp", None)
    column_spec = P("section", None, "dp")
    state = (row_spec, row_spec, row_spec, column_spec)
    micro_spec = P("section", None, "dp", None)
    return jax.shard_map(
        partial(shards, mesh.shape["dp"], mesh.shape["section"]),
        mesh=mesh,
        in_specs=(token_spec, token_spec, P(None, "dp")) + 3 * state,
        out_specs=(micro_spec, micro_spec, P()) + 3 * state,
        check_vma=False,
    )
```

```python
from functools import partial

import jax
import jax.numpy as jnp
from jax import lax
from jax.experimental import pallas as pl
from jax.experimental.pallas import tpu as pltpu
from jax.sharding import PartitionSpec as P

HEADS = 12
STEP = 10
LN_EPS = 1e-06
NEG_BIG = -1e30
BETA_ONE = 0.9
BETA_TWO = 0.999
RATE = 0.1
VECTOR_RATE = 0.5
DECAY_RATE = 0.01
ADAM_EPS = 1e-08
MAX_NORM = 1.0
MESH = pl.DeviceIdType.MESH
VMEM_LIMIT = 61 * 2**20
F32 = jnp.float32
BF16 = jnp.bfloat16


class Ring:
    def __init__(self, devices):
        self.devices = devices
        self.chips = devices // 2
        self.reach = self.chips // 2
        self.me = lax.axis_index("dp")
        self.core = self.me % 2
        chip = self.me // 2
        row, column = chip // 2, chip % 2
        self.place = row * (1 - column) + (self.chips - 1 - row) * column

    def device(self, place, core):
        place = (place + 2 * self.chips) % self.chips
        column = place // self.reach
        row = place * (1 - column) + (self.chips - 1 - place) * column
        return (row * 2 + column) * 2 + core

    def target(self, device):
        return (lax.axis_index("section"), device)

    def right(self):
        return self.target(self.device(self.place + 1, self.core))

    def left(self):
        return self.target(self.device(self.place - 1, self.core))

    def sibling(self):
        return self.target(self.device(self.place, 1 - self.core))


def remote(source, target, send, receive, device):
    return pltpu.make_async_remote_copy(
        src_ref=source,
        dst_ref=target,
        send_sem=send,
        recv_sem=receive,
        device_id=device,
        device_id_type=MESH,
    )


class Shards:
    def __init__(self, ring, whole, rows, stride=None, base=0, first=0, columns=None):
        self.ring, self.whole, self.rows = ring, whole, rows
        self.stride = rows if stride is None else stride
        self.base, self.first = base, first
        self.columns = whole.shape[1] if columns is None else columns

    def row(self, distance, core):
        device = self.ring.device(self.ring.place + distance, core)
        return pl.multiple_of(device * self.stride + self.base, 16)

    def view(self, distance, core, part=None):
        rows = pl.ds(self.row(distance, core), self.rows)
        if part is None:
            return self.whole.at[rows, pl.ds(self.first, self.columns)]
        columns = self.columns // 2
        return self.whole.at[rows, pl.ds(self.first + part * columns, columns)]

    def of_bytes(self, count):
        return self.whole.at[pl.ds(0, count * self.rows), pl.ds(self.first, self.columns)]


class Gather:
    def __init__(self, shards, halves, sent, shared, arrived):
        self.ring, self.shards, self.halves = shards.ring, shards, halves
        self.sent, self.shared, self.arrived = sent, shared, arrived

    def hop(self, way, step, came):
        ring = self.ring
        direction = 1 if way == 0 else -1
        part = None
        if step == ring.reach:
            if self.halves:
                part = way
            elif way == 1:
                return None
        view = self.shards.view(-direction * (step if came else step - 1), ring.core, part)
        device = ring.right() if way == 0 else ring.left()
        return remote(view, view, self.sent, self.arrived.at[way, step - 1], device)

    def push(self, way, step):
        copy = self.hop(way, step, False)
        if copy is not None:
            copy.start()

    def arrive(self, way, step):
        copy = self.hop(way, step, True)
        if copy is not None:
            copy.wait_recv()

    def share(self, distance):
        view = self.shards.view(distance, self.ring.core)
        remote(view, view, self.sent, self.shared, self.ring.sibling()).start()

    def begin(self):
        self.push(0, 1)
        self.push(1, 1)
        self.share(0)

    def step(self, step):
        reach = self.ring.reach
        self.arrive(0, step)
        if step < reach:
            self.push(0, step + 1)
        self.arrive(1, step)
        if step < reach:
            self.push(1, step + 1)
            self.share(-step)
            self.share(step)
        else:
            self.share(reach)

    def bytes_of(self, count):
        view = self.shards.of_bytes(count)
        return remote(view, view, self.sent, self.shared, self.ring.sibling())

    def finish(self):
        self.bytes_of(self.ring.chips).wait_recv()

    def drain(self):
        self.bytes_of(2 * self.ring.chips - 1).wait_send()


class Relay(Gather):
    def __init__(self, shards, home, away, sent, arrived, crossed):
        super().__init__(shards, True, sent, None, arrived)
        self.home, self.away, self.crossed = home, away, crossed

    def across(self, source, target, semaphore):
        section = lax.axis_index("section")
        return remote(source, target, self.sent, semaphore, (1 - section, self.ring.me))

    def lend(self):
        core = self.ring.core
        for home, away in zip(self.home, self.away):
            self.across(home.view(0, core), away.view(0, core), self.crossed.at[0]).start()

    def borrow(self):
        view = self.shards.view(0, self.ring.core)
        self.across(view, view, self.crossed.at[0]).wait_recv()

    def share(self, distance):
        if distance == 0:
            return
        core = self.ring.core
        for index, (home, away) in enumerate(zip(self.home, self.away)):
            self.across(
                away.view(distance, core), home.view(distance, core), self.crossed.at[1 + index]
            ).start()

    def take(self, index):
        view = self.home[index].of_bytes(self.ring.chips - 1)
        self.across(view, view, self.crossed.at[1 + index]).wait_recv()

    def drain(self):
        view = self.shards.of_bytes(2 * self.ring.chips - 2)
        self.across(view, view, self.crossed.at[0]).wait_send()

    def drain_lent(self):
        view = self.shards.of_bytes(1)
        self.across(view, view, self.crossed.at[0]).wait_send()


class Pieces(Gather):
    def __init__(self, shards, sent, shared):
        super().__init__(shards, True, sent, shared, None)

    def share_rest(self):
        for distance in range(1 - self.ring.reach, self.ring.reach + 1):
            if distance != 0:
                self.share(distance)

    def drain(self):
        self.bytes_of(self.ring.chips).wait_send()


class Reduce:
    def __init__(self, shards, put, other, slots, halves, block, sent, swapped, arrived):
        self.ring, self.shards, self.put = shards.ring, shards, put
        self.other, self.slots, self.halves, self.block = other, slots, halves, block
        self.sent, self.swapped, self.arrived = sent, swapped, arrived

    def keys(self):
        reach = self.ring.reach
        order = [(reach, 0)]
        for distance in range(reach - 1, 0, -1):
            order += [(distance, 2 * (reach - distance) - 1), (-distance, 2 * (reach - distance))]
        return order + [(0, 2 * reach - 1)]

    def key(self, distance):
        return dict(self.keys())[distance]

    def swap(self, distance):
        key = self.key(distance)
        remote(
            self.shards.view(distance, 1 - self.ring.core),
            self.other.at[key],
            self.sent,
            self.swapped.at[min(key, 1)],
            self.ring.sibling(),
        ).start()

    def exchange(self):
        for distance, _ in self.keys():
            self.swap(distance)

    def exchanged(self, first):
        slots = self.other.at[pl.ds(0, 1)] if first else self.other.at[pl.ds(1, self.ring.chips - 1)]
        semaphore = self.swapped.at[0 if first else 1]
        remote(slots, slots, self.sent, semaphore, self.ring.sibling()).wait_recv()

    def slot_number(self, way, distance):
        reach = self.ring.reach
        return distance - 1 if way == 0 or distance == reach else reach + distance - 1

    def slot(self, way, distance):
        ref = self.slots.at[self.slot_number(way, distance)]
        if distance == self.ring.reach and self.halves:
            columns = ref.shape[1] // 2
            return ref.at[:, pl.ds(way * columns, columns)]
        return ref

    def hop(self, way, distance, came):
        ring = self.ring
        if distance == ring.reach and not self.halves and way == 1:
            return None
        slot = self.slot(way, distance)
        source = slot
        if not came:
            part = way if distance == ring.reach and self.halves else None
            source = self.shards.view(distance if way == 0 else -distance, ring.core, part)
        device = ring.right() if way == 0 else ring.left()
        return remote(source, slot, self.sent, self.arrived.at[way, distance - 1], device)

    def push(self, way, distance):
        copy = self.hop(way, distance, False)
        if copy is not None:
            copy.start()

    def arrive(self, way, distance):
        copy = self.hop(way, distance, True)
        if copy is not None:
            copy.wait_recv()

    def add(self, distance, arrivals, final=False):
        ring, shards = self.ring, self.shards
        key = self.key(distance)
        base = shards.row(distance, ring.core)
        block = self.block
        half = shards.columns // 2
        columns = pl.ds(shards.first, shards.columns)

        def body(index, _):
            here = pl.ds(pl.multiple_of(base + index * block, 16), block)
            rows = pl.ds(pl.multiple_of(index * block, block), block)
            total = shards.whole[here, columns].astype(F32) + self.other[key, rows, :].astype(F32)
            for way, far in arrivals:
                slot = self.slot_number(way, far)
                if far == ring.reach and self.halves:
                    low, high = total[:, :half], total[:, half:]
                    if way == 0:
                        low = low + self.slots[slot, rows, :half].astype(F32)
                    else:
                        high = high + self.slots[slot, rows, half:].astype(F32)
                    total = jnp.concatenate([low, high], axis=1)
                elif far < ring.reach or way == 0:
                    total = total + self.slots[slot, rows, :].astype(F32)
            if final:
                self.put(index * block, total)
            else:
                shards.whole[here, columns] = total.astype(shards.whole.dtype)
            return 0

        lax.fori_loop(0, shards.rows // block, body, 0)

    def first(self):
        reach = self.ring.reach
        self.exchanged(True)
        self.add(reach, [])
        self.push(0, reach)
        self.push(1, reach)

    def step(self, distance):
        if distance == self.ring.reach - 1:
            self.exchanged(False)
        self.arrive(0, distance + 1)
        self.add(distance, [(0, distance + 1)])
        self.push(0, distance)
        self.arrive(1, distance + 1)
        self.add(-distance, [(1, distance + 1)])
        self.push(1, distance)

    def last(self):
        self.arrive(0, 1)
        self.arrive(1, 1)
        self.add(0, [(0, 1), (1, 1)], True)

    def drain(self):
        view = self.shards.of_bytes(2 * self.ring.chips - 1)
        remote(view, view, self.sent, self.swapped.at[0], self.ring.sibling()).wait_send()


def dot_nn(a, b):
    return lax.dot_general(a, b, (((1,), (0,)), ((), ())), preferred_element_type=F32)


def dot_nt(a, b):
    return lax.dot_general(a, b, (((1,), (1,)), ((), ())), preferred_element_type=F32)


def dot_tn(a, b):
    return lax.dot_general(a, b, (((0,), (0,)), ((), ())), preferred_element_type=F32)


def gelu_parts(value):
    area = 0.5 + 0.5 * lax.erf(value * 0.7071067811865476)
    return area, jnp.exp(-0.5 * value * value) * 0.3989422804014327


def norm_parts(features):
    center = jnp.mean(features, axis=-1, keepdims=True)
    centered = features - center
    spread = jnp.mean(centered * centered, axis=-1, keepdims=True)
    scale = lax.rsqrt(spread + LN_EPS)
    return centered * scale, scale


def norm_back(z, scale, e, gain):
    t = e * gain
    return (
        t - jnp.mean(t, axis=-1, keepdims=True) - z * jnp.mean(t * z, axis=-1, keepdims=True)
    ) * scale


def column_sum(value):
    return jnp.sum(value, axis=0, keepdims=True)


def layer_kernel(
    devices,
    sections,
    tokens,
    cotangent,
    crops_in,
    own_attn,
    own_up,
    own_down,
    own_vec_in,
    boundary_out,
    input_grads_out,
    sum_attn_out,
    sum_up_out,
    sum_down_out,
    sum_vec_out,
    norm,
    sum_attn,
    sum_up,
    sum_down,
    sum_vec,
    crops,
    own_vec,
    boundary,
    input_grads,
    w_attn,
    w_up,
    w_down,
    tiles,
    params,
    x_in,
    hidden,
    qkv,
    log_total,
    mixed,
    middle,
    hidden_two,
    slope,
    active,
    mask,
    dy_in,
    grad_up,
    grad_branch,
    grad_heads,
    grad_qkv,
    flow,
    flow_two,
    vec_sums,
    vec_tiles,
    g_down,
    other_down,
    other_up,
    other_attn,
    other_vec,
    slots_down,
    slots_up,
    slots_attn,
    slots_vec,
    norm_slots,
    local,
    gather_sems,
    gather_ways,
    relay_sems,
    reduce_sems,
    reduce_ways,
    across,
    norm_sem,
):
    section = lax.axis_index("section")
    first_section = section == 0
    last_section = section == 1
    ring = Ring(devices)
    me = ring.me
    micro_count, pack = tokens.shape[0], tokens.shape[1]
    width = tokens.shape[2]
    hidden_units = w_up.shape[1]
    tiles_up = hidden_units // width
    head_width = width // HEADS
    pair_width = 2 * head_width
    head_scale = head_width ** (-0.5)
    vec_rows, vec_columns = own_vec.shape[0], own_vec.shape[2]

    def rows_of(micro):
        return pl.ds(pl.multiple_of(micro * pack, 16), pack)

    def lanes(start, count):
        return pl.ds(pl.multiple_of(start, 128), count)


    stage_attn = slope.at[pl.ds(0, own_attn.shape[1]), :]
    stage_up = slope.at[pl.ds(own_attn.shape[1], own_up.shape[1]), :]
    stage_down = middle.at[pl.ds(0, own_down.shape[1]), :]
    loads = [
        pltpu.make_async_copy(own_attn.at[0], stage_attn, local.at[0]),
        pltpu.make_async_copy(own_up.at[0], stage_up, local.at[1]),
        pltpu.make_async_copy(own_down.at[0], stage_down, local.at[2]),
        pltpu.make_async_copy(own_vec_in, own_vec, local.at[3]),
        pltpu.make_async_copy(crops_in, crops, local.at[4]),
    ]
    for load in loads:
        load.start()

    def load_tokens(micro):
        return pltpu.make_async_copy(tokens.at[micro], x_in.at[rows_of(micro), :], local.at[5 + micro])

    def load_cotangent(micro):
        return pltpu.make_async_copy(
            cotangent.at[micro], dy_in.at[rows_of(micro), :], local.at[5 + micro]
        )

    @pl.when(first_section)
    def _():
        for micro in range(micro_count):
            load_tokens(micro).start()

    @pl.when(last_section)
    def _():
        for micro in range(micro_count):
            load_cotangent(micro).start()

    barrier = pltpu.get_barrier_semaphore()
    neighbours = (ring.right(), ring.left(), ring.sibling(), (1 - section, me))
    for device in neighbours:
        pl.semaphore_signal(barrier, inc=1, device_id=device, device_id_type=MESH)

    vec_tiles[...] = jnp.zeros_like(vec_tiles)
    vec_sums[...] = jnp.zeros_like(vec_sums)
    load_attn, load_up, load_down, load_vec, load_crops = loads
    load_vec.wait()
    vec_tiles[0:vec_rows, 0:vec_columns] = own_vec[:, 0, :]
    tiles[pl.ds(pl.multiple_of(me * 16, 16), 16), :] = vec_tiles[0:16, :].astype(BF16)
    load_attn.wait()
    count = own_attn.shape[1]
    w_attn[pl.ds(pl.multiple_of(me * count, 16), count), :] = stage_attn[...].astype(BF16)
    pl.semaphore_wait(barrier, len(neighbours))


    def gather_of(index, shards, halves=True):
        return Gather(
            shards,
            halves,
            gather_sems.at[index, 0],
            gather_sems.at[index, 1],
            gather_ways.at[index],
        )

    attn_rows, up_rows, down_rows = own_attn.shape[1], own_up.shape[1], own_down.shape[1]
    reach = ring.reach
    get_vec = gather_of(0, Shards(ring, tiles, 16), False)
    get_attn = gather_of(1, Shards(ring, w_attn, attn_rows))

    lent_rows = up_rows
    kept_up = hidden_units - width
    kept_down = down_rows - lent_rows
    home = (
        Shards(ring, w_up, lent_rows, first=kept_up, columns=width),
        Shards(ring, w_down, lent_rows, down_rows, kept_down),
    )
    relay = Relay(
        Shards(ring, g_down, 2 * lent_rows),
        home,
        [Shards(ring, g_down, lent_rows, 2 * lent_rows, part * lent_rows) for part in range(2)],
        gather_sems.at[5, 0],
        gather_ways.at[5],
        relay_sems,
    )
    pieces = [Pieces(home[part], gather_sems.at[6, part], gather_sems.at[7, part]) for part in range(2)]

    def gathers_of(rows, columns):
        cut = (rows // 2 + 15) // 16 * 16
        up = gather_of(2, Shards(ring, w_up, up_rows, columns=columns))
        down = [
            gather_of(3, Shards(ring, w_down, cut, down_rows)),
            gather_of(4, Shards(ring, w_down, rows - cut, down_rows, cut)),
        ]
        return up, down

    first_up, first_down = gathers_of(kept_down, kept_up)
    last_up, last_down = gathers_of(down_rows, hidden_units)

    def each(gathers, call, *values):
        for gather in gathers:
            getattr(gather, call)(*values)

    get_vec.begin()
    get_attn.begin()
    load_up.wait()
    count = own_up.shape[1]
    w_up[pl.ds(pl.multiple_of(me * count, 16), count), :] = stage_up[...].astype(BF16)
    load_down.wait()
    count = own_down.shape[1]
    w_down[pl.ds(pl.multiple_of(me * count, 16), count), :] = stage_down[...].astype(BF16)
    load_crops.wait()

    @pl.when(first_section)
    def _():
        relay.lend()
        first_up.begin()
        for part in range(2):
            pieces[part].share(0)
        for step in range(1, reach + 1):
            get_vec.step(step)
            get_attn.step(step)
            if step < reach:
                first_up.step(step)
            if step == reach - 1:
                each(first_down, "begin")

    @pl.when(last_section)
    def _():
        relay.borrow()
        relay.begin()
        for step in range(1, reach + 1):
            get_vec.step(step)
            get_attn.step(step)
            if step == reach - 1:
                last_up.begin()
            relay.step(step)

    get_vec.finish()
    get_attn.finish()

    @pl.when(last_section)
    def _():
        last_up.step(1)
        each(last_down, "begin")
        for step in range(2, reach + 1):
            last_up.step(step)
            if step < reach:
                each(last_down, "step", step - 1)
        last_up.finish()

    def first_up_done():
        first_up.step(reach)
        relay.take(0)
        pieces[0].share_rest()
        first_up.finish()
        pieces[0].finish()

    def first_pieces():
        relay.take(1)
        pieces[1].share_rest()

    for device in range(devices):
        params[:, device * vec_columns : (device + 1) * vec_columns] = tiles[
            device * 16 : (device + 1) * 16, 0:vec_columns
        ].astype(F32)


    for micro in range(micro_count):
        row = crops[micro : micro + 1, :].astype(F32)
        square = jnp.broadcast_to(row, (pack, pack))
        mask[micro] = jnp.where(square == square.T, 1.0, 0.0)

    lane = lax.broadcasted_iota(jnp.int32, (1, pair_width), 1)
    in_low = lane < head_width

    def of_head(value, sub):
        return jnp.where(in_low if sub == 0 else ~in_low, value, jnp.zeros_like(value))

    def forward_micro(micro, serve):
        here = rows_of(micro)
        inputs = x_in[here, :].astype(F32)
        z, _ = norm_parts(inputs)
        hidden[here, :] = (z * params[0:1, :] + params[1:2, :]).astype(BF16)
        for part in range(3):
            value = dot_nn(hidden[here, :], w_attn[:, part * width : (part + 1) * width])
            if part == 0:
                value = value + params[2:3, :]
            if part == 2:
                value = value + params[3:4, :]
            qkv[here, part * width : (part + 1) * width] = value.astype(BF16)
        serve(0)

        same = mask[micro] > 0.5
        loaded, scores, probs, outs = [], [], [], []
        for at in range(0, width, pair_width):
            loaded.append([qkv[here, part * width + at : part * width + at + pair_width] for part in range(3)])
        for queries, keys, _ in loaded:
            scores.append([dot_nt(keys, of_head(queries, sub)) for sub in range(2)])
        for head in range(HEADS):
            value = jnp.where(same, scores[head // 2][head % 2] * head_scale, NEG_BIG)
            peak = jnp.max(value, axis=0, keepdims=True)
            exponent = jnp.exp(value - peak)
            totals = jnp.sum(exponent, axis=0, keepdims=True)
            probs.append((exponent * (1.0 / totals)).astype(BF16))
            log_total[micro, head : head + 1, :] = peak + jnp.log(totals)
        for index in range(HEADS // 2):
            low, high = (dot_tn(probs[2 * index + sub], loaded[index][2]) for sub in range(2))
            outs.append(jnp.where(in_low, low, high).astype(BF16))
        for index, value in enumerate(outs):
            mixed[here, index * pair_width : (index + 1) * pair_width] = value
        serve(1)
        middle_value = x_in[here, :].astype(F32) + (
            dot_nn(mixed[here, :], w_attn[:, 3 * width :]) + params[4:5, :]
        )
        middle[here, :] = middle_value
        z, _ = norm_parts(middle_value)
        hidden_two[here, :] = (z * params[5:6, :] + params[6:7, :]).astype(BF16)
        serve(2)
        for part in range(tiles_up):
            columns = slice(part * width, (part + 1) * width)
            upward = dot_nn(hidden_two[here, :], w_up[:, columns]) + params[8 + part : 9 + part, :]
            area, density = gelu_parts(upward)
            active[here, columns] = (upward * area).astype(BF16)
            slope[here, columns] = area + upward * density
        serve(3)

    def hand_over(source, target, micro):
        here = rows_of(micro)
        return remote(
            source.at[micro],
            target.at[here, :],
            across.at[0, micro],
            across.at[1, micro],
            (1 - section, me),
        )

    def forward_step(micro, _):
        @pl.when(last_section)
        def _():
            hand_over(boundary, x_in, micro).wait_recv()

        @pl.when(first_section)
        def _():
            load_tokens(micro).wait()

        def serve(point):
            first_of, last_of = micro == 0, micro == micro_count - 1

            @pl.when(first_section & first_of)
            def _():
                if point == 0:
                    first_up_done()
                if point == 2:
                    for step in range(1, reach - 2):
                        each(first_down, "step", step)
                    first_pieces()

            @pl.when(first_section & last_of)
            def _():
                if point == 0:
                    each(first_down, "step", reach - 2)
                if point == 2:
                    each(first_down, "step", reach - 1)
                if point == 3:
                    each(first_down, "step", reach)

            @pl.when(last_section & first_of)
            def _():
                if point == 2:
                    each(last_down, "step", reach - 1)

            @pl.when(last_section & last_of)
            def _():
                if point == 0:
                    each(last_down, "step", reach)

        forward_micro(micro, serve)
        return 0

    lax.fori_loop(0, micro_count, forward_step, 0)

    @pl.when(first_section)
    def _():
        each(first_down, "finish")
        pieces[1].finish()

    @pl.when(last_section)
    def _():
        each(last_down, "finish")

    def finish_step(micro, _):
        here = rows_of(micro)
        output = middle[here, :] + (dot_nn(active[here, :], w_down[...]) + params[7:8, :])
        boundary[micro] = output.astype(BF16)

        hand_over(boundary, x_in, micro).start()
        return 0

    @pl.when(first_section)
    def _():
        lax.fori_loop(0, micro_count, finish_step, 0)

    @pl.when(last_section)
    def _():
        output = middle[...] + (dot_nn(active[...], w_down[...]) + params[7:8, :])
        for micro in range(micro_count):
            boundary[micro] = output[micro * pack : (micro + 1) * pack, :].astype(BF16)

    each((get_vec, get_attn), "drain")

    @pl.when(first_section)
    def _():
        each((first_up, *first_down, *pieces), "drain")
        relay.drain_lent()

    @pl.when(last_section)
    def _():
        each((last_up, *last_down, relay), "drain")

    pltpu.make_async_copy(boundary, boundary_out, local.at[0]).start()


    def into(ref, first=0, row=0):
        def put(start, value):
            rows = pl.ds(pl.multiple_of(row + start, 8), value.shape[0])
            ref[rows, pl.ds(first, value.shape[1])] = value

        return put

    def reduce_of(index, shards, put, other, slots, halves=True, block=16):
        return Reduce(
            shards,
            put,
            other,
            slots,
            halves,
            block,
            reduce_sems.at[index, 0],
            reduce_sems.at[index, pl.ds(1, 2)],
            reduce_ways.at[index],
        )

    half_down = down_rows // 2
    put_down = [
        reduce_of(
            part,
            Shards(ring, g_down, half_down, down_rows, part * half_down),
            into(sum_down, row=part * half_down),
            other_down.at[part],
            slots_down.at[part],
            block=half_down // 2,
        )
        for part in range(2)
    ]
    half_up, half_attn = hidden_units // 2, w_attn.shape[1] // 2
    put_up = [
        reduce_of(
            2 + part,
            Shards(ring, w_up, up_rows, first=part * half_up, columns=half_up),
            into(sum_up, part * half_up),
            other_up.at[part],
            slots_up.at[part],
        )
        for part in range(2)
    ]
    put_attn = [
        reduce_of(
            4 + part,
            Shards(ring, w_attn, attn_rows, first=part * half_attn, columns=half_attn),
            into(sum_attn, part * half_attn),
            other_attn.at[part],
            slots_attn.at[part],
        )
        for part in range(2)
    ]
    put_vec = reduce_of(
        6, Shards(ring, vec_tiles, 16), into(sum_vec), other_vec, slots_vec, False
    )

    chunk = 2 * down_rows

    def weigh_down(distance):
        start = ring.device(ring.place + distance, 0) * down_rows
        columns = lanes(start, chunk)
        g_down[pl.ds(pl.multiple_of(start, 16), chunk), :] = dot_tn(
            active[:, columns], dy_in[...]
        ).astype(BF16)
        each(put_down, "swap", distance)

    def start_down():
        for index, (distance, _) in enumerate(put_down[0].keys()):
            weigh_down(distance)
            if index == 1:
                each(put_down, "first")
        each(put_down, "step", reach - 1)

    def add_vec(row, value):
        vec_sums[row : row + 1, :] += value

    def backward_micro(micro, serve):
        here = rows_of(micro)
        add_vec(7, column_sum(dy_in[here, :].astype(F32)))
        for part in range(tiles_up):
            columns = slice(part * width, (part + 1) * width)
            back = dot_nt(dy_in[here, :], w_down[columns, :]) * slope[here, columns]
            back = back.astype(BF16)
            grad_up[here, columns] = back
            add_vec(8 + part, column_sum(back.astype(F32)))
            more = dot_nt(back, w_up[:, columns])
            if part == 0:
                flow[...] = more
            else:
                flow[...] += more
        serve(0)
        e = flow[...]
        z, scale = norm_parts(middle[here, :])
        add_vec(5, column_sum(e * z))
        add_vec(6, column_sum(e))
        back = dy_in[here, :].astype(F32) + norm_back(z, scale, e, params[5:6, :])
        flow_two[...] = back
        back = back.astype(BF16)
        grad_branch[here, :] = back
        add_vec(4, column_sum(back.astype(F32)))
        grad_heads[...] = dot_nt(back, w_attn[:, 3 * width :]).astype(BF16)
        serve(1)

        same = mask[micro] > 0.5
        loaded, scores, back_probs, mids, results = [], [], [], [], []
        for at in range(0, width, pair_width):
            loaded.append(
                [qkv[here, part * width + at : part * width + at + pair_width] for part in range(3)]
                + [grad_heads[:, at : at + pair_width]]
            )
        for queries, keys, values, back_out in loaded:
            scores.append([dot_nt(keys, of_head(queries, sub)) for sub in range(2)])
            back_probs.append([dot_nt(values, of_head(back_out, sub)) for sub in range(2)])
        for head in range(HEADS):
            value = jnp.where(same, scores[head // 2][head % 2] * head_scale, NEG_BIG)
            probs = jnp.exp(value - log_total[micro, head : head + 1, :])
            back = back_probs[head // 2][head % 2]
            inner = jnp.sum(back * probs, axis=0, keepdims=True)
            mids.append(((probs * (back - inner)).astype(BF16), probs.astype(BF16)))
        for index, (queries, keys, _, back_out) in enumerate(loaded):
            heads = [
                (
                    dot_tn(back_scores, keys) * head_scale,
                    dot_nn(back_scores, queries) * head_scale,
                    dot_nn(probs, back_out),
                )
                for back_scores, probs in mids[2 * index : 2 * index + 2]
            ]
            results.append(
                [jnp.where(in_low, heads[0][part], heads[1][part]).astype(BF16) for part in range(3)]
            )
        for index, values in enumerate(results):
            for part in range(3):
                at = part * width + index * pair_width
                grad_qkv[here, at : at + pair_width] = values[part]
        serve(2)
        e = dot_nt(grad_qkv[here, :], w_attn[:, : 3 * width])
        z, scale = norm_parts(x_in[here, :].astype(F32))
        back = flow_two[...] + norm_back(z, scale, e, params[0:1, :])
        input_grads[micro] = back.astype(BF16)

        @pl.when(last_section)
        def _():
            hand_over(input_grads, dy_in, micro).start()

        add_vec(0, column_sum(e * z))
        add_vec(1, column_sum(e))
        add_vec(2, column_sum(grad_qkv[here, 0:width].astype(F32)))
        add_vec(3, column_sum(grad_qkv[here, 2 * width : 3 * width].astype(F32)))
        serve(3)

    def backward_step(micro, _):
        @pl.when(first_section)
        def _():
            hand_over(input_grads, dy_in, micro).wait_recv()

        @pl.when(last_section)
        def _():
            load_cotangent(micro).wait()

        is_last = micro == micro_count - 1

        def serve(point):
            @pl.when(first_section & is_last)
            def _():
                if point == 1:
                    each(put_down, "step", reach - 2)
                if point == 3:
                    for distance in range(reach - 3, 0, -1):
                        each(put_down, "step", distance)

        @pl.when(first_section & is_last)
        def _():
            start_down()

        backward_micro(micro, serve)
        return 0

    lax.fori_loop(0, micro_count, backward_step, 0)

    copy_input_grads = pltpu.make_async_copy(input_grads, input_grads_out, local.at[1])
    copy_input_grads.start()

    @pl.when(last_section)
    def _():
        start_down()

    def squares(ref):
        value = ref[...]
        value = value * value
        while value.shape[1] > 128:
            value = sum(
                value[:, start : start + 128] for start in range(0, value.shape[1], 128)
            )
        return sum(value[start : start + 8, :] for start in range(0, value.shape[0], 8))

    third = width // 3

    def weigh(source, grad, target, first):
        def body(index, _):
            target[
                pl.ds(pl.multiple_of(index * third, 16), third),
                pl.ds(first, grad.shape[1]),
            ] = dot_tn(source[:, lanes(index * third, third)], grad[...]).astype(BF16)
            return 0

        lax.fori_loop(0, 3, body, 0)

    weigh(hidden_two, grad_up, w_up, 0)
    each(put_up, "exchange")

    @pl.when(last_section)
    def _():
        each(put_down, "step", reach - 2)

    each(put_up, "first")
    vec_tiles[...] = jnp.zeros_like(vec_tiles)
    for device in range(devices):
        vec_tiles[device * 16 : (device + 1) * 16, 0:vec_columns] = vec_sums[
            :, device * vec_columns : (device + 1) * vec_columns
        ]
    put_vec.exchange()
    weigh(hidden, grad_qkv, w_attn, 0)
    put_attn[0].exchange()
    weigh(mixed, grad_branch, w_attn, 3 * width)
    put_attn[1].exchange()

    @pl.when(last_section)
    def _():
        for distance in range(reach - 3, 0, -1):
            each(put_down, "step", distance)

    put_vec.first()
    each(put_up, "step", reach - 1)
    each(put_down, "last")
    each(put_attn, "first")
    put_vec.step(reach - 1)
    each(put_up, "step", reach - 2)
    each(put_attn, "step", reach - 1)
    for distance in range(reach - 2, 0, -1):
        put_vec.step(distance)
        if distance > 1:
            each(put_up, "step", distance - 1)
        else:
            each(put_up, "last")
        each(put_attn, "step", distance)
    put_vec.last()
    leaving = [
        pltpu.make_async_copy(source, target, local.at[2 + index])
        for index, (source, target) in enumerate(
            ((sum_up, sum_up_out), (sum_down, sum_down_out), (sum_vec, sum_vec_out))
        )
    ]
    for copy in leaving:
        copy.start()
    norm_slots[0] = squares(sum_up) + squares(sum_down) + squares(sum_vec)
    each(put_attn, "last")


    total_devices = sections * devices
    flat = section * devices + me

    def other_device(distance):
        other = (flat + distance) % total_devices
        return (other // devices, other % devices)

    norm_slots[0] += squares(sum_attn)

    def tell(distance, _):
        remote(
            norm_slots.at[0],
            norm_slots.at[distance],
            norm_sem.at[0],
            norm_sem.at[1],
            other_device(distance),
        ).start()
        return 0

    lax.fori_loop(1, total_devices, tell, 0)
    leaving.append(pltpu.make_async_copy(sum_attn, sum_attn_out, local.at[5]))
    leaving[-1].start()
    rest = norm_slots.at[pl.ds(1, total_devices - 1)]
    heard = remote(rest, rest, norm_sem.at[0], norm_sem.at[1], other_device(1))
    heard.wait_recv()

    def collect(device, order):
        return order + norm_slots[(flat - device + total_devices) % total_devices]

    order = lax.fori_loop(0, total_devices, collect, jnp.zeros(norm_slots.shape[1:], F32))
    total = jnp.sum(jnp.sum(order, axis=0, keepdims=True), axis=1, keepdims=True)
    norm[0, 0] = jnp.sqrt(total)[0, 0]
    heard.wait_send()


    each((*put_down, *put_up, *put_attn, put_vec), "drain")
    pltpu.make_async_copy(boundary, boundary_out, local.at[0]).wait()
    copy_input_grads.wait()
    for copy in leaving:
        copy.wait()
    for micro in range(micro_count):

        @pl.when(first_section)
        def _():
            hand_over(boundary, x_in, micro).wait_send()

        @pl.when(last_section)
        def _():
            hand_over(input_grads, dy_in, micro).wait_send()


def run_layers(devices, sections, tokens, cotangent, crop_ids, attn, upward_w, downward_w, vectors):
    micro_count, pack, width = tokens.shape
    rows = micro_count * pack
    chips, reach = devices // 2, devices // 4
    hidden_units = upward_w.shape[2]
    attn_rows, up_rows, down_rows = attn.shape[1], upward_w.shape[1], downward_w.shape[1]
    in_hbm = pl.BlockSpec(memory_space=pl.ANY)

    def other(rows_of_shard, columns, kind=BF16):
        return pltpu.VMEM((chips, rows_of_shard, columns), kind)

    def slots(rows_of_shard, columns, kind=BF16):
        return pltpu.VMEM((2 * reach - 1, rows_of_shard, columns), kind)

    scratch = [
        pltpu.VMEM(attn.shape[1:], F32),
        pltpu.VMEM(upward_w.shape[1:], F32),
        pltpu.VMEM(downward_w.shape[1:], F32),
        pltpu.VMEM((16, 128), F32),
        pltpu.VMEM(crop_ids.shape, jnp.int32),
        pltpu.VMEM(vectors.shape, F32),
        pltpu.VMEM(tokens.shape, BF16),
        pltpu.VMEM(tokens.shape, BF16),
        pltpu.VMEM((width, attn.shape[2]), BF16),
        pltpu.VMEM((width, hidden_units), BF16),
        pltpu.VMEM((hidden_units, width), BF16),
        pltpu.VMEM((devices * 16, 128), BF16),
        pltpu.VMEM((16, width), F32),
        pltpu.VMEM((rows, width), BF16),
        pltpu.VMEM((rows, width), BF16),
        pltpu.VMEM((rows, 3 * width), BF16),
        pltpu.VMEM((micro_count, HEADS, pack), F32),
        pltpu.VMEM((rows, width), BF16),
        pltpu.VMEM((rows, width), F32),
        pltpu.VMEM((rows, width), BF16),
        pltpu.VMEM((rows, hidden_units), F32),
        pltpu.VMEM((rows, hidden_units), BF16),
        pltpu.VMEM((micro_count, pack, pack), F32),
        pltpu.VMEM((rows, width), BF16),
        pltpu.VMEM((rows, hidden_units), BF16),
        pltpu.VMEM((rows, width), BF16),
        pltpu.VMEM((pack, width), BF16),
        pltpu.VMEM((rows, 3 * width), BF16),
        pltpu.VMEM((pack, width), F32),
        pltpu.VMEM((pack, width), F32),
        pltpu.VMEM((16, width), F32),
        pltpu.VMEM((devices * 16, 128), F32),
        pltpu.VMEM((hidden_units, width), BF16),
        pltpu.VMEM((2, chips, down_rows // 2, width), BF16),
        pltpu.VMEM((2, chips, up_rows, hidden_units // 2), BF16),
        pltpu.VMEM((2, chips, attn_rows, attn.shape[2] // 2), BF16),
        other(16, 128, F32),
        pltpu.VMEM((2, 2 * reach - 1, down_rows // 2, width), BF16),
        pltpu.VMEM((2, 2 * reach - 1, up_rows, hidden_units // 2), BF16),
        pltpu.VMEM((2, 2 * reach - 1, attn_rows, attn.shape[2] // 2), BF16),
        slots(16, 128, F32),
        pltpu.VMEM((sections * devices, 8, 128), F32),
        pltpu.SemaphoreType.DMA((5 + micro_count,)),
        pltpu.SemaphoreType.DMA((8, 2)),
        pltpu.SemaphoreType.DMA((6, 2, reach)),
        pltpu.SemaphoreType.DMA((3,)),
        pltpu.SemaphoreType.DMA((7, 3)),
        pltpu.SemaphoreType.DMA((7, 2, reach)),
        pltpu.SemaphoreType.DMA((2, micro_count)),
        pltpu.SemaphoreType.DMA((2,)),
    ]
    return pl.pallas_call(
        partial(layer_kernel, devices, sections),
        out_shape=[
            jax.ShapeDtypeStruct(tokens.shape, BF16),
            jax.ShapeDtypeStruct(tokens.shape, BF16),
            jax.ShapeDtypeStruct(attn.shape[1:], F32),
            jax.ShapeDtypeStruct(upward_w.shape[1:], F32),
            jax.ShapeDtypeStruct(downward_w.shape[1:], F32),
            jax.ShapeDtypeStruct((16, 128), F32),
            jax.ShapeDtypeStruct((1, 1), F32),
        ],
        in_specs=[in_hbm] * 7,
        out_specs=[in_hbm] * 6 + [pl.BlockSpec(memory_space=pltpu.SMEM)],
        scratch_shapes=scratch,
        compiler_params=pltpu.CompilerParams(
            collective_id=0, has_side_effects=True, vmem_limit_bytes=VMEM_LIMIT
        ),
        name="two_layers",
    )(tokens, cotangent, crop_ids, attn, upward_w, downward_w, vectors)


def adam_kernel(boundary, input_grads, norm, *refs):
    grads, states, out_boundary, out_input, out_norm = refs[:4], refs[4:16], *refs[16:19]
    results, held, held_grads, held_states = refs[19:31], refs[31], refs[32:36], refs[36:48]
    fetching, leaving = refs[48:]
    take = [
        pltpu.make_async_copy(source, held.at[i], fetching.at[i])
        for i, source in enumerate((boundary, input_grads))
    ]
    hand_on = [
        pltpu.make_async_copy(held.at[i], target, leaving.at[i])
        for i, target in enumerate((out_boundary, out_input))
    ]
    order = (0, 1, 2, 3)

    def fetches(index):
        copies = [pltpu.make_async_copy(grads[index], held_grads[index], fetching.at[2 + index])]
        for part in range(3):
            at = index + 4 * part
            copies.append(pltpu.make_async_copy(states[at], held_states[at], fetching.at[6 + at]))
        return copies

    def leave(at):
        return pltpu.make_async_copy(held_states[at], results[at], leaving.at[2 + at])

    for index in order:
        for copy in fetches(index):
            copy.start()
    for copy in take:
        copy.start()
    out_norm[0, 0] = norm[0, 0]
    clip_factor = jnp.minimum(1.0, MAX_NORM / (jnp.full((1, 1), norm[0, 0]) + 1e-06))
    for index in order:
        for copy in fetches(index):
            copy.wait()
        master, moment_one, moment_two = (held_states[index + 4 * part] for part in range(3))
        vectors = index == 3
        shape = (master.shape[0], master.shape[2]) if vectors else master.shape[1:]
        gradient = held_grads[index][0 : shape[0], 0 : shape[1]] * clip_factor
        old = [ref[:, 0, :] if vectors else ref[0] for ref in (master, moment_one, moment_two)]
        decay, rate = (0.0, VECTOR_RATE) if vectors else (DECAY_RATE, RATE)
        updated = adam_update(old[0], gradient, old[1], old[2], decay, rate)
        for part in range(3):
            at = index + 4 * part
            if vectors:
                held_states[at][:, 0, :] = updated[part]
            else:
                held_states[at][0] = updated[part]
            leave(at).start()
    for first, second in zip(take, hand_on):
        first.wait()
        second.start()
    for at in range(12):
        leave(at).wait()
    for copy in hand_on:
        copy.wait()


def run_adam(boundary, input_grads, attn, upward_w, downward_w, vectors, norm, states):
    grads = (attn, upward_w, downward_w, vectors)
    in_hbm = pl.BlockSpec(memory_space=pl.ANY)
    scalar = pl.BlockSpec(memory_space=pltpu.SMEM)
    return pl.pallas_call(
        adam_kernel,
        out_shape=[
            jax.ShapeDtypeStruct(boundary.shape, BF16),
            jax.ShapeDtypeStruct(input_grads.shape, BF16),
            jax.ShapeDtypeStruct((1, 1), F32),
        ]
        + [jax.ShapeDtypeStruct(a.shape, F32) for a in states],
        in_specs=[in_hbm, in_hbm, scalar] + [in_hbm] * 16,
        out_specs=[in_hbm, in_hbm, scalar] + [in_hbm] * 12,
        scratch_shapes=[pltpu.VMEM((2,) + boundary.shape, BF16)]
        + [pltpu.VMEM(a.shape, F32) for a in grads]
        + [pltpu.VMEM(a.shape, F32) for a in states]
        + [pltpu.SemaphoreType.DMA((18,)), pltpu.SemaphoreType.DMA((14,))],
        compiler_params=pltpu.CompilerParams(vmem_limit_bytes=VMEM_LIMIT),
        name="adam",
    )(boundary, input_grads, norm, *grads, *states)


def layer_norm(features, gain_row, shift_row):
    center = jnp.mean(features, axis=-1, keepdims=True)
    centered = features - center
    spread = jnp.mean(centered * centered, axis=-1, keepdims=True)
    return centered * lax.rsqrt(spread + LN_EPS) * gain_row + shift_row


def split_heads(packed, micro_count, model_width):
    shaped = packed.reshape(micro_count, -1, 3, HEADS, model_width // HEADS)
    return (shaped[:, :, 0], shaped[:, :, 1], shaped[:, :, 2])


def attention_scores(queries, keys_block, crop_rows):
    head_scale = queries.shape[-1] ** (-0.5)
    scores = (
        jnp.einsum("mqhd,mkhd->mhqk", queries, keys_block, preferred_element_type=F32) * head_scale
    )
    same_crop = crop_rows[:, :, None] == crop_rows[:, None, :]
    return jnp.where(same_crop[:, None], scores, NEG_BIG)


def forward_layer(inputs, crop_rows, weights):
    attn, upward_w, downward_w, vectors_b = weights
    model_width = attn.shape[0]
    rows = inputs.shape[0]
    params = vectors_b.astype(F32)
    hidden = layer_norm(inputs, params[0], params[1]).astype(BF16)
    qkv_bias = jnp.concatenate([params[2], jnp.zeros_like(params[2]), params[3]])
    packed = (
        jnp.dot(hidden, attn[:, : 3 * model_width], preferred_element_type=F32) + qkv_bias
    ).astype(BF16)
    queries, keys_block, values_block = split_heads(packed, crop_rows.shape[0], model_width)
    scores = attention_scores(queries, keys_block, crop_rows)
    row_peak = jnp.max(scores, axis=-1, keepdims=True)
    exponent = jnp.exp(scores - row_peak)
    totals = jnp.sum(exponent, axis=-1, keepdims=True)
    soft_weights = (exponent / totals).astype(BF16)
    log_total = row_peak + jnp.log(totals)
    mixed = jnp.einsum("mhqk,mkhd->mqhd", soft_weights, values_block, preferred_element_type=F32)
    mixed = mixed.reshape(rows, model_width).astype(BF16)
    middle = inputs + (
        jnp.dot(mixed, attn[:, 3 * model_width :], preferred_element_type=F32) + params[4]
    )
    hidden_two = layer_norm(middle, params[5], params[6]).astype(BF16)
    upward = jnp.dot(hidden_two, upward_w, preferred_element_type=F32) + params[8:].reshape(-1)
    active = jax.nn.gelu(upward, approximate=False).astype(BF16)
    output = middle + (jnp.dot(active, downward_w, preferred_element_type=F32) + params[7])
    return (output, (inputs, hidden, packed, log_total, mixed, middle, hidden_two, upward, active))


def backward_layer(kept, crop_rows, grad_out, weights, with_grads):
    attn, upward_w, downward_w, vectors_b = weights
    inputs, hidden, packed, log_total, mixed, middle, hidden_two, upward, active = kept
    model_width = attn.shape[0]
    rows = inputs.shape[0]
    params = vectors_b.astype(F32)
    grad_down = grad_out.astype(BF16)
    grad_active = jnp.einsum("pj,ij->pi", grad_down, downward_w, preferred_element_type=F32)
    gelu_back = jax.vjp(partial(jax.nn.gelu, approximate=False), upward)[1]
    grad_up = gelu_back(grad_active)[0].astype(BF16)
    grad_hidden_two = jnp.einsum("pj,ij->pi", grad_up, upward_w, preferred_element_type=F32)
    norm_back_two = jax.vjp(layer_norm, middle, params[5], params[6])[1]
    grad_middle_part, grad_gain_two, grad_shift_two = norm_back_two(grad_hidden_two)
    grad_middle = grad_out + grad_middle_part
    grad_branch = grad_middle.astype(BF16)
    grad_mixed = jnp.einsum(
        "pj,ij->pi", grad_branch, attn[:, 3 * model_width :], preferred_element_type=F32
    ).astype(BF16)
    micro_count = crop_rows.shape[0]
    queries, keys_block, values_block = split_heads(packed, micro_count, model_width)
    scores = attention_scores(queries, keys_block, crop_rows)
    probs = jnp.exp(scores - log_total)
    grad_heads = grad_mixed.reshape(micro_count, -1, HEADS, model_width // HEADS)
    grad_probs = jnp.einsum("mqhd,mkhd->mhqk", grad_heads, values_block, preferred_element_type=F32)
    grad_values = jnp.einsum(
        "mhqk,mqhd->mkhd", probs.astype(BF16), grad_heads, preferred_element_type=F32
    )
    grad_scores = (
        probs * (grad_probs - jnp.sum(grad_probs * probs, axis=-1, keepdims=True))
    ).astype(BF16)
    head_scale = queries.shape[-1] ** (-0.5)
    grad_queries = (
        jnp.einsum("mhqk,mkhd->mqhd", grad_scores, keys_block, preferred_element_type=F32)
        * head_scale
    )
    grad_keys = (
        jnp.einsum("mhqk,mqhd->mkhd", grad_scores, queries, preferred_element_type=F32) * head_scale
    )
    grad_packed = jnp.concatenate(
        [
            grad_queries.reshape(rows, model_width),
            grad_keys.reshape(rows, model_width),
            grad_values.reshape(rows, model_width),
        ],
        axis=1,
    ).astype(BF16)
    grad_hidden = jnp.einsum(
        "pj,ij->pi", grad_packed, attn[:, : 3 * model_width], preferred_element_type=F32
    )
    norm_back_one = jax.vjp(layer_norm, inputs, params[0], params[1])[1]
    grad_in_part, grad_gain_one, grad_shift_one = norm_back_one(grad_hidden)
    grad_inputs = grad_middle + grad_in_part
    if not with_grads:
        return (grad_inputs, None)
    grad_w_down = jnp.einsum("pi,pj->ij", active, grad_down, preferred_element_type=F32)
    grad_w_up = jnp.einsum("pi,pj->ij", hidden_two, grad_up, preferred_element_type=F32)
    grad_w_out = jnp.einsum("pi,pj->ij", mixed, grad_branch, preferred_element_type=F32)
    grad_w_qkv = jnp.einsum("pi,pj->ij", hidden, grad_packed, preferred_element_type=F32)
    packed_sums = jnp.sum(grad_packed, axis=0, dtype=F32)
    vector_rows = jnp.stack(
        [
            grad_gain_one,
            grad_shift_one,
            packed_sums[:model_width],
            packed_sums[2 * model_width :],
            jnp.sum(grad_branch, axis=0, dtype=F32),
            grad_gain_two,
            grad_shift_two,
            jnp.sum(grad_down, axis=0, dtype=F32),
        ]
    )
    up_bias_rows = jnp.sum(grad_up, axis=0, dtype=F32).reshape(-1, model_width)
    grad_vectors = jnp.concatenate([vector_rows, up_bias_rows], axis=0)
    grad_attn = jnp.concatenate([grad_w_qkv, grad_w_out], axis=1)
    return (grad_inputs, (grad_attn, grad_w_up, grad_w_down, grad_vectors))


def adam_update(master, gradient, moment_one, moment_two, decay_rate, step_rate):
    new_one = BETA_ONE * moment_one + (1.0 - BETA_ONE) * gradient
    new_two = BETA_TWO * moment_two + (1.0 - BETA_TWO) * gradient * gradient
    ratio = (
        new_one / (1.0 - BETA_ONE**STEP) / (jnp.sqrt(new_two / (1.0 - BETA_TWO**STEP)) + ADAM_EPS)
    )
    return (master - step_rate * (ratio + decay_rate * master), new_one, new_two)


def shards_by_kernels(devices, sections, tokens, cotangent, crop_ids, *states):
    states = [state.transpose(1, 0, 2) if i % 4 == 3 else state for i, state in enumerate(states)]
    sums = run_layers(devices, sections, tokens, cotangent, crop_ids, *states[:4])
    boundary, input_grads, grad_norm, *updated = run_adam(*sums, states)
    updated = [state.transpose(1, 0, 2) if i % 4 == 3 else state for i, state in enumerate(updated)]
    return (boundary[None], input_grads[None], grad_norm.reshape(())) + tuple(updated)


def shards_by_collectives(devices, sections, tokens, cotangent, crop_ids, *states):
    section_index = lax.axis_index("section")
    flat = (-1, tokens.shape[2])
    masters, firsts, seconds = states[:4], states[4:8], states[8:]
    shards = [master[0].astype(BF16) for master in masters]
    weights = tuple(
        lax.all_gather(shard, "dp", axis=axis, tiled=True) for shard, axis in zip(shards, (0, 0, 0, 1))
    )
    own_tokens = tokens.reshape(flat)
    first_output, _ = forward_layer(own_tokens.astype(F32), crop_ids, weights)
    received = lax.ppermute(first_output.astype(BF16), "section", [(0, 1)])
    layer_input = jnp.where(section_index == 0, own_tokens, received)
    output, kept = forward_layer(layer_input.astype(F32), crop_ids, weights)
    boundary = output.astype(BF16).reshape(tokens.shape)
    own_grad = cotangent.reshape(flat)
    first_back, _ = backward_layer(kept, crop_ids, own_grad.astype(F32), weights, False)
    back_received = lax.ppermute(first_back.astype(BF16), "section", [(1, 0)])
    grad_out = jnp.where(section_index == 1, own_grad, back_received).astype(F32)
    grad_inputs, gradients = backward_layer(kept, crop_ids, grad_out, weights, True)
    input_grads = grad_inputs.astype(BF16).reshape(tokens.shape)
    reduced = tuple(
        lax.psum_scatter(gradient, "dp", scatter_dimension=axis, tiled=True)
        for gradient, axis in zip(gradients, (0, 0, 0, 1))
    )
    squares = sum(jnp.sum(member * member) for member in reduced)
    grad_norm = jnp.sqrt(lax.psum(squares, ("section", "dp")))
    clip_factor = jnp.minimum(1.0, MAX_NORM / (grad_norm + 1e-06))
    decays = (DECAY_RATE, DECAY_RATE, DECAY_RATE, 0.0)
    rates = (RATE, RATE, RATE, VECTOR_RATE)
    updated = [
        adam_update(master[0], gradient * clip_factor, one[0], two[0], decay_rate, step_rate)
        for master, gradient, one, two, decay_rate, step_rate in zip(
            masters, reduced, firsts, seconds, decays, rates
        )
    ]
    new_states = tuple(entry[part][None] for part in range(3) for entry in updated)
    return (boundary[None], input_grads[None], grad_norm) + new_states


def shards(devices, sections, tokens, cotangent, crop_ids, *states):
    whole_tiles = (
        devices % 8 == 0
        and tokens.shape[1] % 32 == 0
        and all(state.shape[1] % 16 == 0 for state in states[:3])
        and states[2].shape[1] % 64 == 0
        and states[3].shape[1] <= 16
        and states[3].shape[2] <= 128
    )
    run = shards_by_kernels if whole_tiles else shards_by_collectives
    return run(devices, sections, tokens, cotangent, crop_ids, *states)


def solution(mesh):
    token_spec = P(None, "dp", None)
    row_spec = P("section", "dp", None)
    column_spec = P("section", None, "dp")
    state = (row_spec, row_spec, row_spec, column_spec)
    micro_spec = P("section", None, "dp", None)
    return jax.shard_map(
        partial(shards, mesh.shape["dp"], mesh.shape["section"]),
        mesh=mesh,
        in_specs=(token_spec, token_spec, P(None, "dp")) + 3 * state,
        out_specs=(micro_spec, micro_spec, P()) + 3 * state,
        check_vma=False,
    )
```
